32 devices in a mesh: seq: 8 (over z, y), grp: 4 (over x, core).
Axes of the slice: x: 2, y: 2, z: 4, core: 2. Of those that a mesh axis runs over, the one named last changes fastest.
Arguments:
- token_ids: int32 [4, 1024], P('grp', 'seq'), may hold values from 0 to 7999
- target_ids: int32 [4, 1024], P('grp', 'seq'), may hold values from 0 to 7999
- start_flags: int32 [4, 1024], P(None, 'seq'), may hold values from 0 to 1, as said below
- route_ids: int32 [4, 1024, 16, 2], P(None, 'seq'), may hold values from 0 to 4, all different within a row
- embed_table: float32 [1024, 8000], P(('seq', 'grp')), may hold values from -0.75 to 0.75
- layer_weights: float32 [2, 1024, 13568], P(None, ('seq', 'grp'))
- router_weights: float32 [2, 1024, 40], P(None, ('seq', 'grp')), may hold values from -0.375 to 0.375
- norm_gains: float32 [1024, 5], P(('seq', 'grp'))
- embed_mean: float32 [1024, 8000], P(('seq', 'grp')), may hold values from -1.335144e-05 to 1.335144e-05
- layer_mean: float32 [2, 1024, 13568], P(None, ('seq', 'grp')), may hold values from -1.335144e-05 to 1.335144e-05
- router_mean: float32 [2, 1024, 40], P(None, ('seq', 'grp')), may hold values from -1.335144e-05 to 1.335144e-05
- gains_mean: float32 [1024, 5], P(('seq', 'grp')), may hold values from -0.00012207031 to 0.00012207031
- embed_square: float32 [1024, 8000], P(('seq', 'grp')), may hold values from 3.465839e-14 to 5.5453423e-13
- layer_square: float32 [2, 1024, 13568], P(None, ('seq', 'grp')), may hold values from 3.465839e-14 to 5.5453423e-13
- router_square: float32 [2, 1024, 40], P(None, ('seq', 'grp')), may hold values from 3.465839e-14 to 5.5453423e-13
- gains_square: float32 [1024, 5], P(('seq', 'grp')), may hold values from 3.465839e-12 to 5.5453423e-11
Outputs:
- loss_sum: float32 [], replicated
- doc_count: float32 [], replicated
- grad_norm: float32 [], replicated
- embed_mean_new: float32 [1024, 8000], P(('seq', 'grp'))
- embed_square_new: float32 [1024, 8000], P(('seq', 'grp'))
- embed_new: float32 [1024, 8000], P(('seq', 'grp'))
- layer_mean_new: float32 [2, 1024, 13568], P(None, ('seq', 'grp'))
- layer_square_new: float32 [2, 1024, 13568], P(None, ('seq', 'grp'))
- layer_new: float32 [2, 1024, 13568], P(None, ('seq', 'grp'))
- router_mean_new: float32 [2, 1024, 40], P(None, ('seq', 'grp'))
- router_square_new: float32 [2, 1024, 40], P(None, ('seq', 'grp'))
- router_new: float32 [2, 1024, 40], P(None, ('seq', 'grp'))
- gains_mean_new: float32 [1024, 5], P(('seq', 'grp'))
- gains_square_new: float32 [1024, 5], P(('seq', 'grp'))
- gains_new: float32 [1024, 5], P(('seq', 'grp'))
The draws below stay inside these ranges and needn't reach their ends.
Inputs may be any that keep to these rules, and one draw needn't show every extreme that they name: `start_flags`: in each chain the first token starts a document and no other device's first token does; documents start more often toward the end of the chain.
All inputs are finite; a program needn't handle non-finite values.
Results may differ from the reference program's by a relative error of at most 0.015.
Values may be sent and summed in bfloat16 or wider, within the bound.
No kernel may reach another device: no remote copies, remote signals or barrier semaphores. Data moves between devices by JAX's collectives and lax.ppermute only.
A program may use at most 320 MiB of HBM per device.

```python
import math
import jax
import jax.numpy as jnp
import numpy as np
from jax import lax

D = 1024
H = 4
DH = 112
E = 5
TOPK = 2
FF = 4096
V = 8000
L = 2
TOK_DEV = 128
STEP = 10
GROUPS = 4
CHAIN = 1024
QKW = 896
VW = 2240
SELW = 40
CW = 13568
NG = 5
PARAMS = 36066304


def draw_start_flags(key, part):
    key = jax.random.fold_in(key, 11)
    positions = jnp.arange(CHAIN, dtype=jnp.int32)
    device_index = positions // TOK_DEV
    span_count = max(CHAIN // TOK_DEV - 1, 1)
    threshold = 1500000 * (span_count + 2 * device_index) // (span_count * TOK_DEV)
    random_ints = jax.random.randint(key, (GROUPS, CHAIN), 0, 1000000, dtype=jnp.int32)
    start_flags = (random_ints < threshold[None, :]).astype(jnp.int32)
    row_heads = positions % TOK_DEV == 0
    first_flag = (positions == 0).astype(jnp.int32)
    return jnp.where(row_heads[None, :], first_flag[None, :], start_flags)


def draw_layer_weights(key, part):
    key = jax.random.fold_in(key, 12)
    column_idx = jnp.arange(CW)
    inner_scale = D ** (-0.5)
    col_scale = jnp.where(column_idx < QKW + VW, inner_scale, jnp.where(column_idx < QKW + 2 * VW, 0.3, jnp.where(column_idx < QKW + 2 * VW + FF, inner_scale, 1.5 * FF ** (-0.5))))
    base_draw = jax.random.normal(key, (L, D, CW), jnp.float32)
    return base_draw * col_scale


def draw_norm_gains(key, part):
    key = jax.random.fold_in(key, 13)
    ramp_rows = jnp.arange(D, dtype=jnp.float32)[:, None] / D
    return (0.5 + ramp_rows) * jax.random.uniform(key, (D, NG), jnp.float32, 0.9, 1.1)


def touch_ends(values, stream_key, smallest, top_value):
    longest = values.shape.index(max(values.shape))
    spots = []
    for shift in (0, 1):
        where = [jax.random.randint(jax.random.fold_in(stream_key, axis), (), 0, length) for axis, length in enumerate(values.shape)]
        where[longest] = (where[longest] + shift) % values.shape[longest]
        spots.append(tuple(where))
    return values.at[spots[0]].set(smallest).at[spots[1]].set(top_value)


def levels(rng, dims, split, low, largest):
    level = 1.0
    for dim, parts in split:
        draws = jax.random.uniform(jax.random.fold_in(jax.random.fold_in(rng, 6), dim), (parts,), jnp.float32, low / len(split), largest / len(split))
        level = level * jnp.repeat(jnp.exp(draws), dims[dim] // parts).reshape((-1,) + (1,) * (len(dims) - 1 - dim))
    return level


def rank_table(count, lean):
    loads = [(1 << 20) // math.isqrt(standing ** lean) + 1 for standing in range(1, count + 1)]
    width = 1 + sum(loads) // (1 << 30)
    return np.cumsum(np.array([max(1, weight // width) for weight in loads]))


def skewed_ids(key, extent, count, slope):
    grid = rank_table(count, slope)
    pick = jax.random.randint(jax.random.fold_in(key, 1), extent, 0, int(grid[count - 1]))
    standing = jnp.searchsorted(jnp.asarray(grid, jnp.int32), pick, side="right")
    return jax.random.permutation(jax.random.fold_in(key, 2), count)[standing].astype(jnp.int32)


def picks_of(key, rows, amount, top, lift):
    ranking = jax.random.permutation(jax.random.fold_in(key, 1), amount)
    pull = ranking
    for power in range(3):
        pull = pull * pull // amount
    pull = pull * lift // amount
    lots = jax.random.randint(jax.random.fold_in(key, 2), (rows, amount), 0, 4096) + pull
    holders = jax.random.permutation(jax.random.fold_in(key, 3), rows)[jnp.arange(amount) % rows]
    lots = jnp.where(jnp.arange(rows)[:, None] == holders[None, :], 1 << 14, lots)
    merit = lots * amount + jnp.arange(amount)
    return lax.top_k(merit.astype(jnp.int32), top)[1].astype(jnp.int32)


def normal_values(stream_key, extent, deviation, reach, cuts=(), kind=jnp.bfloat16):
    values = jax.random.normal(stream_key, extent, jnp.float32) * deviation
    if len(cuts) > 0:
        values = levels(stream_key, extent, cuts, -0.22, 0.18) * values
    return jnp.clip(values, min=-reach, max=reach).astype(kind)


def setup_inputs(seed: int = 0) -> dict:
    streams_of = jax.random.split(jax.random.key(seed), 17)
    return {
        "token_ids": touch_ends(skewed_ids(streams_of[0], (GROUPS, CHAIN), V, 2), jax.random.fold_in(streams_of[0], 3), 0, V - 1).astype(jnp.int32),
        "target_ids": touch_ends(skewed_ids(streams_of[1], (GROUPS, CHAIN), V, 2), jax.random.fold_in(streams_of[1], 3), 0, V - 1).astype(jnp.int32),
        "start_flags": draw_start_flags(jax.random.fold_in(streams_of[16], 71), 0),
        "route_ids": picks_of(streams_of[3], GROUPS * CHAIN * (2 * L * H), E, TOPK, 0).reshape((GROUPS, CHAIN, 2 * L * H, TOPK)),
        "embed_table": normal_values(streams_of[4], (D, V), (1.5 / D ** 0.5), 0.75, ((0, 32),), jnp.float32),
        "layer_weights": draw_layer_weights(jax.random.fold_in(streams_of[16], 71), 0),
        "router_weights": normal_values(streams_of[6], (L, D, SELW), (0.75 / D ** 0.5), 0.375, ((1, 32),), jnp.float32),
        "norm_gains": draw_norm_gains(jax.random.fold_in(streams_of[16], 71), 0),
        "embed_mean": normal_values(streams_of[8], (D, V), (0.0056 / PARAMS ** 0.5), 1.33514404296875e-05, ((0, 32),), jnp.float32),
        "layer_mean": normal_values(streams_of[9], (L, D, CW), (0.0056 / PARAMS ** 0.5), 1.33514404296875e-05, ((1, 32),), jnp.float32),
        "router_mean": normal_values(streams_of[10], (L, D, SELW), (0.0056 / PARAMS ** 0.5), 1.33514404296875e-05, ((1, 32),), jnp.float32),
        "gains_mean": normal_values(streams_of[11], (D, NG), (0.056 / PARAMS ** 0.5), 0.00012207031, ((0, 32),), jnp.float32),
        "embed_square": jnp.clip(jnp.exp(math.log(5.545342288658384e-13) - 2.7725887 * jax.random.uniform(streams_of[12], (D, V), jnp.float32) ** levels(streams_of[12], (D, V), ((0, 32),), -0.2, 0.2)), 3.46583893041149e-14, 5.545342288658384e-13),
        "layer_square": jnp.clip(jnp.exp(math.log(5.545342288658384e-13) - 2.7725887 * jax.random.uniform(streams_of[13], (L, D, CW), jnp.float32) ** levels(streams_of[13], (L, D, CW), ((1, 32),), -0.2, 0.2)), 3.46583893041149e-14, 5.545342288658384e-13),
        "router_square": jnp.clip(jnp.exp(math.log(5.545342288658384e-13) - 2.7725887 * jax.random.uniform(streams_of[14], (L, D, SELW), jnp.float32) ** levels(streams_of[14], (L, D, SELW), ((1, 32),), -0.2, 0.2)), 3.46583893041149e-14, 5.545342288658384e-13),
        "gains_square": jnp.clip(jnp.exp(math.log(5.545342310342427e-11) - 2.7725887 * jax.random.uniform(streams_of[15], (D, NG), jnp.float32) ** levels(streams_of[15], (D, NG), ((0, 32),), -0.2, 0.2)), 3.465838943964017e-12, 5.545342310342427e-11),
    }


@jax.custom_vjp
def low(v):
    return lax.optimization_barrier(v.astype(jnp.bfloat16)).astype(jnp.float32)

@jax.custom_vjp
def low_back(v):
    return v

def low_keep(v):
    return (low(v), None)

def low_pass(kept, grad):
    return (grad,)

def back_keep(v):
    return (v, None)

def back_low(kept, grad):
    return (low(grad),)
low.defvjp(low_keep, low_pass)
low_back.defvjp(back_keep, back_low)
HIGHEST = lax.Precision.HIGHEST
EPS_NORM = 1e-05
CLIP = 0.05
LR_MATRIX = 0.06
LR_GAIN = 0.3
BETA_FIRST = 0.9
BETA_SECOND = 0.999
EPS_ADAM = 1e-08
DECAY = 0.1

def times_plain(left_side, right_side):
    return jnp.dot(left_side, right_side, precision=HIGHEST)

def times_transposed(left_side, right_side):
    return jnp.einsum('rc,dc->rd', left_side, right_side, precision=HIGHEST)

def rms_norm(values, gain_row):
    return values * lax.rsqrt(lax.optimization_barrier(jnp.mean(values * values, axis=-1, keepdims=True)) + EPS_NORM) * gain_row

def attention(queries, keys_in, values_in, documents):
    row_count = queries.shape[0]
    blank = jnp.zeros((TOK_DEV, H, DH), jnp.float32)
    padded_keys = jnp.concatenate([blank, keys_in])
    padded_values = jnp.concatenate([blank, values_in])
    padded_docs = jnp.concatenate([jnp.full((TOK_DEV,), -1, jnp.int32), documents])
    score_scale = DH ** (-0.5)

    def block_fn(block_index):
        start = (block_index * TOK_DEV).astype(jnp.int32)
        query_block = lax.dynamic_slice_in_dim(queries, start, TOK_DEV)
        key_block = lax.dynamic_slice_in_dim(padded_keys, start, 2 * TOK_DEV)
        value_block = lax.dynamic_slice_in_dim(padded_values, start, 2 * TOK_DEV)
        query_docs = lax.dynamic_slice_in_dim(documents, start, TOK_DEV)
        key_docs = lax.dynamic_slice_in_dim(padded_docs, start, 2 * TOK_DEV)
        query_pos = jnp.arange(TOK_DEV, dtype=jnp.int32) + TOK_DEV
        key_pos = jnp.arange(2 * TOK_DEV, dtype=jnp.int32)
        allowed = (query_docs[:, None] == key_docs[None, :]) & (key_pos[None, :] <= query_pos[:, None])
        raw_scores = low_back(jnp.einsum('qhd,khd->hqk', query_block, key_block, precision=HIGHEST) * score_scale)
        raw_scores = jnp.where(allowed[None], raw_scores, -1e+30)
        soft_probs = jax.nn.softmax(raw_scores, axis=-1)
        return jnp.einsum('hqk,khd->qhd', low(soft_probs), value_block, precision=HIGHEST)
    blocks = lax.map(jax.checkpoint(block_fn), jnp.arange(row_count // TOK_DEV, dtype=jnp.int32))
    return blocks.reshape(row_count, H, DH)

def group_loss(embed_table, layer_weights, router_weights, norm_gains, token_ids, target_ids, documents, doc_weight, gate_mask):
    table_low = low(embed_table)
    weights_low = low(layer_weights)
    selectors_low = low(router_weights)
    gains_low = low(norm_gains)
    row_count = token_ids.shape[0]
    stream = D ** 0.5 * table_low[:, token_ids].T
    for layer_index in range(L):
        weights = weights_low[layer_index]
        normed = low(rms_norm(stream, gains_low[:, 2 * layer_index]))
        query_key = low_back(low(times_plain(normed, weights[:, :QKW])))
        queries = query_key[:, :H * DH].reshape(row_count, H, DH)
        key_rows = query_key[:, H * DH:].reshape(row_count, H, DH)
        selector = low_back(times_plain(normed, selectors_low[layer_index]))
        gate_values = jax.nn.sigmoid(selector).reshape(row_count, 2, H, E) * gate_mask[:, layer_index]
        value_all = low_back(times_plain(normed, weights[:, QKW:QKW + VW])).reshape(row_count, H, E, DH)
        value_rows = low_back(low(lax.optimization_barrier(jnp.sum(gate_values[:, 0, :, :, None] * value_all, axis=2))))
        attended = low_back(attention(queries, key_rows, value_rows, documents))
        mixed = low_back(low((gate_values[:, 1, :, :, None] * attended[:, :, None, :]).reshape(row_count, VW)))
        stream = stream + low_back(times_transposed(mixed, weights[:, QKW + VW:QKW + 2 * VW]))
        second = low(rms_norm(stream, gains_low[:, 2 * layer_index + 1]))
        hidden_pre = low_back(times_plain(second, weights[:, QKW + 2 * VW:QKW + 2 * VW + FF]))
        hidden_low = low(jax.nn.gelu(hidden_pre, approximate=False))
        stream = stream + low_back(times_transposed(hidden_low, weights[:, QKW + 2 * VW + FF:]))
    final = low(rms_norm(stream, gains_low[:, 2 * L]))
    block_rows = math.gcd(512, row_count)

    def head_fn(block):
        final_block, target_block, weight_block = block
        logits = low_back(times_plain(final_block, table_low))
        log_total = jax.nn.logsumexp(logits, axis=-1)
        target_logit = jnp.take_along_axis(logits, target_block[:, None], axis=1)[:, 0]
        return jnp.sum((log_total - target_logit) * weight_block)
    pieces = lax.map(jax.checkpoint(head_fn), (final.reshape(-1, block_rows, D), target_ids.reshape(-1, block_rows), doc_weight.reshape(-1, block_rows)))
    return jnp.sum(pieces)

def adamw_update(master, gradient, first, second, factor, rate, decay):
    gradient = gradient * factor
    first_new = BETA_FIRST * first + (1.0 - BETA_FIRST) * gradient
    second_new = BETA_SECOND * second + (1.0 - BETA_SECOND) * gradient * gradient
    first_hat = first_new / (1.0 - BETA_FIRST ** STEP)
    second_hat = second_new / (1.0 - BETA_SECOND ** STEP)
    master_new = master - rate * (first_hat / (jnp.sqrt(second_hat) + EPS_ADAM) + decay * master)
    return (first_new, second_new, master_new)

def reference(token_ids, target_ids, start_flags, route_ids, embed_table, layer_weights, router_weights, norm_gains, embed_mean, layer_mean, router_mean, gains_mean, embed_square, layer_square, router_square, gains_square):
    doc_count = jnp.sum(start_flags.astype(embed_table.dtype))
    masters = (embed_table, layer_weights, router_weights, norm_gains)
    expert_ids = jnp.arange(E, dtype=jnp.int32)

    def per_group(carry, group):
        group_ids, group_targets, group_starts, group_routes = group
        row_count = group_ids.shape[0]
        documents = jnp.cumsum(group_starts, dtype=jnp.int32) - 1
        doc_length = jax.ops.segment_sum(jnp.ones((row_count,), embed_table.dtype), documents, num_segments=row_count)
        doc_weight = 1.0 / doc_length[documents]
        gate_mask = lax.optimization_barrier(jnp.sum((group_routes[..., None] == expert_ids).astype(embed_table.dtype), axis=-2)).reshape(row_count, L, 2, H, E)

        def loss_of(table_arg, layers_arg, routers_arg, gains_arg):
            return group_loss(table_arg, layers_arg, routers_arg, gains_arg, group_ids, group_targets, documents, doc_weight, gate_mask)
        value, backward = jax.vjp(loss_of, *masters)
        grads = backward(jnp.ones((), value.dtype) / doc_count)
        return ((carry[0] + value, tuple((total + member for total, member in zip(carry[1], grads)))), None)
    initial = (jnp.zeros((), embed_table.dtype), tuple((jnp.zeros_like(member) for member in masters)))
    (loss_sum, grads), _ = lax.scan(per_group, initial, (token_ids, target_ids, start_flags, route_ids))
    grad_norm = jnp.sqrt(sum((jnp.sum(member * member) for member in grads)))
    factor = CLIP / jnp.maximum(grad_norm, CLIP)
    embed_out = adamw_update(embed_table, grads[0], embed_mean, embed_square, factor, LR_MATRIX, DECAY)
    layer_out = adamw_update(layer_weights, grads[1], layer_mean, layer_square, factor, LR_MATRIX, DECAY)
    router_out = adamw_update(router_weights, grads[2], router_mean, router_square, factor, LR_MATRIX, DECAY)
    gains_out = adamw_update(norm_gains, grads[3], gains_mean, gains_square, factor, LR_GAIN, 0.0)
    return (loss_sum, doc_count, grad_norm, embed_out[0], embed_out[1], embed_out[2], layer_out[0], layer_out[1], layer_out[2], router_out[0], router_out[1], router_out[2], gains_out[0], gains_out[1], gains_out[2])
```

```python
import jax
import jax.numpy as jnp
from jax import lax
from jax.experimental import pallas as pl
from jax.experimental.pallas import tpu as pltpu
from jax.sharding import PartitionSpec as P

D = 1024
H = 4
DH = 112
E = 5
FF = 4096
V = 8000
L = 2
STEP = 10
QKW = 896
VW = 2240
SELW = 40
LANE = 128
NG = 5

EPS_NORM = 1e-05
CLIP = 0.05
LR_MATRIX = 0.06
LR_GAIN = 0.3
BETA_FIRST = 0.9
BETA_SECOND = 0.999
EPS_ADAM = 1e-08
DECAY = 0.1

QKV_COLS = (2 + E) * LANE
OUT_COLS = E * LANE
ATT_COLS = QKV_COLS + OUT_COLS
BF = jnp.bfloat16
F32 = jnp.float32


def times_plain(left_side, right_side):
    return jnp.dot(left_side, right_side, preferred_element_type=F32)


def times_transposed(left_side, right_side):
    return lax.dot_general(
        left_side, right_side, (((1,), (1,)), ((), ())), preferred_element_type=F32
    )


def transposed_times(left_side, right_side):
    return lax.dot_general(
        left_side, right_side, (((0,), (0,)), ((), ())), preferred_element_type=F32
    )


def rms_norm(values, gain_row):
    return (
        values * lax.rsqrt(jnp.mean(values * values, axis=-1, keepdims=True) + EPS_NORM) * gain_row
    )


def gelu_exact(values):
    return jax.nn.gelu(values, approximate=False)


def swap_group(values, bit):
    count = lax.axis_size("grp")
    return lax.ppermute(values, "grp", [(member, member ^ bit) for member in range(count)])


def group_bits():
    count = lax.axis_size("grp")
    return [1 << power for power in range(count.bit_length() - 1)]


def spread_rows(values):
    blocks = {0: values}
    for bit in reversed(group_bits()):
        for known in list(blocks):
            blocks[known ^ bit] = swap_group(blocks[known], bit)
    return jnp.concatenate([blocks[index] for index in range(len(blocks))], axis=0)


def merge_rows(values):
    count = lax.axis_size("grp")
    rows = values.shape[0] // count
    blocks = {index: values[index * rows : (index + 1) * rows] for index in range(count)}
    for bit in group_bits():
        away = [index for index in sorted(blocks) if index & bit]
        sent = jnp.concatenate([blocks[index].astype(BF) for index in away], axis=0)
        received = swap_group(sent, bit).astype(F32)
        blocks = {
            index ^ bit: blocks[index ^ bit] + received[place * rows : (place + 1) * rows]
            for place, index in enumerate(away)
        }
    return blocks[0]


def group_exchange(values):
    count = lax.axis_size("grp")
    own = lax.axis_index("grp")
    parts = [lax.dynamic_index_in_dim(values, own, 0, keepdims=False)]
    for offset in range(1, count):
        sent = lax.dynamic_index_in_dim(values, own ^ offset, 0, keepdims=False)
        parts.append(swap_group(sent, offset))
    result = jnp.zeros_like(values)
    for offset in range(count):
        result = lax.dynamic_update_index_in_dim(result, parts[offset], own ^ offset, 0)
    return result


def shifted(value, steps):
    count = lax.axis_size("seq")
    first, last = (max(0, -steps), min(count, count - steps))
    return lax.ppermute(value, "seq", [(source, source + steps) for source in range(first, last)])


def gather_chain(values):
    return lax.all_gather(values, "seq", axis=0, tiled=True)


def scatter_chain(values):
    return lax.psum_scatter(values.astype(BF), "seq", scatter_dimension=0, tiled=True)


def pad_lanes(values):
    return jnp.pad(values, [(0, 0)] * (values.ndim - 1) + [(0, LANE - values.shape[-1])])


def attention_columns(weights, router):
    rows = weights.shape[0]
    query = weights[:, : H * DH].reshape(rows, H, DH)
    key = weights[:, H * DH : QKW].reshape(rows, H, DH)
    value = weights[:, QKW : QKW + VW].reshape(rows, H, E, DH)
    output = weights[:, QKW + VW : QKW + 2 * VW].reshape(rows, H, E, DH)
    select = router.reshape(rows, 2, H, E).transpose(0, 2, 1, 3).reshape(rows, H, 2 * E)
    first = pad_lanes(jnp.concatenate([query, select], axis=2))
    return jnp.concatenate(
        [
            first,
            pad_lanes(key),
            pad_lanes(value).reshape(rows, H, E * LANE),
            pad_lanes(output).reshape(rows, H, E * LANE),
        ],
        axis=2,
    ).transpose(1, 0, 2)


def forward_columns(weights):
    rows = weights.shape[0]
    up = weights[:, QKW + 2 * VW : QKW + 2 * VW + FF].reshape(rows, H, FF // H)
    down = weights[:, QKW + 2 * VW + FF :].reshape(rows, H, FF // H)
    return jnp.concatenate([up, down], axis=2).transpose(1, 0, 2)


def table_columns(table):
    rows = table.shape[0]
    quarter = V // H
    width = -(-quarter // LANE) * LANE
    return jnp.pad(
        table.reshape(rows, H, quarter), [(0, 0), (0, 0), (0, width - quarter)]
    ).transpose(1, 0, 2)


def restore_layer(attention_part, forward_part):
    attention_part = attention_part.transpose(1, 0, 2)
    forward_part = forward_part.transpose(1, 0, 2)
    rows = attention_part.shape[0]
    first = attention_part[:, :, :LANE]
    query = first[:, :, :DH].reshape(rows, H * DH)
    select = first[:, :, DH : DH + 2 * E].reshape(rows, H, 2, E)
    select = select.transpose(0, 2, 1, 3).reshape(rows, SELW)
    key = attention_part[:, :, LANE : LANE + DH].reshape(rows, H * DH)

    def experts(start):
        part = attention_part[:, :, start : start + E * LANE].reshape(rows, H, E, LANE)
        return part[..., :DH].reshape(rows, VW)

    up = forward_part[:, :, : FF // H].reshape(rows, FF)
    down = forward_part[:, :, FF // H :].reshape(rows, FF)
    joined = jnp.concatenate(
        [query, key, experts(2 * LANE), experts(QKV_COLS), up, down], axis=1
    )
    return joined, select


def lookup_body(ids_ref, table_ref, out_ref, by_token, picked):
    rows = table_ref.shape[0]
    width = table_ref.shape[1]
    for start in range(0, width, LANE):
        end = min(start + LANE, width)
        by_token[start:end, :rows] = table_ref[:, start:end].T

    @pl.loop(0, out_ref.shape[0])
    def _(device):
        base = device * LANE

        for token in range(LANE):
            picked[pl.ds(token, 1), :] = by_token[pl.ds(ids_ref[base + token], 1), :]
        out_ref[device] = picked[...].T[:rows]


def lookup(ids, table):
    rows, width = table.shape
    devices = ids.shape[0] // LANE
    return pl.pallas_call(
        lookup_body,
        grid_spec=pltpu.PrefetchScalarGridSpec(
            num_scalar_prefetch=1,
            grid=(1,),
            in_specs=[pl.BlockSpec((rows, width), lambda i, ids: (0, 0))],
            out_specs=pl.BlockSpec((devices, rows, LANE), lambda i, ids: (0, 0, 0)),
            scratch_shapes=[pltpu.VMEM((width, LANE), F32), pltpu.VMEM((LANE, LANE), F32)],
        ),
        out_shape=jax.ShapeDtypeStruct((devices, rows, LANE), F32),
        compiler_params=pltpu.CompilerParams(vmem_limit_bytes=48 * 1024 * 1024),
        name="lookup",
    )(ids, table)


ACCUMULATORS = 4


def spread_body(ids_ref, grad_ref, out_ref, *scratch):
    rows = out_ref.shape[0]
    width = out_ref.shape[1]
    totals, picked = scratch[:-1], scratch[-1]
    for total in totals:
        total[...] = jnp.zeros_like(total)

    @pl.loop(0, grad_ref.shape[0])
    def _(device):
        base = device * LANE
        picked[:, :rows] = grad_ref[device].T

        for step in range(LANE // ACCUMULATORS):
            for which, total in enumerate(totals):
                token = step * ACCUMULATORS + which
                place = pl.ds(ids_ref[base + token], 1)
                total[place, :] += picked[pl.ds(token, 1), :]

    for start in range(0, width, LANE):
        end = min(start + LANE, width)
        out_ref[:, start:end] = sum(total[start:end, :] for total in totals).T[:rows]


def spread_tokens(ids, grads, width):
    devices, rows, _ = grads.shape
    return pl.pallas_call(
        spread_body,
        grid_spec=pltpu.PrefetchScalarGridSpec(
            num_scalar_prefetch=1,
            grid=(1,),
            in_specs=[pl.BlockSpec((devices, rows, LANE), lambda i, ids: (0, 0, 0))],
            out_specs=pl.BlockSpec((rows, width), lambda i, ids: (0, 0)),
            scratch_shapes=[pltpu.VMEM((width, LANE), F32) for _ in range(ACCUMULATORS)]
            + [pltpu.VMEM((LANE, LANE), F32)],
        ),
        out_shape=jax.ShapeDtypeStruct((rows, width), F32),
        compiler_params=pltpu.CompilerParams(vmem_limit_bytes=48 * 1024 * 1024),
        name="spread",
    )(ids, grads)


def allowed_keys(segment, memory_tail):
    positions = jnp.arange(segment.shape[1], dtype=jnp.int32)
    own_block = (segment[:, :, None] == segment[:, None, :]) & (
        positions[None, None, :] <= positions[None, :, None]
    )
    past_block = (segment[:, :, None] == 0) & (memory_tail[:, None, :] > 0)
    return jnp.concatenate([past_block, own_block], axis=2)


def masked_scores(queries, all_keys, allowed_mask):
    raw_scores = jnp.einsum("cqd,ckd->cqk", queries, all_keys, preferred_element_type=F32) * DH ** (
        -0.5
    )
    return jnp.where(allowed_mask, raw_scores, -1e30)


def forward_layer(stream_in, pieces, gain_attention, gain_forward, gate_mask, segment, memory_tail):
    attention_weight, forward_weight = pieces
    chain_count, row_count = segment.shape
    total_rows = chain_count * row_count
    qkv_weight = attention_weight[:, :QKV_COLS]
    out_weight = attention_weight[:, QKV_COLS:]
    normed_low = rms_norm(stream_in, gain_attention).astype(BF)
    normed_all = spread_rows(normed_low)
    projected = times_plain(normed_all, qkv_weight)
    head_lanes = jnp.arange(LANE) < DH
    queries = jnp.where(head_lanes, projected[:, :LANE], 0.0).astype(BF)
    queries = queries.reshape(chain_count, row_count, LANE)
    key_rows = projected[:, LANE : 2 * LANE].astype(BF).reshape(chain_count, row_count, LANE)
    selector = projected[:, DH : DH + 2 * E]
    squashed = jax.nn.sigmoid(selector).reshape(total_rows, 2, E)
    gate_values = squashed * gate_mask
    value_all = projected[:, 2 * LANE :].reshape(total_rows, E, LANE)
    value_rows = sum(gate_values[:, 0, e, None] * value_all[:, e] for e in range(E))
    value_rows = value_rows.astype(BF).reshape(chain_count, row_count, LANE)
    memory = shifted(jnp.concatenate([key_rows, value_rows], axis=2), 1)
    all_keys = jnp.concatenate([memory[..., :LANE], key_rows], axis=1)
    all_values = jnp.concatenate([memory[..., LANE:], value_rows], axis=1)
    allowed_mask = allowed_keys(segment, memory_tail)
    raw_scores = masked_scores(queries, all_keys, allowed_mask)
    log_total = jax.nn.logsumexp(raw_scores, axis=-1)
    soft_low = jnp.exp(raw_scores - log_total[..., None]).astype(BF)
    attended = jnp.einsum(
        "cqk,ckd->cqd", soft_low, all_values, preferred_element_type=F32
    ).reshape(total_rows, LANE)
    mixed_low = jnp.concatenate(
        [(gate_values[:, 1, e, None] * attended).astype(BF) for e in range(E)], axis=1
    )
    stream_mid = stream_in + merge_rows(times_transposed(mixed_low, out_weight))
    second_low = rms_norm(stream_mid, gain_forward).astype(BF)
    second_all = spread_rows(second_low)
    up_weight = forward_weight[:, : FF // H]
    down_weight = forward_weight[:, FF // H :]
    hidden_pre = times_plain(second_all, up_weight)
    hidden_low = gelu_exact(hidden_pre).astype(BF)
    stream_out = stream_mid + merge_rows(times_transposed(hidden_low, down_weight))
    stored = (
        stream_in,
        normed_all,
        squashed,
        gate_values,
        gate_mask,
        value_all,
        queries,
        all_keys,
        all_values,
        allowed_mask,
        log_total,
        attended,
        mixed_low,
        stream_mid,
        second_all,
        hidden_pre,
        hidden_low,
    )
    return (stream_out, stored)


def backward_layer(grad_out, pieces, gain_attention, gain_forward, stored):
    (
        stream_in,
        normed_all,
        squashed,
        gate_values,
        gate_mask,
        value_all,
        queries,
        all_keys,
        all_values,
        allowed_mask,
        log_total,
        attended,
        mixed_low,
        stream_mid,
        second_all,
        hidden_pre,
        hidden_low,
    ) = stored
    attention_weight, forward_weight = pieces
    qkv_weight = attention_weight[:, :QKV_COLS]
    out_weight = attention_weight[:, QKV_COLS:]
    up_weight = forward_weight[:, : FF // H]
    down_weight = forward_weight[:, FF // H :]
    chain_count, row_count = (queries.shape[0], queries.shape[1])
    total_rows = chain_count * row_count
    d_down_out = spread_rows(grad_out.astype(BF))
    d_hidden = times_plain(d_down_out, down_weight)
    gelu_value, gelu_back = jax.vjp(gelu_exact, hidden_pre)
    d_hidden_pre = gelu_back(d_hidden)[0].astype(BF)
    d_second = merge_rows(times_transposed(d_hidden_pre, up_weight))
    grad_down = transposed_times(d_down_out, hidden_low)
    grad_up = transposed_times(second_all, d_hidden_pre)
    norm_value, norm_back = jax.vjp(rms_norm, stream_mid, gain_forward)
    d_from_second, grad_gain_forward = norm_back(d_second)
    grad_mid = grad_out + d_from_second
    d_branch = spread_rows(grad_mid.astype(BF))
    grad_output = transposed_times(d_branch, mixed_low)
    d_mixed = times_plain(d_branch, out_weight).astype(BF).reshape(total_rows, E, LANE)
    d_attended = sum(gate_values[:, 1, e, None] * d_mixed[:, e] for e in range(E)).astype(BF)
    d_gate_output = jnp.sum(d_mixed * attended[:, None, :], axis=2)
    d_attended = d_attended.reshape(chain_count, row_count, LANE)
    raw_scores = masked_scores(queries, all_keys, allowed_mask)
    soft_probs = jnp.exp(raw_scores - log_total[..., None])
    d_soft = jnp.einsum("cqd,ckd->cqk", d_attended, all_values, preferred_element_type=F32)
    row_delta = jnp.sum(soft_probs * d_soft, axis=-1, keepdims=True)
    d_scores = (soft_probs * (d_soft - row_delta)).astype(BF)
    score_scale = DH ** (-0.5)
    d_all_keys = (
        jnp.einsum("cqk,cqd->ckd", d_scores, queries, preferred_element_type=F32) * score_scale
    )
    d_all_values = jnp.einsum(
        "cqk,cqd->ckd", soft_probs.astype(BF), d_attended, preferred_element_type=F32
    )
    d_all = jnp.concatenate([d_all_keys, d_all_values], axis=2)
    returned = shifted(d_all[:, :row_count].astype(BF), -1).astype(F32)
    d_query = jnp.einsum("cqk,ckd->cqd", d_scores, all_keys, preferred_element_type=F32)
    d_query = (d_query * score_scale).reshape(total_rows, LANE)
    d_own = (d_all[:, row_count:] + returned).astype(BF).reshape(total_rows, 2 * LANE)
    d_key = d_own[:, :LANE]
    d_value = d_own[:, LANE:]
    d_value_all = jnp.concatenate(
        [(gate_values[:, 0, e, None] * d_value).astype(BF) for e in range(E)], axis=1
    )
    d_gate_value = jnp.sum(d_value[:, None, :] * value_all, axis=2)
    d_gate_values = jnp.stack([d_gate_value, d_gate_output], axis=1) * gate_mask
    d_selector = (d_gate_values * squashed * (1.0 - squashed)).reshape(total_rows, -1)
    d_first = jnp.concatenate(
        [d_query[:, :DH], d_selector, jnp.zeros((total_rows, LANE - DH - 2 * E), F32)], axis=1
    ).astype(BF)
    d_projected = jnp.concatenate([d_first, d_key, d_value_all], axis=1)
    d_normed = merge_rows(times_transposed(d_projected, qkv_weight))
    grad_projected = transposed_times(normed_all, d_projected)
    norm_value_first, norm_back_first = jax.vjp(rms_norm, stream_in, gain_attention)
    d_stream_in, grad_gain_attention = norm_back_first(d_normed)
    return (
        grad_mid + d_stream_in,
        (
            jnp.concatenate([grad_projected, grad_output], axis=1),
            jnp.concatenate([grad_up, grad_down], axis=1),
        ),
        [grad_gain_attention, grad_gain_forward],
    )


def reduce_columns(gradient):
    count = lax.axis_size("grp")
    summed = scatter_chain(gradient)
    summed = summed.reshape(count, summed.shape[0] // count, summed.shape[1])
    return group_exchange(summed.astype(BF)).astype(F32)


def adamw_update(master, gradient, first, second, factor, rate, decay):
    gradient = gradient * factor
    first_new = BETA_FIRST * first + (1.0 - BETA_FIRST) * gradient
    second_new = BETA_SECOND * second + (1.0 - BETA_SECOND) * gradient * gradient
    first_hat = first_new / (1.0 - BETA_FIRST**STEP)
    second_hat = second_new / (1.0 - BETA_SECOND**STEP)
    master_new = master - rate * (first_hat / (jnp.sqrt(second_hat) + EPS_ADAM) + decay * master)
    return (first_new, second_new, master_new)


def all_sum(values):
    devices = lax.axis_size("seq") * lax.axis_size("grp")
    sent = jnp.broadcast_to(values[None], (devices,) + values.shape)
    return jnp.sum(
        lax.all_to_all(sent, ("seq", "grp"), split_axis=0, concat_axis=0, tiled=True), axis=0
    )


def document_weights(segment, seg_total, runs, seq_here, row_count):
    seq_count = runs.shape[0]
    device_ids = jnp.arange(seq_count, dtype=jnp.int32)[:, None]
    starts_there = runs[:, :, 0] > 0
    left_pick = jnp.max(jnp.where(starts_there & (device_ids < seq_here), device_ids, -1), axis=0)
    left_run = jnp.where(
        left_pick >= 0,
        jnp.sum(jnp.where(device_ids == left_pick, runs[:, :, 2], 0), axis=0)
        + (seq_here - 1 - left_pick) * row_count,
        0,
    )
    right_pick = jnp.min(
        jnp.where(starts_there & (device_ids > seq_here), device_ids, seq_count), axis=0
    )
    right_run = (
        jnp.sum(jnp.where(device_ids == right_pick, runs[:, :, 1], 0), axis=0)
        + (right_pick - seq_here - 1) * row_count
    )
    local_length = jnp.sum((segment[:, :, None] == segment[:, None, :]).astype(jnp.int32), axis=2)
    doc_length = (
        local_length
        + jnp.where(segment == 0, left_run[:, None], 0)
        + jnp.where(segment == seg_total[:, None], right_run[:, None], 0)
    )
    return 1.0 / doc_length.astype(F32)


def local(
    token_ids,
    target_ids,
    start_flags,
    route_ids,
    embed_table,
    layer_weights,
    router_weights,
    norm_gains,
    embed_mean,
    layer_mean,
    router_mean,
    gains_mean,
    embed_square,
    layer_square,
    router_square,
    gains_square,
):
    row_count = token_ids.shape[1]
    group_count = lax.axis_size("grp")
    own_group = lax.axis_index("grp")
    seq_count = lax.axis_size("seq")
    seq_here = lax.axis_index("seq")
    device_count = seq_count * group_count
    own_rows = embed_table.shape[0]
    positions = jnp.arange(row_count, dtype=jnp.int32)
    quarter = V // group_count

    total_abs = jnp.sum(start_flags, axis=1)
    first_start = jnp.min(jnp.where(start_flags > 0, positions[None, :], row_count), axis=1)
    last_start = jnp.max(jnp.where(start_flags > 0, positions[None, :], -1), axis=1)
    tail_count = jnp.where(total_abs > 0, row_count - last_start, row_count)
    summary = jnp.concatenate([total_abs, first_start, tail_count])
    summary = jnp.pad(summary, (0, row_count - summary.shape[0]))
    told = jnp.stack([token_ids[0], target_ids[0], summary])
    heard = lax.all_to_all(
        jnp.broadcast_to(told[None], (device_count,) + told.shape),
        ("seq", "grp"),
        split_axis=0,
        concat_axis=0,
        tiled=True,
    )
    all_ids = heard[:, 0].reshape(-1)
    heard = heard.reshape(seq_count, group_count, 3, row_count)
    runs = heard[:, 0, 2, : 3 * group_count].reshape(seq_count, 3, group_count).transpose(0, 2, 1)
    doc_count = jnp.sum(runs[:, :, 0]).astype(F32)

    relative = own_group ^ jnp.arange(group_count, dtype=jnp.int32)
    flags = jnp.take(start_flags, relative, axis=0)
    segment = jnp.cumsum(flags, axis=1, dtype=jnp.int32)
    seg_total = segment[:, -1]
    doc_weight = document_weights(
        segment, seg_total, jnp.take(runs, relative, axis=1), seq_here, row_count
    )
    targets = lax.dynamic_index_in_dim(heard[:, :, 1], seq_here, 0, keepdims=False)
    targets = jnp.take(targets, relative, axis=0)
    memory_tail = shifted((segment == seg_total[:, None]).astype(BF), 1)
    routes = jnp.take(route_ids, relative, axis=0).reshape(
        group_count, row_count, 2 * L, H, 2
    )
    routes = lax.dynamic_index_in_dim(routes, own_group, 3, keepdims=False)
    expert_ids = jnp.arange(E, dtype=jnp.int32)
    gate_all = jnp.sum((routes[..., None] == expert_ids).astype(F32), axis=-2).reshape(
        group_count * row_count, L, 2, E
    )

    weights_low = layer_weights.astype(BF)
    router_low = router_weights.astype(BF)
    pieces = []
    for layer_index in range(L):
        for arranged in (
            attention_columns(weights_low[layer_index], router_low[layer_index]),
            forward_columns(weights_low[layer_index]),
        ):
            swapped = group_exchange(arranged)
            pieces.append(gather_chain(swapped.reshape(-1, swapped.shape[2])))
    table_low = embed_table.astype(BF)
    swapped = group_exchange(table_columns(table_low))
    table_part = gather_chain(swapped.reshape(-1, swapped.shape[2]))
    saved_pieces = [pieces[2 * index : 2 * index + 2] for index in range(L)]

    looked = lookup(all_ids, embed_table).astype(BF) * D**0.5
    gain_rows = norm_gains.astype(BF).T
    gain_rows = jnp.pad(gain_rows, [(0, 16 - NG), (0, row_count - own_rows)])
    sent = jnp.concatenate(
        [looked, jnp.broadcast_to(gain_rows[None], (device_count,) + gain_rows.shape)], axis=1
    )
    received = lax.all_to_all(sent, ("seq", "grp"), split_axis=0, concat_axis=0, tiled=True)
    stream = received[:, :own_rows].reshape(D, row_count).T.astype(F32)
    gains = received[:, own_rows : own_rows + NG, :own_rows].astype(F32)
    gains = gains.transpose(1, 0, 2).reshape(NG, D)

    saved_layers = []
    for layer_index in range(L):
        stream, stored = forward_layer(
            stream,
            saved_pieces[layer_index],
            gains[2 * layer_index],
            gains[2 * layer_index + 1],
            gate_all[:, layer_index],
            segment,
            memory_tail,
        )
        saved_layers.append(stored)

    final_gain = gains[2 * L]
    final_low = rms_norm(stream, final_gain).astype(BF)
    final_all = spread_rows(final_low)
    logits = times_plain(final_all, table_part)
    columns = jnp.arange(logits.shape[1], dtype=jnp.int32)[None, :]
    logits = jnp.where(columns < quarter, logits, -1e30)
    hit = columns == (targets.reshape(-1) - own_group * quarter)[:, None]
    hit = hit & (columns < quarter)
    log_part = jax.nn.logsumexp(logits, axis=-1).reshape(group_count, row_count)
    target_part = jnp.sum(jnp.where(hit, logits, 0.0), axis=1).reshape(group_count, row_count)
    stats = jnp.stack([log_part, target_part], axis=1)
    others = [stats]
    for offset in range(1, group_count):
        got = swap_group(stats, offset)
        others.append(jnp.stack([got[index ^ offset] for index in range(group_count)]))
    others = jnp.stack(others)
    log_total = jax.nn.logsumexp(others[:, :, 0], axis=0)
    target_logit = jnp.sum(others[:, :, 1], axis=0)
    loss_local = jnp.sum((log_total[0] - target_logit[0]) * doc_weight[0])
    scale = (doc_weight / doc_count).reshape(-1)[:, None]
    d_logits = (jnp.exp(logits - log_total.reshape(-1)[:, None]) - hit.astype(F32)) * scale
    d_logits = d_logits.astype(BF)
    d_final = merge_rows(times_transposed(d_logits, table_part))
    table_grad = reduce_columns(transposed_times(final_all, d_logits))
    table_grad = table_grad[:, :, :quarter].transpose(1, 0, 2).reshape(own_rows, V)
    final_value, final_back = jax.vjp(rms_norm, stream, final_gain)
    d_stream, grad_final_gain = final_back(d_final)

    layer_parts = [None] * L
    gain_parts = [None] * L
    for layer_index in reversed(range(L)):
        d_stream, grads, gain_pair = backward_layer(
            d_stream,
            saved_pieces[layer_index],
            gains[2 * layer_index],
            gains[2 * layer_index + 1],
            saved_layers[layer_index],
        )
        layer_parts[layer_index] = restore_layer(*[reduce_columns(member) for member in grads])
        gain_parts[layer_index] = gain_pair

    gain_grads = jnp.stack(sum(gain_parts, []) + [grad_final_gain])
    gain_grads = gain_grads.reshape(NG, device_count, own_rows).transpose(1, 0, 2)
    gain_grads = jnp.pad(gain_grads, [(0, 0), (0, 16 - NG), (0, row_count - own_rows)])
    sent = jnp.concatenate([d_stream.T.reshape(device_count, own_rows, row_count), gain_grads], axis=1)
    received = lax.all_to_all(
        sent.astype(BF), ("seq", "grp"), split_axis=0, concat_axis=0, tiled=True
    ).astype(F32)
    embed_grad = table_grad + D**0.5 * spread_tokens(all_ids, received[:, :own_rows], V)
    gains_grad = jnp.sum(received[:, own_rows : own_rows + NG, :own_rows], axis=0).T
    layer_grad = jnp.stack([member[0] for member in layer_parts])
    router_grad = jnp.stack([member[1] for member in layer_parts])
    square = (
        jnp.sum(embed_grad * embed_grad)
        + jnp.sum(layer_grad * layer_grad)
        + jnp.sum(router_grad * router_grad)
        + jnp.sum(gains_grad * gains_grad)
    )
    sums = all_sum(jnp.stack([loss_local, square]))
    loss_sum = sums[0]
    grad_norm = jnp.sqrt(sums[1])
    factor = CLIP / jnp.maximum(grad_norm, CLIP)
    embed_out = adamw_update(
        embed_table, embed_grad, embed_mean, embed_square, factor, LR_MATRIX, DECAY
    )
    layer_out = adamw_update(
        layer_weights, layer_grad, layer_mean, layer_square, factor, LR_MATRIX, DECAY
    )
    router_out = adamw_update(
        router_weights, router_grad, router_mean, router_square, factor, LR_MATRIX, DECAY
    )
    gains_out = adamw_update(norm_gains, gains_grad, gains_mean, gains_square, factor, LR_GAIN, 0.0)
    return (
        loss_sum,
        doc_count,
        grad_norm,
        embed_out[0],
        embed_out[1],
        embed_out[2],
        layer_out[0],
        layer_out[1],
        layer_out[2],
        router_out[0],
        router_out[1],
        router_out[2],
        gains_out[0],
        gains_out[1],
        gains_out[2],
    )


def solution(mesh):
    rows = P(("seq", "grp"), None)
    layers = P(None, ("seq", "grp"), None)
    return jax.shard_map(
        local,
        mesh=mesh,
        in_specs=(
            P("grp", "seq"),
            P("grp", "seq"),
            P(None, "seq"),
            P(None, "seq", None, None),
            rows,
            layers,
            layers,
            rows,
            rows,
            layers,
            layers,
            rows,
            rows,
            layers,
            layers,
            rows,
        ),
        out_specs=(P(), P(), P()) + (rows,) * 3 + (layers,) * 6 + (rows,) * 3,
        check_vma=False,
    )
```

```python
import jax
import jax.numpy as jnp
from jax import lax
from jax.experimental import pallas as pl
from jax.experimental.pallas import tpu as pltpu
from jax.sharding import PartitionSpec as P

D = 1024
H = 4
DH = 112
E = 5
FF = 4096
V = 8000
L = 2
STEP = 10
QKW = 896
VW = 2240
SELW = 40
LANE = 128
NG = 5

EPS_NORM = 1e-05
CLIP = 0.05
LR_MATRIX = 0.06
LR_GAIN = 0.3
BETA_FIRST = 0.9
BETA_SECOND = 0.999
EPS_ADAM = 1e-08
DECAY = 0.1

QKV_COLS = (2 + E) * LANE
OUT_COLS = E * LANE
ATT_COLS = QKV_COLS + OUT_COLS
BF = jnp.bfloat16
F32 = jnp.float32


def times_plain(left_side, right_side):
    return jnp.dot(left_side, right_side, preferred_element_type=F32)


def times_transposed(left_side, right_side):
    return lax.dot_general(
        left_side, right_side, (((1,), (1,)), ((), ())), preferred_element_type=F32
    )


def transposed_times(left_side, right_side):
    return lax.dot_general(
        left_side, right_side, (((0,), (0,)), ((), ())), preferred_element_type=F32
    )


def rms_norm(values, gain_row):
    return (
        values * lax.rsqrt(jnp.mean(values * values, axis=-1, keepdims=True) + EPS_NORM) * gain_row
    )


def gelu_exact(values):
    return jax.nn.gelu(values, approximate=False)


def swap_group(values, bit):
    count = lax.axis_size("grp")
    return lax.ppermute(values, "grp", [(member, member ^ bit) for member in range(count)])


def group_bits():
    count = lax.axis_size("grp")
    return [1 << power for power in range(count.bit_length() - 1)]


def spread_rows(values):
    blocks = {0: values}
    for bit in reversed(group_bits()):
        for known in list(blocks):
            blocks[known ^ bit] = swap_group(blocks[known], bit)
    return jnp.concatenate([blocks[index] for index in range(len(blocks))], axis=0)


def merge_rows(values):
    count = lax.axis_size("grp")
    rows = values.shape[0] // count
    blocks = {index: values[index * rows : (index + 1) * rows] for index in range(count)}
    for bit in group_bits():
        away = [index for index in sorted(blocks) if index & bit]
        sent = jnp.concatenate([blocks[index].astype(BF) for index in away], axis=0)
        received = swap_group(sent, bit).astype(F32)
        blocks = {
            index ^ bit: blocks[index ^ bit] + received[place * rows : (place + 1) * rows]
            for place, index in enumerate(away)
        }
    return blocks[0]


def group_exchange(values):
    count = lax.axis_size("grp")
    own = lax.axis_index("grp")
    cases = [values[member] for member in range(count)]
    parts = [lax.select_n(own ^ offset, *cases) for offset in range(count)]
    parts = [parts[0]] + [swap_group(parts[offset], offset) for offset in range(1, count)]
    return jnp.stack([lax.select_n(own ^ member, *parts) for member in range(count)])


def shifted(value, steps):
    count = lax.axis_size("seq")
    first, last = (max(0, -steps), min(count, count - steps))
    return lax.ppermute(value, "seq", [(source, source + steps) for source in range(first, last)])


RING_LIMIT = 8


def ring_order(count):
    return list(range(0, count, 2)) + list(range(count - 1, 0, -2))


def ring_pairs(count, step):
    order = ring_order(count)
    return [(order[place], order[(place + step) % count]) for place in range(count)]


def ring_place(device, count):
    return jnp.where(device % 2 == 0, device // 2, count - 1 - device // 2)


def ring_device(place, count):
    return jnp.where(2 * place < count, 2 * place, 2 * (count - 1 - place) + 1)


class Gather:
    def __init__(self, values, ring=True):
        self.count = lax.axis_size("seq")
        self.whole = None
        self.blocks = {0: values}
        self.left = self.count // 2
        if self.count > RING_LIMIT or not ring:
            self.whole = lax.all_gather(values, "seq", axis=0, tiled=True)
            self.left = 0
        self.flying = (values, values)

    def land(self):
        return self.flying

    def step(self, landed):
        ahead, behind = landed
        done = self.count // 2 - self.left + 1
        ahead = lax.ppermute(ahead, "seq", ring_pairs(self.count, 1))
        self.blocks[self.count - done] = ahead
        if done < self.count - self.count // 2:
            behind = lax.ppermute(behind, "seq", ring_pairs(self.count, -1))
            self.blocks[done] = behind
        self.flying = (ahead, behind)
        self.left -= 1

    def result(self):
        while self.left:
            self.step(self.flying)
        if self.whole is not None:
            return [self.whole]
        return [self.blocks[place] for place in range(len(self.blocks))]


class Scatter:
    def __init__(self, left, right, rows):
        self.count = lax.axis_size("seq")
        self.parts, self.rows = (left, right), rows
        self.left = self.count // 2
        self.whole = None
        if self.count > RING_LIMIT:
            joined = jnp.concatenate(self.parts, axis=1)
            self.whole = lax.psum_scatter(joined, "seq", scatter_dimension=0, tiled=True)
            self.left = 0
        self.flying = ()

    def land(self):
        return self.flying

    def step(self, landed):
        back = self.count - 1 - self.count // 2
        done = self.count // 2 - self.left
        places, received = [self.left], [landed[:1]]
        if done < back:
            places.append(self.count - back + done)
            received.append(landed[1:])
        sums = add_blocks(*self.parts, places, received, self.rows)
        ahead = lax.ppermute(sums[0], "seq", ring_pairs(self.count, 1))
        behind = landed[1] if done >= back else lax.ppermute(
            sums[1], "seq", ring_pairs(self.count, -1)
        )
        self.flying = (ahead, behind)
        self.left -= 1

    def result(self):
        while self.left:
            self.step(self.flying)
        if self.whole is not None:
            return self.whole
        return add_blocks(*self.parts, [0], [self.flying], self.rows)[0]


class Feed:
    def __init__(self, tasks=(), width=1):
        self.waiting = list(tasks)
        self.width = width
        self.flying = []

    def tie(self, values, width=1):
        landed = [task.land() for task in self.flying]
        values, landed = lax.optimization_barrier((values, landed))
        for task, arrived in zip(self.flying, landed):
            task.flying = tuple(arrived)
        self.start(width)
        return values

    def start(self, width=1):
        self.waiting = [task for task in self.waiting if task.left]
        self.flying = self.waiting[:width]
        for task in self.flying:
            task.step(task.flying)


def ring_owners():
    count = lax.axis_size("seq")
    if count > RING_LIMIT:
        return jnp.zeros((1,), jnp.int32)
    here = ring_place(lax.axis_index("seq"), count)
    return ring_device(lax.rem(jnp.arange(count, dtype=jnp.int32) + here, count), count)


def ring_places():
    count = lax.axis_size("seq")
    if count > RING_LIMIT:
        return jnp.zeros((1,), jnp.int32)
    here = ring_place(lax.axis_index("seq"), count)
    devices = jnp.arange(count, dtype=jnp.int32)
    return lax.rem(ring_place(devices, count) - here + count, count)


def pick_blocks(values, order):
    if order.shape[0] == 1:
        return values
    shape = values.shape
    return jnp.take(values.reshape((order.shape[0], -1) + shape[1:]), order, axis=0).reshape(shape)


def to_ring(values):
    return pick_blocks(values, ring_owners())


def from_ring(values):
    return pick_blocks(values, ring_places())


def after(values, *others):
    return lax.optimization_barrier((values, *others))[0]


def pad_lanes(values):
    return jnp.pad(values, [(0, 0)] * (values.ndim - 1) + [(0, LANE - values.shape[-1])])


def attention_columns(weights, router):
    rows = weights.shape[0]
    query = weights[:, : H * DH].reshape(rows, H, DH)
    key = weights[:, H * DH : QKW].reshape(rows, H, DH)
    value = weights[:, QKW : QKW + VW].reshape(rows, H, E, DH)
    output = weights[:, QKW + VW : QKW + 2 * VW].reshape(rows, H, E, DH)
    select = router.reshape(rows, 2, H, E).transpose(0, 2, 1, 3).reshape(rows, H, 2 * E)
    first = pad_lanes(jnp.concatenate([query, select], axis=2))
    return jnp.concatenate(
        [
            first,
            pad_lanes(key),
            pad_lanes(value).reshape(rows, H, E * LANE),
            pad_lanes(output).reshape(rows, H, E * LANE),
        ],
        axis=2,
    ).transpose(1, 0, 2)


def forward_columns(weights):
    rows = weights.shape[0]
    up = weights[:, QKW + 2 * VW : QKW + 2 * VW + FF].reshape(rows, H, FF // H)
    down = weights[:, QKW + 2 * VW + FF :].reshape(rows, H, FF // H)
    return jnp.concatenate([up, down], axis=2).transpose(1, 0, 2)


def table_columns(table):
    rows = table.shape[0]
    quarter = V // H
    width = -(-quarter // LANE) * LANE
    return jnp.pad(
        table.reshape(rows, H, quarter), [(0, 0), (0, 0), (0, width - quarter)]
    ).transpose(1, 0, 2)


def lookup_body(ids_ref, table_ref, out_ref, by_token, picked):
    rows = table_ref.shape[0]
    width = table_ref.shape[1]
    for start in range(0, width, LANE):
        end = min(start + LANE, width)
        by_token[start:end, :rows] = table_ref[:, start:end].T

    @pl.loop(0, out_ref.shape[0])
    def _(device):
        base = device * LANE

        for token in range(LANE):
            picked[pl.ds(token, 1), :] = by_token[pl.ds(ids_ref[base + token], 1), :]
        out_ref[device] = picked[...].T[:rows]


def lookup(ids, table):
    rows, width = table.shape
    devices = ids.shape[0] // LANE
    return pl.pallas_call(
        lookup_body,
        grid_spec=pltpu.PrefetchScalarGridSpec(
            num_scalar_prefetch=1,
            grid=(1,),
            in_specs=[pl.BlockSpec((rows, width), lambda i, ids: (0, 0))],
            out_specs=pl.BlockSpec((devices, rows, LANE), lambda i, ids: (0, 0, 0)),
            scratch_shapes=[pltpu.VMEM((width, LANE), F32), pltpu.VMEM((LANE, LANE), F32)],
        ),
        out_shape=jax.ShapeDtypeStruct((devices, rows, LANE), F32),
        compiler_params=pltpu.CompilerParams(vmem_limit_bytes=48 * 1024 * 1024),
        name="lookup",
    )(ids, table)


ACCUMULATORS = 4


def spread_body(ids_ref, grad_ref, table_ref, out_ref, square_ref, *scratch):
    rows, width = out_ref.shape
    members = table_ref.shape[0]
    totals, picked = scratch[:-1], scratch[-1]
    for total in totals:
        total[...] = jnp.zeros_like(total)

    @pl.loop(0, grad_ref.shape[0])
    def _(device):
        base = device * LANE
        picked[:, :rows] = grad_ref[device].T

        for step in range(LANE // ACCUMULATORS):
            for which, total in enumerate(totals):
                token = step * ACCUMULATORS + which
                place = pl.ds(ids_ref[base + token], 1)
                total[place, :] += picked[pl.ds(token, 1), :]

    for start in range(0, width, LANE):
        end = min(start + LANE, width)
        found = sum(total[start:end, :] for total in totals).T[:rows]
        out_ref[:, start:end] = found * D**0.5
    quarter = width // members
    table = jnp.concatenate([table_ref[member][:, :quarter] for member in range(members)], axis=1)
    total = out_ref[...] + table.astype(F32)
    out_ref[...] = total
    square_ref[0, 0] = jnp.sum(total * total)


def spread_tokens(ids, grads, table_parts, width):
    devices, rows, _ = grads.shape
    return pl.pallas_call(
        spread_body,
        grid_spec=pltpu.PrefetchScalarGridSpec(
            num_scalar_prefetch=1,
            grid=(1,),
            in_specs=[
                pl.BlockSpec((devices, rows, LANE), lambda i, ids: (0, 0, 0)),
                pl.BlockSpec(table_parts.shape, lambda i, ids: (0, 0, 0)),
            ],
            out_specs=[
                pl.BlockSpec((rows, width), lambda i, ids: (0, 0)),
                pl.BlockSpec(memory_space=pltpu.SMEM),
            ],
            scratch_shapes=[pltpu.VMEM((width, LANE), F32) for _ in range(ACCUMULATORS)]
            + [pltpu.VMEM((LANE, LANE), F32)],
        ),
        out_shape=[
            jax.ShapeDtypeStruct((rows, width), F32),
            jax.ShapeDtypeStruct((1, 1), F32),
        ],
        compiler_params=pltpu.CompilerParams(vmem_limit_bytes=48 * 1024 * 1024),
        name="spread",
    )(ids, grads, table_parts)


VMEM_LIMIT = 56 * 1024 * 1024
SCALE = DH ** (-0.5)


def whole(array):
    return pl.BlockSpec(array.shape, lambda step: (0,) * array.ndim)


def part(shape):
    return pl.BlockSpec(shape, lambda step: (0,) * len(shape))


def in_scalars():
    return pl.BlockSpec(memory_space=pltpu.SMEM)


def anywhere():
    return pl.BlockSpec(memory_space=pl.ANY)


def call(body, name, inputs, specs, outputs, scratch, ties=()):
    ties = tuple(ties)

    def wrapped(*refs):
        count = len(inputs)
        body(*refs[:count], *refs[count + len(ties) :])

    return pl.pallas_call(
        wrapped,
        grid=(1,),
        in_specs=list(specs) + [anywhere()] * len(ties),
        out_specs=[part(shape) for shape, _ in outputs],
        out_shape=[jax.ShapeDtypeStruct(shape, kind) for shape, kind in outputs],
        scratch_shapes=scratch,
        compiler_params=pltpu.CompilerParams(vmem_limit_bytes=VMEM_LIMIT),
        cost_estimate=pl.CostEstimate(flops=1, bytes_accessed=1, transcendentals=0),
        name=name,
    )(*inputs, *ties)


class Weights:
    def __init__(self, arrays, base=0):
        self.arrays, self.base = list(arrays), base
        self.natural = len(self.arrays) == 1
        self.count = ring_owners().shape[0] if self.natural else len(self.arrays)

    def specs(self):
        return [anywhere() for _ in self.arrays]

    def copies(self, owners, refs, start, width, target, semaphores):
        copies = []
        rows = D // self.count
        columns = pl.ds(self.base + start, width)
        for index in range(self.count):
            if not self.natural:
                source = refs[index].at[:, columns]
            elif self.count == 1:
                source = refs[0].at[:, columns]
            else:
                place = pl.multiple_of(owners[index] * rows, rows)
                source = refs[0].at[pl.ds(place, rows), columns]
            copy = pltpu.make_async_copy(
                source, target.at[pl.ds(index * rows, rows)], semaphores.at[index]
            )
            copy.start()
            copies.append(copy)
        return copies


def gate_column(gates, kind, expert):
    place = DH + kind * E + expert
    return gates[:, place : place + 1]


def expert_lanes(values, expert):
    return values[:, expert * LANE : (expert + 1) * LANE]


def dot_nn(left, right):
    return lax.dot_general(left, right, (((1,), (0,)), ((), ())), preferred_element_type=F32)


def dot_nt(left, right):
    return lax.dot_general(left, right, (((1,), (1,)), ((), ())), preferred_element_type=F32)


def dot_tn(left, right):
    return lax.dot_general(left, right, (((0,), (0,)), ((), ())), preferred_element_type=F32)


def store_split(keep, send, pair, values, rows):
    keep[pl.ds(pair * rows, rows), :] = values[:rows]
    send[pl.ds(pair * rows, rows), :] = values[rows:].astype(BF)


def project(blocks, weights, owners, mask, ties=()):
    chains, rows = len(blocks), blocks[0].shape[0]
    total = chains * rows
    arrays = len(weights.arrays)

    def body(owner_ref, *refs):
        xs, ws, mask_ref = refs[:chains], refs[chains : chains + arrays], refs[chains + arrays]
        normed, queries, key_value, value_all, squashed, weight, semaphores = refs[
            chains + arrays + 1 :
        ]
        copies = weights.copies(owner_ref, ws, 0, QKV_COLS, weight, semaphores)
        for chain in range(chains):
            normed[chain * rows : (chain + 1) * rows, :] = xs[chain][...]
        for copy in copies:
            copy.wait()

        @pl.loop(0, chains // 2)
        def _(pair):
            at = pl.ds(pair * 2 * rows, 2 * rows)
            projected = dot_nn(normed[at, :], weight[...])
            first = projected[:, :LANE]
            lanes = lax.broadcasted_iota(jnp.int32, first.shape, 1)
            queries[at, :] = jnp.where(lanes < DH, first, 0.0).astype(BF)
            soft = jax.nn.sigmoid(first)
            squashed[at, :] = soft
            gates = soft * mask_ref[at, :]
            values = projected[:, 2 * LANE :]
            value_all[at, :] = values
            mixed = sum(
                gate_column(gates, 0, expert) * expert_lanes(values, expert) for expert in range(E)
            )
            key_value[at, :LANE] = projected[:, LANE : 2 * LANE].astype(BF)
            key_value[at, LANE:] = mixed.astype(BF)

    return call(
        body,
        "project",
        (owners, *blocks, *weights.arrays, mask),
        [in_scalars()] + [whole(block) for block in blocks] + weights.specs() + [whole(mask)],
        [
            ((total, D), BF),
            ((total, LANE), BF),
            ((total, 2 * LANE), BF),
            ((total, E * LANE), F32),
            ((total, LANE), F32),
        ],
        [pltpu.VMEM((D, QKV_COLS), BF), pltpu.SemaphoreType.DMA((weights.count,))],
        ties,
    )


def probabilities(queries, keys, allowed):
    scores = jnp.where(allowed > 0, dot_nt(queries, keys) * SCALE, -1e30)
    raised = jnp.exp(scores - jnp.max(scores, axis=1, keepdims=True))
    return raised / jnp.sum(raised, axis=1, keepdims=True)


def attend(queries, key_value, memory, squashed, mask, allowed, weights, owners, rows, ties=()):
    total = queries.shape[0]
    chains = total // rows

    def body(owner_ref, q_ref, own_ref, past_ref, squash_ref, mask_ref, allow_ref, *refs):
        ws = refs[: len(weights.arrays)]
        attended, mixed, keep, send, weight, semaphores = refs[len(weights.arrays) :]
        copies = weights.copies(owner_ref, ws, QKV_COLS, OUT_COLS, weight, semaphores)
        for chain in range(chains):
            at = slice(chain * rows, (chain + 1) * rows)
            keys = jnp.concatenate([past_ref[at, :LANE], own_ref[at, :LANE]], axis=0)
            values = jnp.concatenate([past_ref[at, LANE:], own_ref[at, LANE:]], axis=0)
            soft = probabilities(q_ref[at, :], keys, allow_ref[at, :])
            got = dot_nn(soft.astype(BF), values)
            attended[at, :] = got
            gates = squash_ref[at, :] * mask_ref[at, :]
            for expert in range(E):
                mixed[at, expert * LANE : (expert + 1) * LANE] = (
                    gate_column(gates, 1, expert) * got
                ).astype(BF)
        for copy in copies:
            copy.wait()

        @pl.loop(0, chains // 2)
        def _(pair):
            out = dot_nt(mixed[pl.ds(pair * 2 * rows, 2 * rows), :], weight[...])
            store_split(keep, send, pair, out, rows)

    return call(
        body,
        "attend",
        (owners, queries, key_value, memory, squashed, mask, allowed, *weights.arrays),
        [in_scalars()]
        + [whole(array) for array in (queries, key_value, memory, squashed, mask, allowed)]
        + weights.specs(),
        [
            ((total, LANE), F32),
            ((total, E * LANE), BF),
            ((total // 2, D), F32),
            ((total // 2, D), BF),
        ],
        [pltpu.VMEM((D, OUT_COLS), BF), pltpu.SemaphoreType.DMA((weights.count,))],
        ties,
    )


def feed(blocks, weights, owners, ties=()):
    chains, rows = len(blocks), blocks[0].shape[0]
    total = chains * rows
    width = FF // H
    count, arrays = weights.count, len(weights.arrays)

    def body(owner_ref, *refs):
        xs, ws = refs[:chains], refs[chains : chains + arrays]
        second, hidden, slope, keep, send, up, down, up_sems, down_sems = refs[
            chains + arrays :
        ]
        up_copies = weights.copies(owner_ref, ws, 0, width, up, up_sems)
        down_copies = weights.copies(owner_ref, ws, width, width, down, down_sems)
        for chain in range(chains):
            second[chain * rows : (chain + 1) * rows, :] = xs[chain][...]
        for copy in up_copies:
            copy.wait()

        @pl.loop(0, chains // 2)
        def _(pair):
            at = pl.ds(pair * 2 * rows, 2 * rows)
            pre = dot_nn(second[at, :], up[...])
            rising = 0.5 * (1.0 + lax.erf(pre * 0.5**0.5))
            hidden[at, :] = (pre * rising).astype(BF)
            slope[at, :] = rising + pre * jnp.exp(-0.5 * pre * pre) * 0.3989422804014327

        for copy in down_copies:
            copy.wait()

        @pl.loop(0, chains // 2)
        def _(pair):
            out = dot_nt(hidden[pl.ds(pair * 2 * rows, 2 * rows), :], down[...])
            store_split(keep, send, pair, out, rows)

    return call(
        body,
        "feed",
        (owners, *blocks, *weights.arrays),
        [in_scalars()] + [whole(block) for block in blocks] + weights.specs(),
        [
            ((total, D), BF),
            ((total, width), BF),
            ((total, width), F32),
            ((total // 2, D), F32),
            ((total // 2, D), BF),
        ],
        [pltpu.VMEM((D, width), BF)] * 2 + [pltpu.SemaphoreType.DMA((count,))] * 2,
        ties,
    )


def feed_back(blocks, weights, owners, slope, ties=()):
    chains, rows = len(blocks), blocks[0].shape[0]
    total = chains * rows
    width = FF // H
    count, arrays = weights.count, len(weights.arrays)

    def body(owner_ref, *refs):
        ds, ws = refs[:chains], refs[chains : chains + arrays]
        slope_ref, d_out, d_pre, keep, send, up, down, up_sems, down_sems = refs[
            chains + arrays :
        ]
        down_copies = weights.copies(owner_ref, ws, width, width, down, down_sems)
        up_copies = weights.copies(owner_ref, ws, 0, width, up, up_sems)
        for chain in range(chains):
            d_out[chain * rows : (chain + 1) * rows, :] = ds[chain][...]
        for copy in down_copies:
            copy.wait()

        @pl.loop(0, chains // 2)
        def _(pair):
            at = pl.ds(pair * 2 * rows, 2 * rows)
            d_pre[at, :] = (dot_nn(d_out[at, :], down[...]) * slope_ref[at, :]).astype(BF)

        for copy in up_copies:
            copy.wait()

        @pl.loop(0, chains // 2)
        def _(pair):
            out = dot_nt(d_pre[pl.ds(pair * 2 * rows, 2 * rows), :], up[...])
            store_split(keep, send, pair, out, rows)

    return call(
        body,
        "feed_back",
        (owners, *blocks, *weights.arrays, slope),
        [in_scalars()] + [whole(block) for block in blocks] + weights.specs() + [whole(slope)],
        [
            ((total, D), BF),
            ((total, width), BF),
            ((total // 2, D), F32),
            ((total // 2, D), BF),
        ],
        [pltpu.VMEM((D, width), BF)] * 2 + [pltpu.SemaphoreType.DMA((count,))] * 2,
        ties,
    )


def attend_back(
    blocks, queries, key_value, memory, squashed, mask, allowed, attended, weights, owners, ties=()
):
    chains, rows = len(blocks), blocks[0].shape[0]
    total = chains * rows
    count = len(weights.arrays)

    def body(owner_ref, *refs):
        ds, refs = refs[:chains], refs[chains:]
        q_ref, own_ref, past_ref, squash_ref, mask_ref, allow_ref, att_ref = refs[:7]
        ws, refs = refs[7 : 7 + count], refs[7 + count :]
        d_branch, d_query, d_gate, d_own, d_past, weight, semaphores = refs
        copies = weights.copies(owner_ref, ws, QKV_COLS, OUT_COLS, weight, semaphores)
        for chain in range(chains):
            d_branch[chain * rows : (chain + 1) * rows, :] = ds[chain][...]
        for copy in copies:
            copy.wait()
        for pair in range(chains // 2):
            pair_mixed = dot_nn(
                d_branch[pair * 2 * rows : (pair + 1) * 2 * rows, :], weight[...]
            ).astype(BF)
            for side in range(2):
                chain = pair * 2 + side
                at = slice(chain * rows, (chain + 1) * rows)
                d_mixed = pair_mixed[side * rows : (side + 1) * rows].astype(F32)
                gates = squash_ref[at, :] * mask_ref[at, :]
                d_att = sum(
                    gate_column(gates, 1, expert) * expert_lanes(d_mixed, expert)
                    for expert in range(E)
                ).astype(BF)
                got = att_ref[at, :]
                lanes = lax.broadcasted_iota(jnp.int32, (rows, LANE), 1)
                d_gates = jnp.zeros((rows, LANE), F32)
                for expert in range(E):
                    column = jnp.sum(expert_lanes(d_mixed, expert) * got, axis=1, keepdims=True)
                    d_gates = jnp.where(lanes == DH + E + expert, column, d_gates)
                d_gate[at, :] = d_gates
                keys = jnp.concatenate([past_ref[at, :LANE], own_ref[at, :LANE]], axis=0)
                values = jnp.concatenate([past_ref[at, LANE:], own_ref[at, LANE:]], axis=0)
                query = q_ref[at, :]
                soft = probabilities(query, keys, allow_ref[at, :])
                d_soft = dot_nt(d_att, values)
                delta = jnp.sum(soft * d_soft, axis=1, keepdims=True)
                d_scores = (soft * (d_soft - delta)).astype(BF)
                d_query[at, :] = dot_nn(d_scores, keys) * SCALE
                d_keys = dot_tn(d_scores, query) * SCALE
                d_values = dot_tn(soft.astype(BF), d_att)
                d_past[at, :LANE] = d_keys[:rows].astype(BF)
                d_past[at, LANE:] = d_values[:rows].astype(BF)
                d_own[at, :LANE] = d_keys[rows:]
                d_own[at, LANE:] = d_values[rows:]

    arrays = (queries, key_value, memory, squashed, mask, allowed, attended)
    return call(
        body,
        "attend_back",
        (owners, *blocks, *arrays, *weights.arrays),
        [in_scalars()]
        + [whole(block) for block in blocks]
        + [whole(array) for array in arrays]
        + weights.specs(),
        [
            ((total, D), BF),
            ((total, LANE), F32),
            ((total, LANE), F32),
            ((total, 2 * LANE), F32),
            ((total, 2 * LANE), BF),
        ],
        [pltpu.VMEM((D, OUT_COLS), BF), pltpu.SemaphoreType.DMA((weights.count,))],
        ties,
    )


def project_back(
    d_query, d_gate, d_own, returned, squashed, mask, value_all, weights, owners, rows, ties=()
):
    total = d_query.shape[0]
    chains = total // rows

    def body(owner_ref, dq_ref, dg_ref, own_ref, back_ref, squash_ref, mask_ref, value_ref, *refs):
        ws = refs[: len(weights.arrays)]
        d_projected, keep, send, weight, semaphores = refs[len(weights.arrays) :]
        copies = weights.copies(owner_ref, ws, 0, QKV_COLS, weight, semaphores)
        for chain in range(chains):
            at = slice(chain * rows, (chain + 1) * rows)
            d_own = own_ref[at, :] + back_ref[at, :].astype(F32)
            soft = squash_ref[at, :]
            gates = soft * mask_ref[at, :]
            d_value = d_own[:, LANE:].astype(BF).astype(F32)
            lanes = lax.broadcasted_iota(jnp.int32, (rows, LANE), 1)
            d_gates = dg_ref[at, :]
            for expert in range(E):
                column = jnp.sum(
                    d_value * value_ref[at, expert * LANE : (expert + 1) * LANE],
                    axis=1,
                    keepdims=True,
                )
                d_gates = jnp.where(lanes == DH + expert, column, d_gates)
                start = (2 + expert) * LANE
                d_projected[at, start : start + LANE] = (
                    gate_column(gates, 0, expert) * d_value
                ).astype(BF)
            d_select = d_gates * mask_ref[at, :] * soft * (1.0 - soft)
            first = jnp.where(lanes < DH, dq_ref[at, :], d_select)
            d_projected[at, :LANE] = first.astype(BF)
            d_projected[at, LANE : 2 * LANE] = d_own[:, :LANE].astype(BF)
        for copy in copies:
            copy.wait()

        @pl.loop(0, chains // 2)
        def _(pair):
            out = dot_nt(d_projected[pl.ds(pair * 2 * rows, 2 * rows), :], weight[...])
            store_split(keep, send, pair, out, rows)

    arrays = (d_query, d_gate, d_own, returned, squashed, mask, value_all)
    return call(
        body,
        "project_back",
        (owners, *arrays, *weights.arrays),
        [in_scalars()] + [whole(array) for array in arrays] + weights.specs(),
        [((total, QKV_COLS), BF), ((total // 2, D), F32), ((total // 2, D), BF)],
        [pltpu.VMEM((D, QKV_COLS), BF), pltpu.SemaphoreType.DMA((weights.count,))],
        ties,
    )


def join_norm(stream, sums, gain, ties=()):
    rows = stream.shape[0]

    def body(stream_ref, keep_ref, near_ref, far_ref, gain_ref, joined, normed):
        values = (
            stream_ref[...]
            + keep_ref[...]
            + near_ref[...].astype(F32)
            + far_ref[...].astype(F32)
        )
        joined[...] = values
        scale = lax.rsqrt(jnp.mean(values * values, axis=1, keepdims=True) + EPS_NORM)
        normed[...] = (values * scale * gain_ref[...]).astype(BF)

    block = part((rows, D))
    return call(
        body,
        "join_norm",
        (stream, *sums, gain),
        [block, block, block, block, part((1, D))],
        [((rows, D), F32), ((rows, D), BF)],
        [],
        ties,
    )


def norm_back(grad_out, sums, stream, gain, ties=()):
    rows = stream.shape[0]

    def body(out_ref, keep_ref, near_ref, far_ref, stream_ref, gain_ref, grad, low, gain_grad):
        d_norm = keep_ref[...] + near_ref[...].astype(F32) + far_ref[...].astype(F32)
        values = stream_ref[...]
        scale = lax.rsqrt(jnp.mean(values * values, axis=1, keepdims=True) + EPS_NORM)
        unit = values * scale
        gain_grad[...] = jnp.sum(d_norm * unit, axis=0, keepdims=True)
        d_unit = d_norm * gain_ref[...]
        inner = jnp.mean(d_unit * unit, axis=1, keepdims=True)
        total = out_ref[...] + scale * (d_unit - unit * inner)
        grad[...] = total
        low[...] = total.astype(BF)

    block = part((rows, D))
    return call(
        body,
        "norm_back",
        (grad_out, *sums, stream, gain),
        [block] * 5 + [part((1, D))],
        [((rows, D), F32), ((rows, D), BF), ((1, D), F32)],
        [],
        ties,
    )


def grad_whole(pairs, places):
    total = pairs[0][0].shape[0]
    rows = D // places.shape[0]
    widths = [d_part.shape[1] for _, d_part in pairs]

    def body(place_ref, *refs):
        count = len(pairs)
        start = 0
        for left, part_ref, width in zip(refs[:count], refs[count : 2 * count], widths):
            turned = left[...].T
            for first in range(0, width, 512):
                size = min(512, width - first)
                value = dot_nn(turned, part_ref[:, first : first + size])
                refs[-1][:, start + first : start + first + size] = value.astype(BF)
            start += width

    return pl.pallas_call(
        body,
        grid_spec=pltpu.PrefetchScalarGridSpec(
            num_scalar_prefetch=1,
            grid=(places.shape[0],),
            in_specs=[pl.BlockSpec((total, rows), lambda step, at: (0, at[step])) for _ in pairs]
            + [pl.BlockSpec((total, width), lambda step, at: (0, 0)) for width in widths],
            out_specs=pl.BlockSpec((rows, sum(widths)), lambda step, at: (step, 0)),
        ),
        out_shape=jax.ShapeDtypeStruct((D, sum(widths)), BF),
        compiler_params=pltpu.CompilerParams(vmem_limit_bytes=VMEM_LIMIT),
        cost_estimate=pl.CostEstimate(flops=1, bytes_accessed=1, transcendentals=0),
        name="grad_whole",
    )(places, *[left for left, _ in pairs], *[d_part for _, d_part in pairs])


def add_blocks(left, right, places, received, rows):
    widths = (left.shape[1], right.shape[1])
    flat = [array for arrays in received for array in arrays]

    def body(*refs):
        count = len(places)
        parts = (refs[:count], refs[count : 2 * count])
        arrived = list(refs[2 * count : 2 * count + len(flat)])
        outs = refs[2 * count + len(flat) :]
        for index in range(count):
            mine = [arrived.pop(0) for _ in received[index]]
            start = 0
            for part_refs, width in zip(parts, widths):
                at = slice(start, start + width)
                value = part_refs[index][...].astype(F32)
                for ref in mine:
                    value = value + ref[:, at].astype(F32)
                outs[index][:, at] = value.astype(BF)
                start += width

    def row_blocks(width):
        return [
            pl.BlockSpec((rows, width), lambda step, place=place: (place, 0)) for place in places
        ]

    return call(
        body,
        "add_blocks",
        (*[left] * len(places), *[right] * len(places), *flat),
        row_blocks(widths[0]) + row_blocks(widths[1]) + [whole(array) for array in flat],
        [((rows, sum(widths)), BF) for _ in places],
        [],
    )


def spread_blocks(values, feeder=None):
    blocks = {0: values}
    for bit in reversed(group_bits()):
        for known in list(blocks):
            blocks[known ^ bit] = swap_group(blocks[known], bit)
            if feeder is not None and bit > 1:
                blocks[known ^ bit] = feeder.tie(blocks[known ^ bit], feeder.width)
    return [blocks[index] for index in range(len(blocks))]


def merge_sums(keep, send, feeder=None):
    count = lax.axis_size("grp")
    assert count == 4
    rows = keep.shape[0] // (count // 2)
    near = swap_group(send, 1)
    blocks = {
        index: keep[index * rows : (index + 1) * rows] + near[index * rows : (index + 1) * rows].astype(F32)
        for index in range(1, count // 2)
    }
    far = swap_group(blocks[1].astype(BF), 2)
    if feeder is not None:
        far = feeder.tie(far)
    return keep, near, far


def forward_layer(
    state, attention_weights, forward_weights, owners, gains, mask, allowed, rows, feeder
):
    stream, normed_low = state
    blocks = feeder.tie(spread_blocks(normed_low, feeder))
    attention_weights = attention_weights()
    normed, queries, key_value, value_all, squashed = project(
        blocks, attention_weights, owners, mask
    )
    memory = feeder.tie(shifted(key_value, 1))
    attended, mixed, keep, send = attend(
        queries, key_value, memory, squashed, mask, allowed, attention_weights, owners, rows
    )
    stream_mid, second_low = join_norm(stream, merge_sums(keep, send, feeder), gains[0])
    blocks = feeder.tie(spread_blocks(second_low, feeder))
    forward_weights = forward_weights()
    second, hidden, slope, keep, send = feed(blocks, forward_weights, owners)
    send = feeder.tie(send)
    stream_out, next_low = join_norm(stream_mid, merge_sums(keep, send, feeder), gains[1])
    stored = (
        stream,
        normed,
        queries,
        key_value,
        memory,
        value_all,
        squashed,
        attended,
        mixed,
        stream_mid,
        second,
        hidden,
        slope,
    )
    return (stream_out, next_low), stored, (attention_weights, forward_weights)


def backward_layer(
    state, attention_weights, forward_weights, owners, gains, mask, allowed, stored, rows, feeder
):
    (
        stream,
        normed,
        queries,
        key_value,
        memory,
        value_all,
        squashed,
        attended,
        mixed,
        stream_mid,
        second,
        hidden,
        slope,
    ) = stored
    grad_out, grad_low = state
    block_rows = D // owners.shape[0]
    blocks = spread_blocks(grad_low, feeder)
    d_out, d_pre, keep, send = feed_back(blocks, forward_weights, owners, slope)
    sums = merge_sums(keep, send)
    parts = (
        transposed_times(second, d_pre).astype(BF),
        transposed_times(d_out, hidden).astype(BF),
    )
    sums, parts = lax.optimization_barrier((sums, parts))
    forward_grad = Scatter(*parts, block_rows)
    feeder.waiting.append(forward_grad)
    sums = feeder.tie(sums, 2)
    grad_mid, grad_mid_low, gain_forward = norm_back(grad_out, sums, stream_mid, gains[1])
    blocks = spread_blocks(grad_mid_low, feeder)
    d_branch, d_query, d_gate, d_own, d_past = attend_back(
        blocks, queries, key_value, memory, squashed, mask, allowed, attended, attention_weights, owners
    )
    returned = feeder.tie(shifted(d_past, -1), 2)
    d_projected, keep, send = project_back(
        d_query, d_gate, d_own, returned, squashed, mask, value_all, attention_weights, owners, rows
    )
    sums = merge_sums(keep, send)
    parts = (
        transposed_times(normed, d_projected).astype(BF),
        transposed_times(d_branch, mixed).astype(BF),
    )
    sums, parts = lax.optimization_barrier((sums, parts))
    attention_grad = Scatter(*parts, block_rows)
    feeder.waiting.append(attention_grad)
    sums = feeder.tie(sums, 2)
    grad_in, grad_in_low, gain_attention = norm_back(grad_mid, sums, stream, gains[0])
    return (grad_in, grad_in_low), (attention_grad, forward_grad), [gain_attention, gain_forward]


def scatter_whole(gradient):
    return lax.psum_scatter(gradient, "seq", scatter_dimension=0, tiled=True)


def own_columns(summed):
    count = lax.axis_size("grp")
    summed = summed.reshape(count, summed.shape[0] // count, summed.shape[1])
    return group_exchange(summed.astype(BF))


def allowed_keys(segment, memory_tail):
    positions = jnp.arange(segment.shape[1], dtype=jnp.int32)
    own_block = (segment[:, :, None] == segment[:, None, :]) & (
        positions[None, None, :] <= positions[None, :, None]
    )
    past_block = (segment[:, :, None] == 0) & (memory_tail[:, None, :] > 0)
    return jnp.concatenate([past_block, own_block], axis=2)


def adamw_update(master, gradient, first, second, factor, rate, decay):
    gradient = gradient * factor
    first_new = BETA_FIRST * first + (1.0 - BETA_FIRST) * gradient
    second_new = BETA_SECOND * second + (1.0 - BETA_SECOND) * gradient * gradient
    first_hat = first_new / (1.0 - BETA_FIRST**STEP)
    second_hat = second_new / (1.0 - BETA_SECOND**STEP)
    master_new = master - rate * (first_hat / (jnp.sqrt(second_hat) + EPS_ADAM) + decay * master)
    return (first_new, second_new, master_new)


def update_layers(factor, grads, masters, firsts, seconds):
    rows = masters[0].shape[1]
    chunk = 8 * DH

    def body(factor_ref, *refs):
        parts = refs[: 2 * L]
        ins = refs[2 * L : 2 * L + 6]
        outs = refs[2 * L + 6 :]
        scale = factor_ref[0, 0]

        def apply(kind, columns, gradient):
            old = [ref[0, :, columns] for ref in ins[3 * kind : 3 * kind + 3]]
            first, second, master = adamw_update(
                old[0], gradient, old[1], old[2], scale, LR_MATRIX, DECAY
            )
            new = (master, first, second)
            for ref, values in zip(outs[3 * kind : 3 * kind + 3], new):
                ref[0, :, columns] = values

        for layer in range(L):

            @pl.when(pl.program_id(0) == layer)
            def _(layer=layer):
                attention, forward = parts[2 * layer : 2 * layer + 2]

                def heads(start):
                    return [
                        attention[member, :, start : start + DH].astype(F32)
                        for member in range(H)
                    ]

                def experts(start):
                    return [
                        attention[member, :, start + e * LANE : start + e * LANE + DH].astype(F32)
                        for member in range(H)
                        for e in range(E)
                    ]

                chunks = heads(0) + heads(LANE) + experts(2 * LANE) + experts(QKV_COLS)
                for group in range(len(chunks) // 8):
                    gradient = jnp.concatenate(chunks[8 * group : 8 * group + 8], axis=1)
                    apply(0, slice(group * chunk, (group + 1) * chunk), gradient)
                base = QKW + 2 * VW
                for side in range(2):
                    for member in range(H):
                        width = FF // H
                        start = base + side * FF + member * width
                        gradient = forward[member, :, side * width : (side + 1) * width]
                        apply(0, slice(start, start + width), gradient.astype(F32))
                selects = [
                    attention[member, :, DH + kind * E : DH + (kind + 1) * E].astype(F32)
                    for kind in range(2)
                    for member in range(H)
                ]
                apply(1, slice(0, SELW), jnp.concatenate(selects, axis=1))

    def layer_block(array):
        return pl.BlockSpec((1,) + array.shape[1:], lambda step: (step, 0, 0))

    flat = [part for pair in grads for part in pair]
    states = [masters[0], firsts[0], seconds[0], masters[1], firsts[1], seconds[1]]
    return pl.pallas_call(
        body,
        grid=(L,),
        in_specs=[in_scalars()]
        + [pl.BlockSpec(part.shape, lambda step: (0, 0, 0)) for part in flat]
        + [layer_block(array) for array in states],
        out_specs=[layer_block(array) for array in states],
        out_shape=[jax.ShapeDtypeStruct(array.shape, F32) for array in states],
        compiler_params=pltpu.CompilerParams(vmem_limit_bytes=VMEM_LIMIT),
        name="update_layers",
    )(factor, *flat, *states)


def all_sum(values):
    devices = lax.axis_size("seq") * lax.axis_size("grp")
    sent = jnp.broadcast_to(values[None], (devices,) + values.shape)
    return jnp.sum(
        lax.all_to_all(sent, ("seq", "grp"), split_axis=0, concat_axis=0, tiled=True), axis=0
    )


def document_weights(segment, seg_total, runs, seq_here, row_count):
    seq_count = runs.shape[0]
    device_ids = jnp.arange(seq_count, dtype=jnp.int32)[:, None]
    starts_there = runs[:, :, 0] > 0
    left_pick = jnp.max(jnp.where(starts_there & (device_ids < seq_here), device_ids, -1), axis=0)
    left_run = jnp.where(
        left_pick >= 0,
        jnp.sum(jnp.where(device_ids == left_pick, runs[:, :, 2], 0), axis=0)
        + (seq_here - 1 - left_pick) * row_count,
        0,
    )
    right_pick = jnp.min(
        jnp.where(starts_there & (device_ids > seq_here), device_ids, seq_count), axis=0
    )
    right_run = (
        jnp.sum(jnp.where(device_ids == right_pick, runs[:, :, 1], 0), axis=0)
        + (right_pick - seq_here - 1) * row_count
    )
    local_length = jnp.sum((segment[:, :, None] == segment[:, None, :]).astype(jnp.int32), axis=2)
    doc_length = (
        local_length
        + jnp.where(segment == 0, left_run[:, None], 0)
        + jnp.where(segment == seg_total[:, None], right_run[:, None], 0)
    )
    return 1.0 / doc_length.astype(F32)


def local(
    token_ids,
    target_ids,
    start_flags,
    route_ids,
    embed_table,
    layer_weights,
    router_weights,
    norm_gains,
    embed_mean,
    layer_mean,
    router_mean,
    gains_mean,
    embed_square,
    layer_square,
    router_square,
    gains_square,
):
    row_count = token_ids.shape[1]
    group_count = lax.axis_size("grp")
    own_group = lax.axis_index("grp")
    seq_count = lax.axis_size("seq")
    seq_here = lax.axis_index("seq")
    device_count = seq_count * group_count
    own_rows = embed_table.shape[0]
    positions = jnp.arange(row_count, dtype=jnp.int32)
    quarter = V // group_count

    total_abs = jnp.sum(start_flags, axis=1)
    first_start = jnp.min(jnp.where(start_flags > 0, positions[None, :], row_count), axis=1)
    last_start = jnp.max(jnp.where(start_flags > 0, positions[None, :], -1), axis=1)
    tail_count = jnp.where(total_abs > 0, row_count - last_start, row_count)
    summary = jnp.concatenate([total_abs, first_start, tail_count])
    summary = jnp.pad(summary, (0, row_count - summary.shape[0]))
    told = jnp.stack([token_ids[0], target_ids[0], summary])
    heard = lax.all_to_all(
        jnp.broadcast_to(told[None], (device_count,) + told.shape),
        ("seq", "grp"),
        split_axis=0,
        concat_axis=0,
        tiled=True,
    )
    all_ids = heard[:, 0].reshape(-1)
    heard = heard.reshape(seq_count, group_count, 3, row_count)
    runs = heard[:, 0, 2, : 3 * group_count].reshape(seq_count, 3, group_count).transpose(0, 2, 1)
    doc_count = jnp.sum(runs[:, :, 0]).astype(F32)

    relative = own_group ^ jnp.arange(group_count, dtype=jnp.int32)
    flags = jnp.take(start_flags, relative, axis=0)
    segment = jnp.cumsum(flags, axis=1, dtype=jnp.int32)
    seg_total = segment[:, -1]
    doc_weight = document_weights(
        segment, seg_total, jnp.take(runs, relative, axis=1), seq_here, row_count
    )
    targets = lax.dynamic_index_in_dim(heard[:, :, 1], seq_here, 0, keepdims=False)
    targets = jnp.take(targets, relative, axis=0)
    memory_tail = shifted((segment == seg_total[:, None]).astype(BF), 1)
    routes = jnp.take(route_ids, relative, axis=0).reshape(
        group_count, row_count, 2 * L, H, 2
    )
    routes = lax.dynamic_index_in_dim(routes, own_group, 3, keepdims=False)
    expert_ids = jnp.arange(E, dtype=jnp.int32)
    gate_all = jnp.sum((routes[..., None] == expert_ids).astype(F32), axis=-2)
    gate_all = gate_all.reshape(group_count * row_count, L, 2 * E).transpose(1, 0, 2)
    gate_all = jnp.pad(gate_all, [(0, 0), (0, 0), (DH, LANE - DH - 2 * E)])
    allowed = allowed_keys(segment, memory_tail).astype(F32)
    allowed = allowed.reshape(group_count * row_count, 2 * row_count)

    def exchanged(arranged):
        swapped = group_exchange(arranged)
        return swapped.reshape(-1, swapped.shape[2])

    owners = ring_owners()
    first = exchanged(
        attention_columns(layer_weights[0].astype(BF), router_weights[0].astype(BF))
    )
    gate_all, first, weights = lax.optimization_barrier((gate_all, first, layer_weights[0]))
    first_attention = Gather(first)
    first_forward = Gather(exchanged(forward_columns(weights.astype(BF))))
    feeder = Feed([first_attention])
    feeder.start()
    all_ids, gate_all, first_forward.flying = feeder.tie((all_ids, gate_all, first_forward.flying))
    feeder.waiting.append(first_forward)

    looked = lookup(all_ids, embed_table).astype(BF) * D**0.5
    looked = feeder.tie(looked)
    gain_rows = norm_gains.astype(BF).T
    gain_rows = jnp.pad(gain_rows, [(0, 16 - NG), (0, row_count - own_rows)])
    sent = jnp.concatenate(
        [looked, jnp.broadcast_to(gain_rows[None], (device_count,) + gain_rows.shape)], axis=1
    )
    received = lax.all_to_all(sent, ("seq", "grp"), split_axis=0, concat_axis=0, tiled=True)
    received = feeder.tie(received)
    stream = to_ring(received[:, :own_rows].reshape(D, row_count)).T.astype(F32)
    gains = received[:, own_rows : own_rows + NG, :own_rows].transpose(0, 2, 1).reshape(D, NG)
    gains = to_ring(gains).T.astype(F32)[:, None, :]

    state = (stream, rms_norm(stream, gains[0]).astype(BF))
    later, router_later, table_later, normed_here = lax.optimization_barrier(
        (layer_weights[1], router_weights[1], embed_table, state[1])
    )
    state = (stream, normed_here)
    second_attention = exchanged(attention_columns(later.astype(BF), router_later.astype(BF)))
    second_forward = exchanged(forward_columns(later.astype(BF)))
    table_own = exchanged(table_columns(table_later.astype(BF)))
    gathers = [
        first_attention,
        first_forward,
        Gather(second_attention),
        Gather(second_forward),
        Gather(table_own),
    ]
    feeder.waiting.extend(gathers[2:])
    layer_pieces = [
        tuple(lambda gather=gather: Weights(gather.result()) for gather in gathers[start : start + 2])
        for start in (0, 2)
    ]
    saved_layers = []
    saved_pieces = []
    for layer_index in range(L):
        state, stored, pieces = forward_layer(
            state,
            *layer_pieces[layer_index],
            owners,
            gains[2 * layer_index + 1 : 2 * layer_index + 3],
            gate_all[layer_index],
            allowed,
            row_count,
            feeder,
        )
        saved_layers.append(stored)
        saved_pieces.append(pieces)

    stream, final_low = state
    final_gain = gains[2 * L]
    final_all = jnp.concatenate(spread_blocks(final_low, feeder), axis=0)
    table_part = jnp.concatenate(gathers[4].result(), axis=0)
    logits = times_plain(final_all, table_part)
    columns = jnp.arange(logits.shape[1], dtype=jnp.int32)[None, :]
    logits = jnp.where(columns < quarter, logits, -1e30)
    hit = columns == (targets.reshape(-1) - own_group * quarter)[:, None]
    hit = hit & (columns < quarter)
    log_part = jax.nn.logsumexp(logits, axis=-1).reshape(group_count, row_count)
    target_part = jnp.sum(jnp.where(hit, logits, 0.0), axis=1).reshape(group_count, row_count)
    stats = jnp.stack([log_part, target_part], axis=1)
    others = [stats]
    for offset in range(1, group_count):
        got = swap_group(stats, offset)
        others.append(jnp.stack([got[index ^ offset] for index in range(group_count)]))
    others = jnp.stack(others)
    log_total = jax.nn.logsumexp(others[:, :, 0], axis=0)
    target_logit = jnp.sum(others[:, :, 1], axis=0)
    loss_local = jnp.sum((log_total[0] - target_logit[0]) * doc_weight[0])
    scale = (doc_weight / doc_count).reshape(-1)[:, None]
    d_logits = (jnp.exp(logits - log_total.reshape(-1)[:, None]) - hit.astype(F32)) * scale
    d_logits = d_logits.astype(BF)
    d_final, d_logits = lax.optimization_barrier((times_transposed(d_logits, table_part), d_logits))
    d_final = merge_rows(d_final)
    table_grad = grad_whole([(final_all, d_logits)], ring_places())
    d_final, table_grad = lax.optimization_barrier((d_final, table_grad))
    table_grad = scatter_whole(table_grad)
    final_value, final_back = jax.vjp(rms_norm, stream, final_gain)
    d_stream, grad_final_gain = final_back(d_final)

    state = (d_stream, d_stream.astype(BF))
    feeder = Feed(width=2)
    layer_grads = [None] * L
    gain_parts = [None] * L
    for layer_index in reversed(range(L)):
        state, layer_grads[layer_index], gain_parts[layer_index] = backward_layer(
            state,
            *saved_pieces[layer_index],
            owners,
            gains[2 * layer_index : 2 * layer_index + 2],
            gate_all[layer_index],
            allowed,
            saved_layers[layer_index],
            row_count,
            feeder,
        )

    d_stream = from_ring(state[0].T)
    gain_grads = jnp.concatenate(sum(gain_parts, []) + [grad_final_gain])
    gain_grads = from_ring(gain_grads.T)
    gain_grads = gain_grads.reshape(device_count, own_rows, NG).transpose(0, 2, 1)
    gain_grads = jnp.pad(gain_grads, [(0, 0), (0, 16 - NG), (0, row_count - own_rows)])
    sent = jnp.concatenate([d_stream.reshape(device_count, own_rows, row_count), gain_grads], axis=1)
    received = lax.all_to_all(
        sent.astype(BF), ("seq", "grp"), split_axis=0, concat_axis=0, tiled=True
    ).astype(F32)
    embed_grad, square = spread_tokens(all_ids, received[:, :own_rows], own_columns(table_grad), V)
    gains_grad = jnp.sum(received[:, own_rows : own_rows + NG, :own_rows], axis=0).T
    square = square[0, 0] + jnp.sum(gains_grad * gains_grad)
    layer_parts = []
    for grads in layer_grads:
        summed = [member.result() if isinstance(member, Scatter) else member for member in grads]
        summed = [own_columns(member) for member in summed]
        square = square + sum(jnp.sum(jnp.square(member.astype(F32))) for member in summed)
        layer_parts.append(summed)
    sums = all_sum(jnp.stack([loss_local, square]))
    loss_sum = sums[0]
    grad_norm = jnp.sqrt(sums[1])
    factor = CLIP / jnp.maximum(grad_norm, CLIP)
    embed_out = adamw_update(
        embed_table, embed_grad, embed_mean, embed_square, factor, LR_MATRIX, DECAY
    )
    updated = update_layers(
        factor.reshape(1, 1),
        layer_parts,
        (layer_weights, router_weights),
        (layer_mean, router_mean),
        (layer_square, router_square),
    )
    layer_out, router_out = [(new[1], new[2], new[0]) for new in (updated[:3], updated[3:])]
    gains_out = adamw_update(norm_gains, gains_grad, gains_mean, gains_square, factor, LR_GAIN, 0.0)
    return (
        loss_sum,
        doc_count,
        grad_norm,
        embed_out[0],
        embed_out[1],
        embed_out[2],
        layer_out[0],
        layer_out[1],
        layer_out[2],
        router_out[0],
        router_out[1],
        router_out[2],
        gains_out[0],
        gains_out[1],
        gains_out[2],
    )


def solution(mesh):
    rows = P(("seq", "grp"), None)
    layers = P(None, ("seq", "grp"), None)
    return jax.shard_map(
        local,
        mesh=mesh,
        in_specs=(
            P("grp", "seq"),
            P("grp", "seq"),
            P(None, "seq"),
            P(None, "seq", None, None),
            rows,
            layers,
            layers,
            rows,
            rows,
            layers,
            layers,
            rows,
            rows,
            layers,
            layers,
            rows,
        ),
        out_specs=(P(), P(), P()) + (rows,) * 3 + (layers,) * 6 + (rows,) * 3,
        check_vma=False,
    )
```

```python
import jax
import jax.numpy as jnp
from jax import lax
from jax.experimental import pallas as pl
from jax.experimental.pallas import tpu as pltpu
from jax.sharding import PartitionSpec as P

D = 1024
H = 4
DH = 112
E = 5
FF = 4096
V = 8000
L = 2
STEP = 10
QKW = 896
VW = 2240
SELW = 40
LANE = 128
NG = 5

EPS_NORM = 1e-05
CLIP = 0.05
LR_MATRIX = 0.06
LR_GAIN = 0.3
BETA_FIRST = 0.9
BETA_SECOND = 0.999
EPS_ADAM = 1e-08
DECAY = 0.1

QKV_COLS = (2 + E) * LANE
OUT_COLS = E * LANE
ATT_COLS = QKV_COLS + OUT_COLS
BF = jnp.bfloat16
F32 = jnp.float32


def times_plain(left_side, right_side):
    return jnp.dot(left_side, right_side, preferred_element_type=F32)


def times_transposed(left_side, right_side):
    return lax.dot_general(
        left_side, right_side, (((1,), (1,)), ((), ())), preferred_element_type=F32
    )


def transposed_times(left_side, right_side):
    return lax.dot_general(
        left_side, right_side, (((0,), (0,)), ((), ())), preferred_element_type=F32
    )


def rms_norm(values, gain_row):
    return (
        values * lax.rsqrt(jnp.mean(values * values, axis=-1, keepdims=True) + EPS_NORM) * gain_row
    )


def gelu_exact(values):
    return jax.nn.gelu(values, approximate=False)


def swap_group(values, bit):
    count = lax.axis_size("grp")
    return lax.ppermute(values, "grp", [(member, member ^ bit) for member in range(count)])


def group_bits():
    count = lax.axis_size("grp")
    return [1 << power for power in range(count.bit_length() - 1)]


def spread_rows(values):
    blocks = {0: values}
    for bit in reversed(group_bits()):
        for known in list(blocks):
            blocks[known ^ bit] = swap_group(blocks[known], bit)
    return jnp.concatenate([blocks[index] for index in range(len(blocks))], axis=0)


def merge_rows(values):
    count = lax.axis_size("grp")
    rows = values.shape[0] // count
    blocks = {index: values[index * rows : (index + 1) * rows] for index in range(count)}
    for bit in group_bits():
        away = [index for index in sorted(blocks) if index & bit]
        sent = jnp.concatenate([blocks[index].astype(BF) for index in away], axis=0)
        received = swap_group(sent, bit).astype(F32)
        blocks = {
            index ^ bit: blocks[index ^ bit] + received[place * rows : (place + 1) * rows]
            for place, index in enumerate(away)
        }
    return blocks[0]


def exchange_parts(parts):
    own = lax.axis_index("grp")
    parts = [parts[0]] + [swap_group(part, offset) for offset, part in enumerate(parts) if offset]
    return jnp.stack([lax.select_n(own ^ member, *parts) for member in range(len(parts))])


def group_exchange(values):
    count = lax.axis_size("grp")
    own = lax.axis_index("grp")
    cases = [values[member] for member in range(count)]
    parts = [lax.select_n(own ^ offset, *cases) for offset in range(count)]
    parts = [parts[0]] + [swap_group(parts[offset], offset) for offset in range(1, count)]
    return jnp.stack([lax.select_n(own ^ member, *parts) for member in range(count)])


def shifted(value, steps):
    count = lax.axis_size("seq")
    first, last = (max(0, -steps), min(count, count - steps))
    return lax.ppermute(value, "seq", [(source, source + steps) for source in range(first, last)])


RING_LIMIT = 8


def ring_order(count):
    return list(range(0, count, 2)) + list(range(count - 1, 0, -2))


def ring_pairs(count, step):
    order = ring_order(count)
    return [(order[place], order[(place + step) % count]) for place in range(count)]


def ring_place(device, count):
    return jnp.where(device % 2 == 0, device // 2, count - 1 - device // 2)


def ring_device(place, count):
    return jnp.where(2 * place < count, 2 * place, 2 * (count - 1 - place) + 1)


class Gather:
    def __init__(self, values, ring=True):
        self.count = lax.axis_size("seq")
        self.whole = None
        self.blocks = {0: values}
        self.left = self.count // 2
        if self.count > RING_LIMIT or not ring:
            self.whole = lax.all_gather(values, "seq", axis=0, tiled=True)
            self.left = 0
        self.flying = (values, values)

    def land(self):
        return self.flying

    def step(self, landed):
        ahead, behind = landed
        done = self.count // 2 - self.left + 1
        ahead = lax.ppermute(ahead, "seq", ring_pairs(self.count, 1))
        self.blocks[self.count - done] = ahead
        if done < self.count - self.count // 2:
            behind = lax.ppermute(behind, "seq", ring_pairs(self.count, -1))
            self.blocks[done] = behind
        self.flying = (ahead, behind)
        self.left -= 1

    def result(self):
        while self.left:
            self.step(self.flying)
        if self.whole is not None:
            return [self.whole]
        return [self.blocks[place] for place in range(len(self.blocks))]


class Scatter:
    def __init__(self, *parts):
        self.count = lax.axis_size("seq")
        self.parts, self.rows = parts, D // self.count
        self.left = self.count // 2
        self.whole = None
        if self.count > RING_LIMIT:
            joined = jnp.concatenate(self.parts, axis=1)
            self.whole = lax.psum_scatter(joined, "seq", scatter_dimension=0, tiled=True)
            self.left = 0
        self.flying = ()

    def land(self):
        return self.flying

    def step(self, landed):
        back = self.count - 1 - self.count // 2
        done = self.count // 2 - self.left
        places, received = [self.left], [landed[:1]]
        if done < back:
            places.append(self.count - back + done)
            received.append(landed[1:])
        sums = add_blocks(self.parts, places, received, self.rows)
        ahead = lax.ppermute(sums[0], "seq", ring_pairs(self.count, 1))
        behind = landed[1] if done >= back else lax.ppermute(
            sums[1], "seq", ring_pairs(self.count, -1)
        )
        self.flying = (ahead, behind)
        self.left -= 1

    def result(self):
        while self.left:
            self.step(self.flying)
        if self.whole is not None:
            return self.whole
        return add_blocks(self.parts, [0], [self.flying], self.rows)[0]


class Feed:
    def __init__(self, tasks=(), width=1):
        self.waiting = list(tasks)
        self.width = width
        self.flying = []

    def tie(self, values, width=1):
        landed = [task.land() for task in self.flying]
        values, landed = lax.optimization_barrier((values, landed))
        for task, arrived in zip(self.flying, landed):
            task.flying = tuple(arrived)
        self.start(width)
        return values

    def start(self, width=1):
        self.waiting = [task for task in self.waiting if task.left]
        self.flying = self.waiting[:width]
        for task in self.flying:
            task.step(task.flying)


def ring_owners():
    count = lax.axis_size("seq")
    if count > RING_LIMIT:
        return jnp.zeros((1,), jnp.int32)
    here = ring_place(lax.axis_index("seq"), count)
    return ring_device(lax.rem(jnp.arange(count, dtype=jnp.int32) + here, count), count)


def ring_places():
    count = lax.axis_size("seq")
    if count > RING_LIMIT:
        return jnp.zeros((1,), jnp.int32)
    here = ring_place(lax.axis_index("seq"), count)
    devices = jnp.arange(count, dtype=jnp.int32)
    return lax.rem(ring_place(devices, count) - here + count, count)


def pick_blocks(values, order):
    if order.shape[0] == 1:
        return values
    shape = values.shape
    return jnp.take(values.reshape((order.shape[0], -1) + shape[1:]), order, axis=0).reshape(shape)


def to_ring(values):
    return pick_blocks(values, ring_owners())


def from_ring(values):
    return pick_blocks(values, ring_places())


def after(values, *others):
    return lax.optimization_barrier((values, *others))[0]


def pad_lanes(values):
    return jnp.pad(values, [(0, 0)] * (values.ndim - 1) + [(0, LANE - values.shape[-1])])


def choose(own, offset, cases):
    member = own ^ offset
    value = cases[0]
    for index in range(1, len(cases)):
        value = jnp.where(member == index, cases[index], value)
    return value


def arrange_layer(own, layer, weights, routers):
    rows, columns = weights.shape[1:]
    members = H

    def body(own_ref, weight_ref, router_ref, *outs):
        here = own_ref[0]

        def lanes(pieces):
            filled = sum(piece.shape[1] for piece in pieces)
            zeros = [jnp.zeros((rows, LANE - filled), F32)]
            return jnp.concatenate(pieces + zeros, axis=1).astype(BF)

        def chunk(start):
            return weight_ref[0, :, start : start + DH]

        tiles = []
        for member in range(members):
            picked = [
                router_ref[0, :, (kind * H + member) * E : (kind * H + member + 1) * E]
                for kind in range(2)
            ]
            group = [lanes([chunk(member * DH)] + picked), lanes([chunk((H + member) * DH)])]
            for base in (QKW, QKW + VW):
                for expert in range(E):
                    group.append(lanes([chunk(base + (member * E + expert) * DH)]))
            tiles.append(group)
        base = QKW + 2 * VW
        width = FF // members
        for offset in range(members):
            for index in range(len(tiles[0])):
                outs[offset][:, index * LANE : (index + 1) * LANE] = choose(
                    here, offset, [group[index] for group in tiles]
                )
            for side in range(2):
                start = base + side * FF
                outs[members + offset][:, side * width : (side + 1) * width] = choose(
                    here,
                    offset,
                    [
                        weight_ref[0, :, start + member * width : start + (member + 1) * width]
                        for member in range(members)
                    ],
                ).astype(BF)

    shapes = [(rows, ATT_COLS)] * members + [(rows, 2 * FF // members)] * members
    parts = pl.pallas_call(
        body,
        grid=(1,),
        in_specs=[
            in_scalars(),
            pl.BlockSpec((1, rows, columns), lambda step: (layer, 0, 0)),
            pl.BlockSpec((1, rows, SELW), lambda step: (layer, 0, 0)),
        ],
        out_specs=[part(shape) for shape in shapes],
        out_shape=[jax.ShapeDtypeStruct(shape, BF) for shape in shapes],
        compiler_params=pltpu.CompilerParams(vmem_limit_bytes=VMEM_LIMIT),
        cost_estimate=pl.CostEstimate(flops=1, bytes_accessed=1, transcendentals=0),
        name="arrange_layer",
    )(own, weights, routers)
    return parts[:members], parts[members:]


def arrange_table(own, table):
    rows, width = table.shape
    quarter = width // H
    padded = -(-quarter // LANE) * LANE

    def body(own_ref, table_ref, *outs):
        zeros = jnp.zeros((rows, padded - quarter), F32)
        cases = [
            jnp.concatenate([table_ref[:, member * quarter : (member + 1) * quarter], zeros], axis=1)
            for member in range(H)
        ]
        for offset in range(H):
            outs[offset][...] = choose(own_ref[0], offset, cases).astype(BF)

    return call(
        body,
        "arrange_table",
        (own, table),
        [in_scalars(), whole(table)],
        [((rows, padded), BF) for _ in range(H)],
        [],
    )


def lookup_body(ids_ref, table_ref, out_ref, by_token, picked):
    rows = table_ref.shape[0]
    width = table_ref.shape[1]
    for start in range(0, width, LANE):
        end = min(start + LANE, width)
        by_token[start:end, :rows] = table_ref[:, start:end].T

    @pl.loop(0, out_ref.shape[0])
    def _(device):
        base = device * LANE

        for token in range(LANE):
            picked[pl.ds(token, 1), :] = by_token[pl.ds(ids_ref[base + token], 1), :]
        out_ref[device] = picked[...].T[:rows]


def lookup(ids, table):
    rows, width = table.shape
    devices = ids.shape[0] // LANE
    return pl.pallas_call(
        lookup_body,
        grid_spec=pltpu.PrefetchScalarGridSpec(
            num_scalar_prefetch=1,
            grid=(1,),
            in_specs=[pl.BlockSpec((rows, width), lambda i, ids: (0, 0))],
            out_specs=pl.BlockSpec((devices, rows, LANE), lambda i, ids: (0, 0, 0)),
            scratch_shapes=[pltpu.VMEM((width, LANE), F32), pltpu.VMEM((LANE, LANE), F32)],
        ),
        out_shape=jax.ShapeDtypeStruct((devices, rows, LANE), F32),
        compiler_params=pltpu.CompilerParams(vmem_limit_bytes=48 * 1024 * 1024),
        name="lookup",
    )(ids, table)


ACCUMULATORS = 4


def spread_body(ids_ref, grad_ref, table_ref, out_ref, square_ref, *scratch):
    rows, width = out_ref.shape
    members = table_ref.shape[0]
    totals, picked = scratch[:-1], scratch[-1]
    for total in totals:
        total[...] = jnp.zeros_like(total)

    @pl.loop(0, grad_ref.shape[0])
    def _(device):
        base = device * LANE
        picked[:, :rows] = grad_ref[device].T

        for step in range(LANE // ACCUMULATORS):
            for which, total in enumerate(totals):
                token = step * ACCUMULATORS + which
                place = pl.ds(ids_ref[base + token], 1)
                total[place, :] += picked[pl.ds(token, 1), :]

    for start in range(0, width, LANE):
        end = min(start + LANE, width)
        found = sum(total[start:end, :] for total in totals).T[:rows]
        out_ref[:, start:end] = found * D**0.5
    quarter = width // members
    table = jnp.concatenate([table_ref[member][:, :quarter] for member in range(members)], axis=1)
    total = out_ref[...] + table.astype(F32)
    out_ref[...] = total
    square_ref[0, 0] = jnp.sum(total * total)


def spread_tokens(ids, grads, table_parts, width):
    devices, rows, _ = grads.shape
    return pl.pallas_call(
        spread_body,
        grid_spec=pltpu.PrefetchScalarGridSpec(
            num_scalar_prefetch=1,
            grid=(1,),
            in_specs=[
                pl.BlockSpec((devices, rows, LANE), lambda i, ids: (0, 0, 0)),
                pl.BlockSpec(table_parts.shape, lambda i, ids: (0, 0, 0)),
            ],
            out_specs=[
                pl.BlockSpec((rows, width), lambda i, ids: (0, 0)),
                pl.BlockSpec(memory_space=pltpu.SMEM),
            ],
            scratch_shapes=[pltpu.VMEM((width, LANE), F32) for _ in range(ACCUMULATORS)]
            + [pltpu.VMEM((LANE, LANE), F32)],
        ),
        out_shape=[
            jax.ShapeDtypeStruct((rows, width), F32),
            jax.ShapeDtypeStruct((1, 1), F32),
        ],
        compiler_params=pltpu.CompilerParams(vmem_limit_bytes=48 * 1024 * 1024),
        name="spread",
    )(ids, grads, table_parts)


VMEM_LIMIT = 56 * 1024 * 1024
SCALE = DH ** (-0.5)


def whole(array):
    return pl.BlockSpec(array.shape, lambda step: (0,) * array.ndim)


def part(shape):
    return pl.BlockSpec(shape, lambda step: (0,) * len(shape))


def in_scalars():
    return pl.BlockSpec(memory_space=pltpu.SMEM)


def anywhere():
    return pl.BlockSpec(memory_space=pl.ANY)


def call(body, name, inputs, specs, outputs, scratch, ties=()):
    ties = tuple(ties)

    def wrapped(*refs):
        count = len(inputs)
        body(*refs[:count], *refs[count + len(ties) :])

    return pl.pallas_call(
        wrapped,
        grid=(1,),
        in_specs=list(specs) + [anywhere()] * len(ties),
        out_specs=[part(shape) for shape, _ in outputs],
        out_shape=[jax.ShapeDtypeStruct(shape, kind) for shape, kind in outputs],
        scratch_shapes=scratch,
        compiler_params=pltpu.CompilerParams(vmem_limit_bytes=VMEM_LIMIT),
        cost_estimate=pl.CostEstimate(flops=1, bytes_accessed=1, transcendentals=0),
        name=name,
    )(*inputs, *ties)


class Weights:
    def __init__(self, arrays, base=0):
        self.arrays, self.base = list(arrays), base
        self.natural = len(self.arrays) == 1
        self.count = ring_owners().shape[0] if self.natural else len(self.arrays)

    def specs(self):
        return [anywhere() for _ in self.arrays]

    def copies(self, owners, refs, start, width, target, semaphores):
        copies = []
        rows = D // self.count
        columns = pl.ds(self.base + start, width)
        for index in range(self.count):
            if not self.natural:
                source = refs[index].at[:, columns]
            elif self.count == 1:
                source = refs[0].at[:, columns]
            else:
                place = pl.multiple_of(owners[index] * rows, rows)
                source = refs[0].at[pl.ds(place, rows), columns]
            copy = pltpu.make_async_copy(
                source, target.at[pl.ds(index * rows, rows)], semaphores.at[index]
            )
            copy.start()
            copies.append(copy)
        return copies


def gate_column(gates, kind, expert):
    place = DH + kind * E + expert
    return gates[:, place : place + 1]


def expert_lanes(values, expert):
    return values[:, expert * LANE : (expert + 1) * LANE]


def dot_nn(left, right):
    return lax.dot_general(left, right, (((1,), (0,)), ((), ())), preferred_element_type=F32)


def dot_nt(left, right):
    return lax.dot_general(left, right, (((1,), (1,)), ((), ())), preferred_element_type=F32)


def dot_tn(left, right):
    return lax.dot_general(left, right, (((0,), (0,)), ((), ())), preferred_element_type=F32)


def store_split(keep, send, pair, values, rows):
    keep[pl.ds(pair * rows, rows), :] = values[:rows]
    send[pl.ds(pair * rows, rows), :] = values[rows:].astype(BF)


def project(blocks, weights, owners, mask, ties=()):
    chains, rows = len(blocks), blocks[0].shape[0]
    total = chains * rows
    arrays = len(weights.arrays)

    def body(owner_ref, *refs):
        xs, ws, mask_ref = refs[:chains], refs[chains : chains + arrays], refs[chains + arrays]
        normed, queries, key_value, value_all, squashed, weight, semaphores = refs[
            chains + arrays + 1 :
        ]
        copies = weights.copies(owner_ref, ws, 0, QKV_COLS, weight, semaphores)
        for chain in range(chains):
            normed[chain * rows : (chain + 1) * rows, :] = xs[chain][...]
        for copy in copies:
            copy.wait()

        @pl.loop(0, chains // 2)
        def _(pair):
            at = pl.ds(pair * 2 * rows, 2 * rows)
            projected = dot_nn(normed[at, :], weight[...])
            first = projected[:, :LANE]
            lanes = lax.broadcasted_iota(jnp.int32, first.shape, 1)
            queries[at, :] = jnp.where(lanes < DH, first, 0.0).astype(BF)
            soft = jax.nn.sigmoid(first)
            squashed[at, :] = soft
            gates = soft * mask_ref[at, :]
            values = projected[:, 2 * LANE :]
            value_all[at, :] = values
            mixed = sum(
                gate_column(gates, 0, expert) * expert_lanes(values, expert) for expert in range(E)
            )
            key_value[at, :LANE] = projected[:, LANE : 2 * LANE].astype(BF)
            key_value[at, LANE:] = mixed.astype(BF)

    return call(
        body,
        "project",
        (owners, *blocks, *weights.arrays, mask),
        [in_scalars()] + [whole(block) for block in blocks] + weights.specs() + [whole(mask)],
        [
            ((total, D), BF),
            ((total, LANE), BF),
            ((total, 2 * LANE), BF),
            ((total, E * LANE), F32),
            ((total, LANE), F32),
        ],
        [pltpu.VMEM((D, QKV_COLS), BF), pltpu.SemaphoreType.DMA((weights.count,))],
        ties,
    )


def probabilities(queries, keys, allowed):
    scores = jnp.where(allowed > 0, dot_nt(queries, keys) * SCALE, -1e30)
    raised = jnp.exp(scores - jnp.max(scores, axis=1, keepdims=True))
    return raised / jnp.sum(raised, axis=1, keepdims=True)


def attend(queries, key_value, memory, squashed, mask, allowed, weights, owners, rows, ties=()):
    total = queries.shape[0]
    chains = total // rows

    def body(owner_ref, q_ref, own_ref, past_ref, squash_ref, mask_ref, allow_ref, *refs):
        ws = refs[: len(weights.arrays)]
        attended, mixed, keep, send, weight, semaphores = refs[len(weights.arrays) :]
        copies = weights.copies(owner_ref, ws, QKV_COLS, OUT_COLS, weight, semaphores)
        for chain in range(chains):
            at = slice(chain * rows, (chain + 1) * rows)
            keys = jnp.concatenate([past_ref[at, :LANE], own_ref[at, :LANE]], axis=0)
            values = jnp.concatenate([past_ref[at, LANE:], own_ref[at, LANE:]], axis=0)
            soft = probabilities(q_ref[at, :], keys, allow_ref[at, :])
            got = dot_nn(soft.astype(BF), values)
            attended[at, :] = got
            gates = squash_ref[at, :] * mask_ref[at, :]
            for expert in range(E):
                mixed[at, expert * LANE : (expert + 1) * LANE] = (
                    gate_column(gates, 1, expert) * got
                ).astype(BF)
        for copy in copies:
            copy.wait()

        @pl.loop(0, chains // 2)
        def _(pair):
            out = dot_nt(mixed[pl.ds(pair * 2 * rows, 2 * rows), :], weight[...])
            store_split(keep, send, pair, out, rows)

    return call(
        body,
        "attend",
        (owners, queries, key_value, memory, squashed, mask, allowed, *weights.arrays),
        [in_scalars()]
        + [whole(array) for array in (queries, key_value, memory, squashed, mask, allowed)]
        + weights.specs(),
        [
            ((total, LANE), F32),
            ((total, E * LANE), BF),
            ((total // 2, D), F32),
            ((total // 2, D), BF),
        ],
        [pltpu.VMEM((D, OUT_COLS), BF), pltpu.SemaphoreType.DMA((weights.count,))],
        ties,
    )


def feed(blocks, weights, owners, ties=()):
    chains, rows = len(blocks), blocks[0].shape[0]
    total = chains * rows
    width = FF // H
    count, arrays = weights.count, len(weights.arrays)

    def body(owner_ref, *refs):
        xs, ws = refs[:chains], refs[chains : chains + arrays]
        second, hidden, slope, keep, send, up, down, up_sems, down_sems = refs[
            chains + arrays :
        ]
        up_copies = weights.copies(owner_ref, ws, 0, width, up, up_sems)
        down_copies = weights.copies(owner_ref, ws, width, width, down, down_sems)
        for chain in range(chains):
            second[chain * rows : (chain + 1) * rows, :] = xs[chain][...]
        for copy in up_copies:
            copy.wait()

        @pl.loop(0, chains // 2)
        def _(pair):
            at = pl.ds(pair * 2 * rows, 2 * rows)
            pre = dot_nn(second[at, :], up[...])
            rising = 0.5 * (1.0 + lax.erf(pre * 0.5**0.5))
            hidden[at, :] = (pre * rising).astype(BF)
            slope[at, :] = rising + pre * jnp.exp(-0.5 * pre * pre) * 0.3989422804014327

        for copy in down_copies:
            copy.wait()

        @pl.loop(0, chains // 2)
        def _(pair):
            out = dot_nt(hidden[pl.ds(pair * 2 * rows, 2 * rows), :], down[...])
            store_split(keep, send, pair, out, rows)

    return call(
        body,
        "feed",
        (owners, *blocks, *weights.arrays),
        [in_scalars()] + [whole(block) for block in blocks] + weights.specs(),
        [
            ((total, D), BF),
            ((total, width), BF),
            ((total, width), F32),
            ((total // 2, D), F32),
            ((total // 2, D), BF),
        ],
        [pltpu.VMEM((D, width), BF)] * 2 + [pltpu.SemaphoreType.DMA((count,))] * 2,
        ties,
    )


def feed_back(blocks, weights, owners, slope, ties=()):
    chains, rows = len(blocks), blocks[0].shape[0]
    total = chains * rows
    width = FF // H
    count, arrays = weights.count, len(weights.arrays)

    def body(owner_ref, *refs):
        ds, ws = refs[:chains], refs[chains : chains + arrays]
        slope_ref, d_out, d_pre, keep, send, up, down, up_sems, down_sems = refs[
            chains + arrays :
        ]
        down_copies = weights.copies(owner_ref, ws, width, width, down, down_sems)
        up_copies = weights.copies(owner_ref, ws, 0, width, up, up_sems)
        for chain in range(chains):
            d_out[chain * rows : (chain + 1) * rows, :] = ds[chain][...]
        for copy in down_copies:
            copy.wait()

        @pl.loop(0, chains // 2)
        def _(pair):
            at = pl.ds(pair * 2 * rows, 2 * rows)
            d_pre[at, :] = (dot_nn(d_out[at, :], down[...]) * slope_ref[at, :]).astype(BF)

        for copy in up_copies:
            copy.wait()

        @pl.loop(0, chains // 2)
        def _(pair):
            out = dot_nt(d_pre[pl.ds(pair * 2 * rows, 2 * rows), :], up[...])
            store_split(keep, send, pair, out, rows)

    return call(
        body,
        "feed_back",
        (owners, *blocks, *weights.arrays, slope),
        [in_scalars()] + [whole(block) for block in blocks] + weights.specs() + [whole(slope)],
        [
            ((total, D), BF),
            ((total, width), BF),
            ((total // 2, D), F32),
            ((total // 2, D), BF),
        ],
        [pltpu.VMEM((D, width), BF)] * 2 + [pltpu.SemaphoreType.DMA((count,))] * 2,
        ties,
    )


def attend_back(
    blocks, queries, key_value, memory, squashed, mask, allowed, attended, weights, owners, ties=()
):
    chains, rows = len(blocks), blocks[0].shape[0]
    total = chains * rows
    count = len(weights.arrays)

    def body(owner_ref, *refs):
        ds, refs = refs[:chains], refs[chains:]
        q_ref, own_ref, past_ref, squash_ref, mask_ref, allow_ref, att_ref = refs[:7]
        ws, refs = refs[7 : 7 + count], refs[7 + count :]
        d_branch, d_query, d_gate, d_own, d_past, weight, semaphores = refs
        copies = weights.copies(owner_ref, ws, QKV_COLS, OUT_COLS, weight, semaphores)
        for chain in range(chains):
            d_branch[chain * rows : (chain + 1) * rows, :] = ds[chain][...]
        for copy in copies:
            copy.wait()
        for pair in range(chains // 2):
            pair_mixed = dot_nn(
                d_branch[pair * 2 * rows : (pair + 1) * 2 * rows, :], weight[...]
            ).astype(BF)
            for side in range(2):
                chain = pair * 2 + side
                at = slice(chain * rows, (chain + 1) * rows)
                d_mixed = pair_mixed[side * rows : (side + 1) * rows].astype(F32)
                gates = squash_ref[at, :] * mask_ref[at, :]
                d_att = sum(
                    gate_column(gates, 1, expert) * expert_lanes(d_mixed, expert)
                    for expert in range(E)
                ).astype(BF)
                got = att_ref[at, :]
                lanes = lax.broadcasted_iota(jnp.int32, (rows, LANE), 1)
                d_gates = jnp.zeros((rows, LANE), F32)
                for expert in range(E):
                    column = jnp.sum(expert_lanes(d_mixed, expert) * got, axis=1, keepdims=True)
                    d_gates = jnp.where(lanes == DH + E + expert, column, d_gates)
                d_gate[at, :] = d_gates
                keys = jnp.concatenate([past_ref[at, :LANE], own_ref[at, :LANE]], axis=0)
                values = jnp.concatenate([past_ref[at, LANE:], own_ref[at, LANE:]], axis=0)
                query = q_ref[at, :]
                soft = probabilities(query, keys, allow_ref[at, :])
                d_soft = dot_nt(d_att, values)
                delta = jnp.sum(soft * d_soft, axis=1, keepdims=True)
                d_scores = (soft * (d_soft - delta)).astype(BF)
                d_query[at, :] = dot_nn(d_scores, keys) * SCALE
                d_keys = dot_tn(d_scores, query) * SCALE
                d_values = dot_tn(soft.astype(BF), d_att)
                d_past[at, :LANE] = d_keys[:rows].astype(BF)
                d_past[at, LANE:] = d_values[:rows].astype(BF)
                d_own[at, :LANE] = d_keys[rows:]
                d_own[at, LANE:] = d_values[rows:]

    arrays = (queries, key_value, memory, squashed, mask, allowed, attended)
    return call(
        body,
        "attend_back",
        (owners, *blocks, *arrays, *weights.arrays),
        [in_scalars()]
        + [whole(block) for block in blocks]
        + [whole(array) for array in arrays]
        + weights.specs(),
        [
            ((total, D), BF),
            ((total, LANE), F32),
            ((total, LANE), F32),
            ((total, 2 * LANE), F32),
            ((total, 2 * LANE), BF),
        ],
        [pltpu.VMEM((D, OUT_COLS), BF), pltpu.SemaphoreType.DMA((weights.count,))],
        ties,
    )


def project_back(
    d_query, d_gate, d_own, returned, squashed, mask, value_all, weights, owners, rows, ties=()
):
    total = d_query.shape[0]
    chains = total // rows

    def body(owner_ref, dq_ref, dg_ref, own_ref, back_ref, squash_ref, mask_ref, value_ref, *refs):
        ws = refs[: len(weights.arrays)]
        d_projected, keep, send, weight, semaphores = refs[len(weights.arrays) :]
        copies = weights.copies(owner_ref, ws, 0, QKV_COLS, weight, semaphores)
        for chain in range(chains):
            at = slice(chain * rows, (chain + 1) * rows)
            d_own = own_ref[at, :] + back_ref[at, :].astype(F32)
            soft = squash_ref[at, :]
            gates = soft * mask_ref[at, :]
            d_value = d_own[:, LANE:].astype(BF).astype(F32)
            lanes = lax.broadcasted_iota(jnp.int32, (rows, LANE), 1)
            d_gates = dg_ref[at, :]
            for expert in range(E):
                column = jnp.sum(
                    d_value * value_ref[at, expert * LANE : (expert + 1) * LANE],
                    axis=1,
                    keepdims=True,
                )
                d_gates = jnp.where(lanes == DH + expert, column, d_gates)
                start = (2 + expert) * LANE
                d_projected[at, start : start + LANE] = (
                    gate_column(gates, 0, expert) * d_value
                ).astype(BF)
            d_select = d_gates * mask_ref[at, :] * soft * (1.0 - soft)
            first = jnp.where(lanes < DH, dq_ref[at, :], d_select)
            d_projected[at, :LANE] = first.astype(BF)
            d_projected[at, LANE : 2 * LANE] = d_own[:, :LANE].astype(BF)
        for copy in copies:
            copy.wait()

        @pl.loop(0, chains // 2)
        def _(pair):
            out = dot_nt(d_projected[pl.ds(pair * 2 * rows, 2 * rows), :], weight[...])
            store_split(keep, send, pair, out, rows)

    arrays = (d_query, d_gate, d_own, returned, squashed, mask, value_all)
    return call(
        body,
        "project_back",
        (owners, *arrays, *weights.arrays),
        [in_scalars()] + [whole(array) for array in arrays] + weights.specs(),
        [((total, QKV_COLS), BF), ((total // 2, D), F32), ((total // 2, D), BF)],
        [pltpu.VMEM((D, QKV_COLS), BF), pltpu.SemaphoreType.DMA((weights.count,))],
        ties,
    )


def join_norm(stream, sums, gain, ties=()):
    rows = stream.shape[0]

    def body(stream_ref, keep_ref, near_ref, far_ref, gain_ref, joined, normed):
        values = (
            stream_ref[...]
            + keep_ref[...]
            + near_ref[...].astype(F32)
            + far_ref[...].astype(F32)
        )
        joined[...] = values
        scale = lax.rsqrt(jnp.mean(values * values, axis=1, keepdims=True) + EPS_NORM)
        normed[...] = (values * scale * gain_ref[...]).astype(BF)

    block = part((rows, D))
    return call(
        body,
        "join_norm",
        (stream, *sums, gain),
        [block, block, block, block, part((1, D))],
        [((rows, D), F32), ((rows, D), BF)],
        [],
        ties,
    )


def norm_back(grad_out, sums, stream, gain, ties=()):
    rows = stream.shape[0]

    def body(out_ref, keep_ref, near_ref, far_ref, stream_ref, gain_ref, grad, low, gain_grad):
        d_norm = keep_ref[...] + near_ref[...].astype(F32) + far_ref[...].astype(F32)
        values = stream_ref[...]
        scale = lax.rsqrt(jnp.mean(values * values, axis=1, keepdims=True) + EPS_NORM)
        unit = values * scale
        gain_grad[...] = jnp.sum(d_norm * unit, axis=0, keepdims=True)
        d_unit = d_norm * gain_ref[...]
        inner = jnp.mean(d_unit * unit, axis=1, keepdims=True)
        total = out_ref[...] + scale * (d_unit - unit * inner)
        grad[...] = total
        low[...] = total.astype(BF)

    block = part((rows, D))
    return call(
        body,
        "norm_back",
        (grad_out, *sums, stream, gain),
        [block] * 5 + [part((1, D))],
        [((rows, D), F32), ((rows, D), BF), ((1, D), F32)],
        [],
        ties,
    )


def grad_whole(pairs, places):
    total = pairs[0][0].shape[0]
    rows = D // places.shape[0]
    together = 2 if places.shape[0] > 1 else 1
    widths = [d_part.shape[1] for _, d_part in pairs]

    def body(place_ref, *refs):
        count = len(pairs) * together
        start = 0
        for index, width in enumerate(widths):
            lefts = refs[index * together : (index + 1) * together]
            part_ref = refs[count + index]
            turned = jnp.concatenate([left[...].T for left in lefts], axis=0)
            for first in range(0, width, 512):
                size = min(512, width - first)
                value = dot_nn(turned, part_ref[:, first : first + size])
                refs[-1][:, start + first : start + first + size] = value.astype(BF)
            start += width

    left_specs = [
        pl.BlockSpec((total, rows), lambda step, at, side=side: (0, at[together * step + side]))
        for side in range(together)
    ]
    return pl.pallas_call(
        body,
        grid_spec=pltpu.PrefetchScalarGridSpec(
            num_scalar_prefetch=1,
            grid=(places.shape[0] // together,),
            in_specs=left_specs * len(pairs)
            + [pl.BlockSpec((total, width), lambda step, at: (0, 0)) for width in widths],
            out_specs=pl.BlockSpec((together * rows, sum(widths)), lambda step, at: (step, 0)),
        ),
        out_shape=jax.ShapeDtypeStruct((D, sum(widths)), BF),
        compiler_params=pltpu.CompilerParams(vmem_limit_bytes=VMEM_LIMIT),
        cost_estimate=pl.CostEstimate(flops=1, bytes_accessed=1, transcendentals=0),
        name="grad_whole",
    )(
        places,
        *[left for left, _ in pairs for _ in range(together)],
        *[d_part for _, d_part in pairs],
    )


def add_blocks(parts, places, received, rows):
    widths = [array.shape[1] for array in parts]
    flat = [array for arrays in received for array in arrays]

    def body(*refs):
        count = len(places)
        part_refs = [refs[side * count : (side + 1) * count] for side in range(len(parts))]
        arrived = list(refs[len(parts) * count : len(parts) * count + len(flat)])
        outs = refs[len(parts) * count + len(flat) :]
        for index in range(count):
            mine = [arrived.pop(0) for _ in received[index]]
            start = 0
            for side, width in zip(part_refs, widths):
                at = slice(start, start + width)
                value = side[index][...].astype(F32)
                for ref in mine:
                    value = value + ref[:, at].astype(F32)
                outs[index][:, at] = value.astype(BF)
                start += width

    def row_blocks(width):
        return [
            pl.BlockSpec((rows, width), lambda step, place=place: (place, 0)) for place in places
        ]

    return call(
        body,
        "add_blocks",
        (*[array for array in parts for _ in places], *flat),
        [spec for width in widths for spec in row_blocks(width)] + [whole(array) for array in flat],
        [((rows, sum(widths)), BF) for _ in places],
        [],
    )


def stream_of_rows(received, owners, own_rows):
    tokens = received.shape[2]
    per_block = D // owners.shape[0] // own_rows

    def body(owner_ref, received_ref, stream, normed, gains):
        for block in range(owners.shape[0]):
            sources = [owner_ref[block] * per_block + member for member in range(per_block)]
            at = slice(block * LANE, (block + 1) * LANE)
            rows = [received_ref[source, :own_rows, :].astype(F32) for source in sources]
            stream[:, at] = jnp.concatenate(rows, axis=0).T
            pieces = [received_ref[source, own_rows:, :].astype(F32) for source in sources]
            gains[:, at] = jnp.concatenate([piece[:, :own_rows] for piece in pieces], axis=1)[:8]
        values = stream[...]
        scale = lax.rsqrt(jnp.mean(values * values, axis=1, keepdims=True) + EPS_NORM)
        normed[...] = (values * scale * gains[0:1, :]).astype(BF)

    return call(
        body,
        "stream_of_rows",
        (owners, received),
        [in_scalars(), whole(received)],
        [((tokens, D), F32), ((tokens, D), BF), ((8, D), F32)],
        [],
    )


def rows_of_stream(d_stream, gain_grads, owners, own_rows):
    tokens = d_stream.shape[0]
    per_block = D // owners.shape[0] // own_rows

    def body(owner_ref, stream_ref, *refs):
        gain_refs, out = refs[:NG], refs[NG]
        for block in range(owners.shape[0]):
            at = slice(block * LANE, (block + 1) * LANE)
            turned = stream_ref[:, at].T.astype(BF)
            gains = jnp.concatenate(
                [ref[:, at] for ref in gain_refs] + [jnp.zeros((16 - NG, LANE), F32)], axis=0
            ).astype(BF)
            for member in range(per_block):
                rows = slice(member * own_rows, (member + 1) * own_rows)
                target = owner_ref[block] * per_block + member
                out[target, :own_rows, :] = turned[rows]
                out[target, own_rows:, :] = jnp.concatenate(
                    [gains[:, rows], jnp.zeros((16, tokens - own_rows), BF)], axis=1
                )

    return call(
        body,
        "rows_of_stream",
        (owners, d_stream, *gain_grads),
        [in_scalars(), whole(d_stream)] + [whole(grad) for grad in gain_grads],
        [((owners.shape[0] * per_block, own_rows + 16, tokens), BF)],
        [],
    )[0]


def spread_blocks(values, feeder=None):
    blocks = {0: values}
    for bit in reversed(group_bits()):
        for known in list(blocks):
            blocks[known ^ bit] = swap_group(blocks[known], bit)
            if feeder is not None and bit > 1:
                blocks[known ^ bit] = feeder.tie(blocks[known ^ bit], feeder.width)
    return [blocks[index] for index in range(len(blocks))]


def merge_sums(keep, send, feeder=None):
    count = lax.axis_size("grp")
    assert count == 4
    rows = keep.shape[0] // (count // 2)
    near = swap_group(send, 1)
    blocks = {
        index: keep[index * rows : (index + 1) * rows] + near[index * rows : (index + 1) * rows].astype(F32)
        for index in range(1, count // 2)
    }
    far = swap_group(blocks[1].astype(BF), 2)
    if feeder is not None:
        far = feeder.tie(far)
    return keep, near, far


def forward_layer(
    state, attention_weights, forward_weights, owners, gains, mask, allowed, rows, feeder
):
    stream, normed_low = state
    blocks = feeder.tie(spread_blocks(normed_low, feeder))
    attention_weights = attention_weights()
    normed, queries, key_value, value_all, squashed = project(
        blocks, attention_weights, owners, mask
    )
    memory = feeder.tie(shifted(key_value, 1))
    attended, mixed, keep, send = attend(
        queries, key_value, memory, squashed, mask, allowed, attention_weights, owners, rows
    )
    stream_mid, second_low = join_norm(stream, merge_sums(keep, send, feeder), gains[0])
    blocks = feeder.tie(spread_blocks(second_low, feeder))
    forward_weights = forward_weights()
    second, hidden, slope, keep, send = feed(blocks, forward_weights, owners)
    send = feeder.tie(send)
    stream_out, next_low = join_norm(stream_mid, merge_sums(keep, send, feeder), gains[1])
    stored = (
        stream,
        normed,
        queries,
        key_value,
        memory,
        value_all,
        squashed,
        attended,
        mixed,
        stream_mid,
        second,
        hidden,
        slope,
    )
    return (stream_out, next_low), stored, (attention_weights, forward_weights)


def backward_layer(
    state,
    attention_weights,
    forward_weights,
    owners,
    gains,
    mask,
    allowed,
    stored,
    rows,
    feeder,
    ring,
    pending,
):
    (
        stream,
        normed,
        queries,
        key_value,
        memory,
        value_all,
        squashed,
        attended,
        mixed,
        stream_mid,
        second,
        hidden,
        slope,
    ) = stored
    grad_out, grad_low = state
    def tied(values):
        return feeder.tie(values) if ring else values

    def products(sums, pairs):
        pairs, near = lax.optimization_barrier((pairs, sums[1]))
        parts = [transposed_times(left, right).astype(BF) for left, right in pairs]
        return lax.optimization_barrier(((sums[0], near, sums[2]), parts))

    blocks = spread_blocks(grad_low, feeder if ring else None)
    blocks, pending = lax.optimization_barrier((blocks, pending))
    d_out, d_pre, keep, send = feed_back(blocks, forward_weights, owners, slope)
    sums, parts = products(merge_sums(keep, send), [(second, d_pre), (d_out, hidden)])
    sums = tied(sums)
    grad_mid, grad_mid_low, gain_forward = norm_back(grad_out, sums, stream_mid, gains[1])
    blocks = spread_blocks(grad_mid_low, feeder if ring else None)
    d_branch, d_query, d_gate, d_own, d_past = attend_back(
        blocks, queries, key_value, memory, squashed, mask, allowed, attended, attention_weights, owners
    )
    returned = tied(shifted(d_past, -1))
    d_projected, keep, send = project_back(
        d_query, d_gate, d_own, returned, squashed, mask, value_all, attention_weights, owners, rows
    )
    sums = merge_sums(keep, send)
    if ring:
        sums, more = products(sums, [(normed, d_projected), (d_branch, mixed)])
        sums = tied(sums)
        grads = [(Scatter(*parts, *more), ("up", "down", "project", "output"))]
        feeder.waiting.append(grads[0][0])
        feeder.start()
    else:
        pairs, near = lax.optimization_barrier(
            ([(normed, d_projected), (d_branch, mixed)], sums[1])
        )
        sums = (sums[0], near, sums[2])
        pending = grad_whole(pairs, ring_places())
        grads = [
            (Scatter(*parts), ("up", "down")),
            (scatter_whole(pending), ("project", "output")),
        ]
        feeder.waiting.append(grads[0][0])
        feeder.start()
    grad_in, grad_in_low, gain_attention = norm_back(grad_mid, sums, stream, gains[0])
    return (grad_in, grad_in_low), grads, [gain_attention, gain_forward], pending


def scatter_whole(gradient):
    return lax.psum_scatter(gradient, "seq", scatter_dimension=0, tiled=True)


def own_columns(summed):
    count = lax.axis_size("grp")
    summed = summed.reshape(count, summed.shape[0] // count, summed.shape[1])
    return group_exchange(summed.astype(BF))


def allowed_keys(segment, memory_tail):
    positions = jnp.arange(segment.shape[1], dtype=jnp.int32)
    own_block = (segment[:, :, None] == segment[:, None, :]) & (
        positions[None, None, :] <= positions[None, :, None]
    )
    past_block = (segment[:, :, None] == 0) & (memory_tail[:, None, :] > 0)
    return jnp.concatenate([past_block, own_block], axis=2)


def adamw_update(master, gradient, first, second, factor, rate, decay):
    gradient = gradient * factor
    first_new = BETA_FIRST * first + (1.0 - BETA_FIRST) * gradient
    second_new = BETA_SECOND * second + (1.0 - BETA_SECOND) * gradient * gradient
    first_hat = first_new / (1.0 - BETA_FIRST**STEP)
    second_hat = second_new / (1.0 - BETA_SECOND**STEP)
    master_new = master - rate * (first_hat / (jnp.sqrt(second_hat) + EPS_ADAM) + decay * master)
    return (first_new, second_new, master_new)


def update_layers(factor, grads, masters, firsts, seconds):
    rows = masters[0].shape[1]
    chunk = 8 * DH

    widths = {"up": FF // H, "down": FF // H, "project": QKV_COLS, "output": OUT_COLS}
    flat = [part for parts in grads for part, _ in parts]
    found, index = [], 0
    for parts in grads:
        found.append({})
        for _, names in parts:
            start = 0
            for name in names:
                found[-1][name] = (index, start)
                start += widths[name]
            index += 1

    def body(factor_ref, *refs):
        parts = refs[: len(flat)]
        ins = refs[len(flat) : len(flat) + 6]
        outs = refs[len(flat) + 6 :]
        scale = factor_ref[0, 0]

        def apply(kind, columns, gradient):
            old = [ref[0, :, columns] for ref in ins[3 * kind : 3 * kind + 3]]
            first, second, master = adamw_update(
                old[0], gradient, old[1], old[2], scale, LR_MATRIX, DECAY
            )
            new = (master, first, second)
            for ref, values in zip(outs[3 * kind : 3 * kind + 3], new):
                ref[0, :, columns] = values

        for layer in range(L):

            @pl.when(pl.program_id(0) == layer)
            def _(layer=layer):
                def columns_of(name, member, start, width):
                    place, base = found[layer][name]
                    return parts[place][member, :, base + start : base + start + width].astype(F32)

                def heads(start):
                    return [columns_of("project", member, start, DH) for member in range(H)]

                def experts(name, start):
                    return [
                        columns_of(name, member, start + expert * LANE, DH)
                        for member in range(H)
                        for expert in range(E)
                    ]

                chunks = heads(0) + heads(LANE) + experts("project", 2 * LANE) + experts("output", 0)
                for group in range(len(chunks) // 8):
                    gradient = jnp.concatenate(chunks[8 * group : 8 * group + 8], axis=1)
                    apply(0, slice(group * chunk, (group + 1) * chunk), gradient)
                width = FF // H
                for side, name in enumerate(("up", "down")):
                    for member in range(H):
                        start = QKW + 2 * VW + side * FF + member * width
                        gradient = columns_of(name, member, 0, width)
                        apply(0, slice(start, start + width), gradient)
                selects = [
                    columns_of("project", member, DH + kind * E, E)
                    for kind in range(2)
                    for member in range(H)
                ]
                apply(1, slice(0, SELW), jnp.concatenate(selects, axis=1))

    def layer_block(array):
        return pl.BlockSpec((1,) + array.shape[1:], lambda step: (step, 0, 0))

    states = [masters[0], firsts[0], seconds[0], masters[1], firsts[1], seconds[1]]
    return pl.pallas_call(
        body,
        grid=(L,),
        in_specs=[in_scalars()]
        + [pl.BlockSpec(part.shape, lambda step: (0, 0, 0)) for part in flat]
        + [layer_block(array) for array in states],
        out_specs=[layer_block(array) for array in states],
        out_shape=[jax.ShapeDtypeStruct(array.shape, F32) for array in states],
        compiler_params=pltpu.CompilerParams(vmem_limit_bytes=VMEM_LIMIT),
        name="update_layers",
    )(factor, *flat, *states)


def all_sum(values):
    devices = lax.axis_size("seq") * lax.axis_size("grp")
    sent = jnp.broadcast_to(values[None], (devices,) + values.shape)
    return jnp.sum(
        lax.all_to_all(sent, ("seq", "grp"), split_axis=0, concat_axis=0, tiled=True), axis=0
    )


def document_weights(segment, seg_total, runs, seq_here, row_count):
    seq_count = runs.shape[0]
    device_ids = jnp.arange(seq_count, dtype=jnp.int32)[:, None]
    starts_there = runs[:, :, 0] > 0
    left_pick = jnp.max(jnp.where(starts_there & (device_ids < seq_here), device_ids, -1), axis=0)
    left_run = jnp.where(
        left_pick >= 0,
        jnp.sum(jnp.where(device_ids == left_pick, runs[:, :, 2], 0), axis=0)
        + (seq_here - 1 - left_pick) * row_count,
        0,
    )
    right_pick = jnp.min(
        jnp.where(starts_there & (device_ids > seq_here), device_ids, seq_count), axis=0
    )
    right_run = (
        jnp.sum(jnp.where(device_ids == right_pick, runs[:, :, 1], 0), axis=0)
        + (right_pick - seq_here - 1) * row_count
    )
    local_length = jnp.sum((segment[:, :, None] == segment[:, None, :]).astype(jnp.int32), axis=2)
    doc_length = (
        local_length
        + jnp.where(segment == 0, left_run[:, None], 0)
        + jnp.where(segment == seg_total[:, None], right_run[:, None], 0)
    )
    return 1.0 / doc_length.astype(F32)


def local(
    token_ids,
    target_ids,
    start_flags,
    route_ids,
    embed_table,
    layer_weights,
    router_weights,
    norm_gains,
    embed_mean,
    layer_mean,
    router_mean,
    gains_mean,
    embed_square,
    layer_square,
    router_square,
    gains_square,
):
    row_count = token_ids.shape[1]
    group_count = lax.axis_size("grp")
    own_group = lax.axis_index("grp")
    seq_count = lax.axis_size("seq")
    seq_here = lax.axis_index("seq")
    device_count = seq_count * group_count
    own_rows = embed_table.shape[0]
    positions = jnp.arange(row_count, dtype=jnp.int32)
    quarter = V // group_count

    total_abs = jnp.sum(start_flags, axis=1)
    first_start = jnp.min(jnp.where(start_flags > 0, positions[None, :], row_count), axis=1)
    last_start = jnp.max(jnp.where(start_flags > 0, positions[None, :], -1), axis=1)
    tail_count = jnp.where(total_abs > 0, row_count - last_start, row_count)
    summary = jnp.concatenate([total_abs, first_start, tail_count])
    summary = jnp.pad(summary, (0, row_count - summary.shape[0]))
    told = jnp.stack([token_ids[0], target_ids[0], summary])
    heard = lax.all_to_all(
        jnp.broadcast_to(told[None], (device_count,) + told.shape),
        ("seq", "grp"),
        split_axis=0,
        concat_axis=0,
        tiled=True,
    )
    all_ids = heard[:, 0].reshape(-1)
    heard = heard.reshape(seq_count, group_count, 3, row_count)
    runs = heard[:, 0, 2, : 3 * group_count].reshape(seq_count, 3, group_count).transpose(0, 2, 1)
    doc_count = jnp.sum(runs[:, :, 0]).astype(F32)

    relative = own_group ^ jnp.arange(group_count, dtype=jnp.int32)
    flags = jnp.take(start_flags, relative, axis=0)
    segment = jnp.cumsum(flags, axis=1, dtype=jnp.int32)
    seg_total = segment[:, -1]
    doc_weight = document_weights(
        segment, seg_total, jnp.take(runs, relative, axis=1), seq_here, row_count
    )
    targets = lax.dynamic_index_in_dim(heard[:, :, 1], seq_here, 0, keepdims=False)
    targets = jnp.take(targets, relative, axis=0)
    memory_tail = shifted((segment == seg_total[:, None]).astype(BF), 1)
    routes = jnp.take(route_ids, relative, axis=0).reshape(
        group_count, row_count, 2 * L, H, 2
    )
    routes = lax.dynamic_index_in_dim(routes, own_group, 3, keepdims=False)
    expert_ids = jnp.arange(E, dtype=jnp.int32)
    gate_all = jnp.sum((routes[..., None] == expert_ids).astype(F32), axis=-2)
    gate_all = gate_all.reshape(group_count * row_count, L, 2 * E).transpose(1, 0, 2)
    gate_all = jnp.pad(gate_all, [(0, 0), (0, 0), (DH, LANE - DH - 2 * E)])
    allowed = allowed_keys(segment, memory_tail).astype(F32)
    allowed = allowed.reshape(group_count * row_count, 2 * row_count)

    def exchanged(parts):
        swapped = exchange_parts(parts)
        return swapped.reshape(-1, swapped.shape[2])

    owners = ring_owners()
    own_scalar = own_group.astype(jnp.int32).reshape(1)
    attention_parts, forward_parts = arrange_layer(own_scalar, 0, layer_weights, router_weights)
    first = exchanged(attention_parts)
    first, forward_parts = lax.optimization_barrier((first, forward_parts))
    first_attention = Gather(first)
    first_forward = Gather(exchanged(forward_parts))
    feeder = Feed([first_attention])
    feeder.start()
    all_ids = feeder.tie(all_ids)

    looked = lookup(all_ids, embed_table).astype(BF) * D**0.5
    gate_all, looked, first_forward.flying = lax.optimization_barrier(
        (gate_all, looked, first_forward.flying)
    )
    looked = feeder.tie(looked)
    feeder.waiting.append(first_forward)
    gain_rows = norm_gains.astype(BF).T
    gain_rows = jnp.pad(gain_rows, [(0, 16 - NG), (0, row_count - own_rows)])
    sent = jnp.concatenate(
        [looked, jnp.broadcast_to(gain_rows[None], (device_count,) + gain_rows.shape)], axis=1
    )
    received = lax.all_to_all(sent, ("seq", "grp"), split_axis=0, concat_axis=0, tiled=True)
    received = feeder.tie(received)
    if seq_count > RING_LIMIT:
        stream = received[:, :own_rows].reshape(D, row_count).T.astype(F32)
        gains = received[:, own_rows : own_rows + NG, :own_rows].transpose(1, 0, 2)
        gains = gains.reshape(NG, D).astype(F32)
        state = (stream, rms_norm(stream, gains[0]).astype(BF))
    else:
        stream, normed_low, gains = stream_of_rows(received, owners, own_rows)
        state = (stream, normed_low)
    gains = gains[:NG, None, :]
    later, table_later, normed_here = lax.optimization_barrier(
        (layer_weights, embed_table, state[1])
    )
    state = (stream, normed_here)
    attention_parts, forward_parts = arrange_layer(own_scalar, 1, later, router_weights)
    second_attention = exchanged(attention_parts)
    second_forward = exchanged(forward_parts)
    table_own = exchanged(arrange_table(own_scalar, table_later))
    gathers = [
        first_attention,
        first_forward,
        Gather(second_attention),
        Gather(second_forward),
        Gather(table_own),
    ]
    feeder.waiting.extend(gathers[2:])
    layer_pieces = [
        tuple(lambda gather=gather: Weights(gather.result()) for gather in gathers[start : start + 2])
        for start in (0, 2)
    ]
    saved_layers = []
    saved_pieces = []
    for layer_index in range(L):
        state, stored, pieces = forward_layer(
            state,
            *layer_pieces[layer_index],
            owners,
            gains[2 * layer_index + 1 : 2 * layer_index + 3],
            gate_all[layer_index],
            allowed,
            row_count,
            feeder,
        )
        saved_layers.append(stored)
        saved_pieces.append(pieces)

    stream, final_low = state
    final_gain = gains[2 * L]
    final_all = jnp.concatenate(spread_blocks(final_low, feeder), axis=0)
    table_part = jnp.concatenate(gathers[4].result(), axis=0)
    logits = times_plain(final_all, table_part)
    columns = jnp.arange(logits.shape[1], dtype=jnp.int32)[None, :]
    logits = jnp.where(columns < quarter, logits, -1e30)
    hit = columns == (targets.reshape(-1) - own_group * quarter)[:, None]
    hit = hit & (columns < quarter)
    log_part = jax.nn.logsumexp(logits, axis=-1).reshape(group_count, row_count)
    target_part = jnp.sum(jnp.where(hit, logits, 0.0), axis=1).reshape(group_count, row_count)
    stats = jnp.stack([log_part, target_part], axis=1)
    others = [stats]
    for offset in range(1, group_count):
        got = swap_group(stats, offset)
        others.append(jnp.stack([got[index ^ offset] for index in range(group_count)]))
    others = jnp.stack(others)
    log_total = jax.nn.logsumexp(others[:, :, 0], axis=0)
    target_logit = jnp.sum(others[:, :, 1], axis=0)
    loss_local = jnp.sum((log_total[0] - target_logit[0]) * doc_weight[0])
    scale = (doc_weight / doc_count).reshape(-1)[:, None]
    d_logits = (jnp.exp(logits - log_total.reshape(-1)[:, None]) - hit.astype(F32)) * scale
    d_logits = d_logits.astype(BF)
    d_final = times_transposed(d_logits, table_part).reshape(group_count, row_count, D)
    keep = d_final[0::2].reshape(-1, D)
    send = d_final[1::2].reshape(-1, D).astype(BF)
    keep, send, d_logits = lax.optimization_barrier((keep, send, d_logits))
    sums = merge_sums(keep, send)
    table_grad = grad_whole([(final_all, d_logits)], ring_places())
    sums, table_grad = lax.optimization_barrier((sums, table_grad))
    table_grad = scatter_whole(table_grad)
    feeder = Feed()
    d_stream, d_stream_low, grad_final_gain = norm_back(
        jnp.zeros_like(stream), sums, stream, final_gain
    )

    state = (d_stream, d_stream_low)
    layer_grads = [None] * L
    gain_parts = [None] * L
    pending = ()
    for layer_index in reversed(range(L)):
        state, layer_grads[layer_index], gain_parts[layer_index], pending = backward_layer(
            state,
            *saved_pieces[layer_index],
            owners,
            gains[2 * layer_index : 2 * layer_index + 2],
            gate_all[layer_index],
            allowed,
            saved_layers[layer_index],
            row_count,
            feeder,
            layer_index == 0,
            pending,
        )

    gain_grads = sum(gain_parts, []) + [grad_final_gain]
    if seq_count > RING_LIMIT:
        gain_grads = jnp.concatenate(gain_grads).reshape(NG, device_count, own_rows)
        gain_grads = jnp.pad(
            gain_grads.transpose(1, 0, 2), [(0, 0), (0, 16 - NG), (0, row_count - own_rows)]
        )
        d_stream = state[0].T.reshape(device_count, own_rows, row_count)
        sent = jnp.concatenate([d_stream, gain_grads], axis=1).astype(BF)
    else:
        sent = rows_of_stream(state[0], gain_grads, owners, own_rows)
    received = lax.all_to_all(
        sent, ("seq", "grp"), split_axis=0, concat_axis=0, tiled=True
    ).astype(F32)
    received = feeder.tie(received)
    embed_grad, square = spread_tokens(
        all_ids, received[:, :own_rows], own_columns(table_grad), V
    )
    embed_grad, square = feeder.tie((embed_grad, square))
    gains_grad = jnp.sum(received[:, own_rows : own_rows + NG, :own_rows], axis=0).T
    square = square[0, 0] + jnp.sum(gains_grad * gains_grad)
    layer_parts = []
    for grads in layer_grads:
        parts = []
        for member, names in grads:
            part = member.result() if isinstance(member, Scatter) else member
            square = square + jnp.sum(jnp.square(part.astype(F32)))
            part = own_columns(part)
            parts.append((part, names))
        layer_parts.append(parts)
    sums = all_sum(jnp.stack([loss_local, square]))
    loss_sum = sums[0]
    grad_norm = jnp.sqrt(sums[1])
    factor = CLIP / jnp.maximum(grad_norm, CLIP)
    embed_out = adamw_update(
        embed_table, embed_grad, embed_mean, embed_square, factor, LR_MATRIX, DECAY
    )
    updated = update_layers(
        factor.reshape(1, 1),
        layer_parts,
        (layer_weights, router_weights),
        (layer_mean, router_mean),
        (layer_square, router_square),
    )
    layer_out, router_out = [(new[1], new[2], new[0]) for new in (updated[:3], updated[3:])]
    gains_out = adamw_update(norm_gains, gains_grad, gains_mean, gains_square, factor, LR_GAIN, 0.0)
    return (
        loss_sum,
        doc_count,
        grad_norm,
        embed_out[0],
        embed_out[1],
        embed_out[2],
        layer_out[0],
        layer_out[1],
        layer_out[2],
        router_out[0],
        router_out[1],
        router_out[2],
        gains_out[0],
        gains_out[1],
        gains_out[2],
    )


def solution(mesh):
    rows = P(("seq", "grp"), None)
    layers = P(None, ("seq", "grp"), None)
    return jax.shard_map(
        local,
        mesh=mesh,
        in_specs=(
            P("grp", "seq"),
            P("grp", "seq"),
            P(None, "seq"),
            P(None, "seq", None, None),
            rows,
            layers,
            layers,
            rows,
            rows,
            layers,
            layers,
            rows,
            rows,
            layers,
            layers,
            rows,
        ),
        out_specs=(P(), P(), P()) + (rows,) * 3 + (layers,) * 6 + (rows,) * 3,
        check_vma=False,
    )
```

```python
import jax
import jax.numpy as jnp
from jax import lax
from jax.experimental import pallas as pl
from jax.experimental.pallas import tpu as pltpu
from jax.sharding import PartitionSpec as P

D = 1024
H = 4
DH = 112
E = 5
FF = 4096
V = 8000
L = 2
STEP = 10
QKW = 896
VW = 2240
SELW = 40
LANE = 128
NG = 5

EPS_NORM = 1e-05
CLIP = 0.05
LR_MATRIX = 0.06
LR_GAIN = 0.3
BETA_FIRST = 0.9
BETA_SECOND = 0.999
EPS_ADAM = 1e-08
DECAY = 0.1

QKV_COLS = (2 + E) * LANE
OUT_COLS = E * LANE
ATT_COLS = QKV_COLS + OUT_COLS
BF = jnp.bfloat16
F32 = jnp.float32


def times_plain(left_side, right_side):
    return jnp.dot(left_side, right_side, preferred_element_type=F32)


def times_transposed(left_side, right_side):
    return lax.dot_general(
        left_side, right_side, (((1,), (1,)), ((), ())), preferred_element_type=F32
    )


def transposed_times(left_side, right_side):
    return lax.dot_general(
        left_side, right_side, (((0,), (0,)), ((), ())), preferred_element_type=F32
    )


def rms_norm(values, gain_row):
    return (
        values * lax.rsqrt(jnp.mean(values * values, axis=-1, keepdims=True) + EPS_NORM) * gain_row
    )


def gelu_exact(values):
    return jax.nn.gelu(values, approximate=False)


def swap_group(values, bit):
    count = lax.axis_size("grp")
    return lax.ppermute(values, "grp", [(member, member ^ bit) for member in range(count)])


def group_bits():
    count = lax.axis_size("grp")
    return [1 << power for power in range(count.bit_length() - 1)]


def spread_rows(values):
    blocks = {0: values}
    for bit in reversed(group_bits()):
        for known in list(blocks):
            blocks[known ^ bit] = swap_group(blocks[known], bit)
    return jnp.concatenate([blocks[index] for index in range(len(blocks))], axis=0)


def merge_rows(values):
    count = lax.axis_size("grp")
    rows = values.shape[0] // count
    blocks = {index: values[index * rows : (index + 1) * rows] for index in range(count)}
    for bit in group_bits():
        away = [index for index in sorted(blocks) if index & bit]
        sent = jnp.concatenate([blocks[index].astype(BF) for index in away], axis=0)
        received = swap_group(sent, bit).astype(F32)
        blocks = {
            index ^ bit: blocks[index ^ bit] + received[place * rows : (place + 1) * rows]
            for place, index in enumerate(away)
        }
    return blocks[0]


def exchange_parts(parts):
    own = lax.axis_index("grp")
    parts = [parts[0]] + [swap_group(part, offset) for offset, part in enumerate(parts) if offset]
    return jnp.stack([lax.select_n(own ^ member, *parts) for member in range(len(parts))])


def group_exchange(values):
    count = lax.axis_size("grp")
    own = lax.axis_index("grp")
    cases = [values[member] for member in range(count)]
    parts = [lax.select_n(own ^ offset, *cases) for offset in range(count)]
    parts = [parts[0]] + [swap_group(parts[offset], offset) for offset in range(1, count)]
    return jnp.stack([lax.select_n(own ^ member, *parts) for member in range(count)])


def shifted(value, steps):
    count = lax.axis_size("seq")
    first, last = (max(0, -steps), min(count, count - steps))
    return lax.ppermute(value, "seq", [(source, source + steps) for source in range(first, last)])


RING_LIMIT = 8


def ring_order(count):
    return list(range(0, count, 2)) + list(range(count - 1, 0, -2))


def ring_pairs(count, step):
    order = ring_order(count)
    return [(order[place], order[(place + step) % count]) for place in range(count)]


def ring_place(device, count):
    return jnp.where(device % 2 == 0, device // 2, count - 1 - device // 2)


def ring_device(place, count):
    return jnp.where(2 * place < count, 2 * place, 2 * (count - 1 - place) + 1)


class Gather:
    def __init__(self, values, ring=True):
        self.count = lax.axis_size("seq")
        self.whole = None
        self.blocks = {0: values}
        self.left = self.count // 2
        if self.count > RING_LIMIT or not ring:
            self.whole = lax.all_gather(values, "seq", axis=0, tiled=True)
            self.left = 0
        self.flying = (values, values)

    def land(self):
        return self.flying

    def step(self, landed):
        ahead, behind = landed
        done = self.count // 2 - self.left + 1
        ahead = lax.ppermute(ahead, "seq", ring_pairs(self.count, 1))
        self.blocks[self.count - done] = ahead
        if done < self.count - self.count // 2:
            behind = lax.ppermute(behind, "seq", ring_pairs(self.count, -1))
            self.blocks[done] = behind
        self.flying = (ahead, behind)
        self.left -= 1

    def result(self):
        while self.left:
            self.step(self.flying)
        if self.whole is not None:
            return [self.whole]
        return [self.blocks[place] for place in range(len(self.blocks))]


class Scatter:
    def __init__(self, *parts):
        self.count = lax.axis_size("seq")
        self.parts, self.rows = parts, D // self.count
        self.left = self.count // 2
        self.whole = None
        if self.count > RING_LIMIT:
            joined = jnp.concatenate(self.parts, axis=1)
            self.whole = lax.psum_scatter(joined, "seq", scatter_dimension=0, tiled=True)
            self.left = 0
        self.flying = ()

    def land(self):
        return self.flying

    def step(self, landed):
        back = self.count - 1 - self.count // 2
        done = self.count // 2 - self.left
        places, received = [self.left], [landed[:1]]
        if done < back:
            places.append(self.count - back + done)
            received.append(landed[1:])
        sums = add_blocks(self.parts, places, received, self.rows)
        ahead = lax.ppermute(sums[0], "seq", ring_pairs(self.count, 1))
        behind = landed[1] if done >= back else lax.ppermute(
            sums[1], "seq", ring_pairs(self.count, -1)
        )
        self.flying = (ahead, behind)
        self.left -= 1

    def result(self):
        while self.left:
            self.step(self.flying)
        if self.whole is not None:
            return self.whole
        return add_blocks(self.parts, [0], [self.flying], self.rows)[0]


class Feed:
    def __init__(self, tasks=(), width=1):
        self.waiting = list(tasks)
        self.width = width
        self.flying = []

    def tie(self, values, width=1):
        landed = [task.land() for task in self.flying]
        values, landed = lax.optimization_barrier((values, landed))
        for task, arrived in zip(self.flying, landed):
            task.flying = tuple(arrived)
        self.start(width)
        return values

    def start(self, width=1):
        self.waiting = [task for task in self.waiting if task.left]
        self.flying = self.waiting[:width]
        for task in self.flying:
            task.step(task.flying)


def ring_owners():
    count = lax.axis_size("seq")
    if count > RING_LIMIT:
        return jnp.zeros((1,), jnp.int32)
    here = ring_place(lax.axis_index("seq"), count)
    return ring_device(lax.rem(jnp.arange(count, dtype=jnp.int32) + here, count), count)


def ring_places():
    count = lax.axis_size("seq")
    if count > RING_LIMIT:
        return jnp.zeros((1,), jnp.int32)
    here = ring_place(lax.axis_index("seq"), count)
    devices = jnp.arange(count, dtype=jnp.int32)
    return lax.rem(ring_place(devices, count) - here + count, count)


def pick_blocks(values, order):
    if order.shape[0] == 1:
        return values
    shape = values.shape
    return jnp.take(values.reshape((order.shape[0], -1) + shape[1:]), order, axis=0).reshape(shape)


def to_ring(values):
    return pick_blocks(values, ring_owners())


def from_ring(values):
    return pick_blocks(values, ring_places())


def after(values, *others):
    return lax.optimization_barrier((values, *others))[0]


def pad_lanes(values):
    return jnp.pad(values, [(0, 0)] * (values.ndim - 1) + [(0, LANE - values.shape[-1])])


def choose(own, offset, cases):
    member = own ^ offset
    value = cases[0]
    for index in range(1, len(cases)):
        value = jnp.where(member == index, cases[index], value)
    return value


def arrange_layer(own, layer, weights, routers):
    rows, columns = weights.shape[1:]
    members = H

    def body(own_ref, weight_ref, router_ref, *outs):
        here = own_ref[0]

        def lanes(pieces):
            filled = sum(piece.shape[1] for piece in pieces)
            zeros = [jnp.zeros((rows, LANE - filled), F32)]
            return jnp.concatenate(pieces + zeros, axis=1).astype(BF)

        def chunk(start):
            return weight_ref[0, :, start : start + DH]

        tiles = []
        for member in range(members):
            picked = [
                router_ref[0, :, (kind * H + member) * E : (kind * H + member + 1) * E]
                for kind in range(2)
            ]
            group = [lanes([chunk(member * DH)] + picked), lanes([chunk((H + member) * DH)])]
            for base in (QKW, QKW + VW):
                for expert in range(E):
                    group.append(lanes([chunk(base + (member * E + expert) * DH)]))
            tiles.append(group)
        base = QKW + 2 * VW
        width = FF // members
        for offset in range(members):
            for index in range(len(tiles[0])):
                outs[offset][:, index * LANE : (index + 1) * LANE] = choose(
                    here, offset, [group[index] for group in tiles]
                )
            for side in range(2):
                start = base + side * FF
                outs[members + offset][:, side * width : (side + 1) * width] = choose(
                    here,
                    offset,
                    [
                        weight_ref[0, :, start + member * width : start + (member + 1) * width]
                        for member in range(members)
                    ],
                ).astype(BF)

    shapes = [(rows, ATT_COLS)] * members + [(rows, 2 * FF // members)] * members
    parts = pl.pallas_call(
        body,
        grid=(1,),
        in_specs=[
            in_scalars(),
            pl.BlockSpec((1, rows, columns), lambda step: (layer, 0, 0)),
            pl.BlockSpec((1, rows, SELW), lambda step: (layer, 0, 0)),
        ],
        out_specs=[part(shape) for shape in shapes],
        out_shape=[jax.ShapeDtypeStruct(shape, BF) for shape in shapes],
        compiler_params=pltpu.CompilerParams(vmem_limit_bytes=VMEM_LIMIT),
        cost_estimate=pl.CostEstimate(flops=1, bytes_accessed=1, transcendentals=0),
        name="arrange_layer",
    )(own, weights, routers)
    return parts[:members], parts[members:]


def arrange_table(own, table):
    rows, width = table.shape
    quarter = width // H
    padded = -(-quarter // LANE) * LANE

    def body(own_ref, table_ref, *outs):
        zeros = jnp.zeros((rows, padded - quarter), F32)
        cases = [
            jnp.concatenate([table_ref[:, member * quarter : (member + 1) * quarter], zeros], axis=1)
            for member in range(H)
        ]
        for offset in range(H):
            outs[offset][...] = choose(own_ref[0], offset, cases).astype(BF)

    return call(
        body,
        "arrange_table",
        (own, table),
        [in_scalars(), whole(table)],
        [((rows, padded), BF) for _ in range(H)],
        [],
    )


def lookup_body(ids_ref, table_ref, out_ref, by_token, picked):
    rows = table_ref.shape[0]
    width = table_ref.shape[1]
    for start in range(0, width, LANE):
        end = min(start + LANE, width)
        by_token[start:end, :rows] = table_ref[:, start:end].T

    @pl.loop(0, out_ref.shape[0])
    def _(device):
        base = device * LANE

        for token in range(LANE):
            picked[pl.ds(token, 1), :] = by_token[pl.ds(ids_ref[base + token], 1), :]
        out_ref[device] = picked[...].T[:rows]


def lookup(ids, table):
    rows, width = table.shape
    devices = ids.shape[0] // LANE
    return pl.pallas_call(
        lookup_body,
        grid_spec=pltpu.PrefetchScalarGridSpec(
            num_scalar_prefetch=1,
            grid=(1,),
            in_specs=[pl.BlockSpec((rows, width), lambda i, ids: (0, 0))],
            out_specs=pl.BlockSpec((devices, rows, LANE), lambda i, ids: (0, 0, 0)),
            scratch_shapes=[pltpu.VMEM((width, LANE), F32), pltpu.VMEM((LANE, LANE), F32)],
        ),
        out_shape=jax.ShapeDtypeStruct((devices, rows, LANE), F32),
        compiler_params=pltpu.CompilerParams(vmem_limit_bytes=48 * 1024 * 1024),
        name="lookup",
    )(ids, table)


ACCUMULATORS = 4


def spread_body(ids_ref, grad_ref, table_ref, out_ref, square_ref, *scratch):
    rows, width = out_ref.shape
    members = table_ref.shape[0]
    totals, picked = scratch[:-1], scratch[-1]
    for total in totals:
        total[...] = jnp.zeros_like(total)

    @pl.loop(0, grad_ref.shape[0])
    def _(device):
        base = device * LANE
        picked[:, :rows] = grad_ref[device].T

        for step in range(LANE // ACCUMULATORS):
            for which, total in enumerate(totals):
                token = step * ACCUMULATORS + which
                place = pl.ds(ids_ref[base + token], 1)
                total[place, :] += picked[pl.ds(token, 1), :]

    for start in range(0, width, LANE):
        end = min(start + LANE, width)
        found = sum(total[start:end, :] for total in totals).T[:rows]
        out_ref[:, start:end] = found * D**0.5
    quarter = width // members
    table = jnp.concatenate([table_ref[member][:, :quarter] for member in range(members)], axis=1)
    total = out_ref[...] + table.astype(F32)
    out_ref[...] = total
    square_ref[0, 0] = jnp.sum(total * total)


def spread_tokens(ids, grads, table_parts, width):
    devices, rows, _ = grads.shape
    return pl.pallas_call(
        spread_body,
        grid_spec=pltpu.PrefetchScalarGridSpec(
            num_scalar_prefetch=1,
            grid=(1,),
            in_specs=[
                pl.BlockSpec((devices, rows, LANE), lambda i, ids: (0, 0, 0)),
                pl.BlockSpec(table_parts.shape, lambda i, ids: (0, 0, 0)),
            ],
            out_specs=[
                pl.BlockSpec((rows, width), lambda i, ids: (0, 0)),
                pl.BlockSpec(memory_space=pltpu.SMEM),
            ],
            scratch_shapes=[pltpu.VMEM((width, LANE), F32) for _ in range(ACCUMULATORS)]
            + [pltpu.VMEM((LANE, LANE), F32)],
        ),
        out_shape=[
            jax.ShapeDtypeStruct((rows, width), F32),
            jax.ShapeDtypeStruct((1, 1), F32),
        ],
        compiler_params=pltpu.CompilerParams(vmem_limit_bytes=48 * 1024 * 1024),
        name="spread",
    )(ids, grads, table_parts)


VMEM_LIMIT = 56 * 1024 * 1024
SCALE = DH ** (-0.5)


def whole(array):
    return pl.BlockSpec(array.shape, lambda step: (0,) * array.ndim)


def part(shape):
    return pl.BlockSpec(shape, lambda step: (0,) * len(shape))


def in_scalars():
    return pl.BlockSpec(memory_space=pltpu.SMEM)


def anywhere():
    return pl.BlockSpec(memory_space=pl.ANY)


def call(body, name, inputs, specs, outputs, scratch, ties=()):
    ties = tuple(ties)

    def wrapped(*refs):
        count = len(inputs)
        body(*refs[:count], *refs[count + len(ties) :])

    return pl.pallas_call(
        wrapped,
        grid=(1,),
        in_specs=list(specs) + [anywhere()] * len(ties),
        out_specs=[part(shape) for shape, _ in outputs],
        out_shape=[jax.ShapeDtypeStruct(shape, kind) for shape, kind in outputs],
        scratch_shapes=scratch,
        compiler_params=pltpu.CompilerParams(vmem_limit_bytes=VMEM_LIMIT),
        cost_estimate=pl.CostEstimate(flops=1, bytes_accessed=1, transcendentals=0),
        name=name,
    )(*inputs, *ties)


class Weights:
    def __init__(self, arrays, base=0):
        self.arrays, self.base = list(arrays), base
        self.natural = len(self.arrays) == 1
        self.count = ring_owners().shape[0] if self.natural else len(self.arrays)

    def specs(self):
        return [anywhere() for _ in self.arrays]

    def copies(self, owners, refs, start, width, target, semaphores):
        copies = []
        rows = D // self.count
        columns = pl.ds(self.base + start, width)
        for index in range(self.count):
            if not self.natural:
                source = refs[index].at[:, columns]
            elif self.count == 1:
                source = refs[0].at[:, columns]
            else:
                place = pl.multiple_of(owners[index] * rows, rows)
                source = refs[0].at[pl.ds(place, rows), columns]
            copy = pltpu.make_async_copy(
                source, target.at[pl.ds(index * rows, rows)], semaphores.at[index]
            )
            copy.start()
            copies.append(copy)
        return copies


def gate_column(gates, kind, expert):
    place = DH + kind * E + expert
    return gates[:, place : place + 1]


def expert_lanes(values, expert):
    return values[:, expert * LANE : (expert + 1) * LANE]


def dot_nn(left, right):
    return lax.dot_general(left, right, (((1,), (0,)), ((), ())), preferred_element_type=F32)


def dot_nt(left, right):
    return lax.dot_general(left, right, (((1,), (1,)), ((), ())), preferred_element_type=F32)


def dot_tn(left, right):
    return lax.dot_general(left, right, (((0,), (0,)), ((), ())), preferred_element_type=F32)


def store_split(keep, send, pair, values, rows):
    keep[pl.ds(pair * rows, rows), :] = values[:rows]
    send[pl.ds(pair * rows, rows), :] = values[rows:].astype(BF)


def project(blocks, weights, owners, mask, ties=()):
    chains, rows = len(blocks), blocks[0].shape[0]
    total = chains * rows
    arrays = len(weights.arrays)

    def body(owner_ref, *refs):
        xs, ws, mask_ref = refs[:chains], refs[chains : chains + arrays], refs[chains + arrays]
        normed, queries, key_value, value_all, squashed, weight, semaphores = refs[
            chains + arrays + 1 :
        ]
        copies = weights.copies(owner_ref, ws, 0, QKV_COLS, weight, semaphores)
        for chain in range(chains):
            normed[chain * rows : (chain + 1) * rows, :] = xs[chain][...]
        for copy in copies:
            copy.wait()

        @pl.loop(0, chains // 2)
        def _(pair):
            at = pl.ds(pair * 2 * rows, 2 * rows)
            projected = dot_nn(normed[at, :], weight[...])
            first = projected[:, :LANE]
            lanes = lax.broadcasted_iota(jnp.int32, first.shape, 1)
            queries[at, :] = jnp.where(lanes < DH, first, 0.0).astype(BF)
            soft = jax.nn.sigmoid(first)
            squashed[at, :] = soft
            gates = soft * mask_ref[at, :]
            values = projected[:, 2 * LANE :]
            value_all[at, :] = values
            mixed = sum(
                gate_column(gates, 0, expert) * expert_lanes(values, expert) for expert in range(E)
            )
            key_value[at, :LANE] = projected[:, LANE : 2 * LANE].astype(BF)
            key_value[at, LANE:] = mixed.astype(BF)

    return call(
        body,
        "project",
        (owners, *blocks, *weights.arrays, mask),
        [in_scalars()] + [whole(block) for block in blocks] + weights.specs() + [whole(mask)],
        [
            ((total, D), BF),
            ((total, LANE), BF),
            ((total, 2 * LANE), BF),
            ((total, E * LANE), F32),
            ((total, LANE), F32),
        ],
        [pltpu.VMEM((D, QKV_COLS), BF), pltpu.SemaphoreType.DMA((weights.count,))],
        ties,
    )


def probabilities(queries, keys, allowed):
    scores = jnp.where(allowed > 0, dot_nt(queries, keys) * SCALE, -1e30)
    raised = jnp.exp(scores - jnp.max(scores, axis=1, keepdims=True))
    return raised / jnp.sum(raised, axis=1, keepdims=True)


def attend(queries, key_value, memory, squashed, mask, allowed, weights, owners, rows, ties=()):
    total = queries.shape[0]
    chains = total // rows

    def body(owner_ref, q_ref, own_ref, past_ref, squash_ref, mask_ref, allow_ref, *refs):
        ws = refs[: len(weights.arrays)]
        attended, mixed, keep, send, weight, semaphores = refs[len(weights.arrays) :]
        copies = weights.copies(owner_ref, ws, QKV_COLS, OUT_COLS, weight, semaphores)
        for chain in range(chains):
            at = slice(chain * rows, (chain + 1) * rows)
            keys = jnp.concatenate([past_ref[at, :LANE], own_ref[at, :LANE]], axis=0)
            values = jnp.concatenate([past_ref[at, LANE:], own_ref[at, LANE:]], axis=0)
            soft = probabilities(q_ref[at, :], keys, allow_ref[at, :])
            got = dot_nn(soft.astype(BF), values)
            attended[at, :] = got
            gates = squash_ref[at, :] * mask_ref[at, :]
            for expert in range(E):
                mixed[at, expert * LANE : (expert + 1) * LANE] = (
                    gate_column(gates, 1, expert) * got
                ).astype(BF)
        for copy in copies:
            copy.wait()

        @pl.loop(0, chains // 2)
        def _(pair):
            out = dot_nt(mixed[pl.ds(pair * 2 * rows, 2 * rows), :], weight[...])
            store_split(keep, send, pair, out, rows)

    return call(
        body,
        "attend",
        (owners, queries, key_value, memory, squashed, mask, allowed, *weights.arrays),
        [in_scalars()]
        + [whole(array) for array in (queries, key_value, memory, squashed, mask, allowed)]
        + weights.specs(),
        [
            ((total, LANE), F32),
            ((total, E * LANE), BF),
            ((total // 2, D), F32),
            ((total // 2, D), BF),
        ],
        [pltpu.VMEM((D, OUT_COLS), BF), pltpu.SemaphoreType.DMA((weights.count,))],
        ties,
    )


def feed(blocks, weights, owners, ties=()):
    chains, rows = len(blocks), blocks[0].shape[0]
    total = chains * rows
    width = FF // H
    count, arrays = weights.count, len(weights.arrays)

    def body(owner_ref, *refs):
        xs, ws = refs[:chains], refs[chains : chains + arrays]
        second, hidden, slope, keep, send, up, down, up_sems, down_sems = refs[
            chains + arrays :
        ]
        up_copies = weights.copies(owner_ref, ws, 0, width, up, up_sems)
        down_copies = weights.copies(owner_ref, ws, width, width, down, down_sems)
        for chain in range(chains):
            second[chain * rows : (chain + 1) * rows, :] = xs[chain][...]
        for copy in up_copies:
            copy.wait()

        @pl.loop(0, chains // 2)
        def _(pair):
            at = pl.ds(pair * 2 * rows, 2 * rows)
            pre = dot_nn(second[at, :], up[...])
            rising = 0.5 * (1.0 + lax.erf(pre * 0.5**0.5))
            hidden[at, :] = (pre * rising).astype(BF)
            slope[at, :] = rising + pre * jnp.exp(-0.5 * pre * pre) * 0.3989422804014327

        for copy in down_copies:
            copy.wait()

        @pl.loop(0, chains // 2)
        def _(pair):
            out = dot_nt(hidden[pl.ds(pair * 2 * rows, 2 * rows), :], down[...])
            store_split(keep, send, pair, out, rows)

    return call(
        body,
        "feed",
        (owners, *blocks, *weights.arrays),
        [in_scalars()] + [whole(block) for block in blocks] + weights.specs(),
        [
            ((total, D), BF),
            ((total, width), BF),
            ((total, width), F32),
            ((total // 2, D), F32),
            ((total // 2, D), BF),
        ],
        [pltpu.VMEM((D, width), BF)] * 2 + [pltpu.SemaphoreType.DMA((count,))] * 2,
        ties,
    )


def feed_back(blocks, weights, owners, slope, ties=()):
    chains, rows = len(blocks), blocks[0].shape[0]
    total = chains * rows
    width = FF // H
    count, arrays = weights.count, len(weights.arrays)

    def body(owner_ref, *refs):
        ds, ws = refs[:chains], refs[chains : chains + arrays]
        slope_ref, d_out, d_pre, keep, send, up, down, up_sems, down_sems = refs[
            chains + arrays :
        ]
        down_copies = weights.copies(owner_ref, ws, width, width, down, down_sems)
        up_copies = weights.copies(owner_ref, ws, 0, width, up, up_sems)
        for chain in range(chains):
            d_out[chain * rows : (chain + 1) * rows, :] = ds[chain][...]
        for copy in down_copies:
            copy.wait()

        @pl.loop(0, chains // 2)
        def _(pair):
            at = pl.ds(pair * 2 * rows, 2 * rows)
            d_pre[at, :] = (dot_nn(d_out[at, :], down[...]) * slope_ref[at, :]).astype(BF)

        for copy in up_copies:
            copy.wait()

        @pl.loop(0, chains // 2)
        def _(pair):
            out = dot_nt(d_pre[pl.ds(pair * 2 * rows, 2 * rows), :], up[...])
            store_split(keep, send, pair, out, rows)

    return call(
        body,
        "feed_back",
        (owners, *blocks, *weights.arrays, slope),
        [in_scalars()] + [whole(block) for block in blocks] + weights.specs() + [whole(slope)],
        [
            ((total, D), BF),
            ((total, width), BF),
            ((total // 2, D), F32),
            ((total // 2, D), BF),
        ],
        [pltpu.VMEM((D, width), BF)] * 2 + [pltpu.SemaphoreType.DMA((count,))] * 2,
        ties,
    )


def attend_back(
    blocks, queries, key_value, memory, squashed, mask, allowed, attended, weights, owners, ties=()
):
    chains, rows = len(blocks), blocks[0].shape[0]
    total = chains * rows
    count = len(weights.arrays)

    def body(owner_ref, *refs):
        ds, refs = refs[:chains], refs[chains:]
        q_ref, own_ref, past_ref, squash_ref, mask_ref, allow_ref, att_ref = refs[:7]
        ws, refs = refs[7 : 7 + count], refs[7 + count :]
        d_branch, d_query, d_gate, d_own, d_past, weight, semaphores = refs
        copies = weights.copies(owner_ref, ws, QKV_COLS, OUT_COLS, weight, semaphores)
        for chain in range(chains):
            d_branch[chain * rows : (chain + 1) * rows, :] = ds[chain][...]
        for copy in copies:
            copy.wait()
        for pair in range(chains // 2):
            pair_mixed = dot_nn(
                d_branch[pair * 2 * rows : (pair + 1) * 2 * rows, :], weight[...]
            ).astype(BF)
            for side in range(2):
                chain = pair * 2 + side
                at = slice(chain * rows, (chain + 1) * rows)
                d_mixed = pair_mixed[side * rows : (side + 1) * rows].astype(F32)
                gates = squash_ref[at, :] * mask_ref[at, :]
                d_att = sum(
                    gate_column(gates, 1, expert) * expert_lanes(d_mixed, expert)
                    for expert in range(E)
                ).astype(BF)
                got = att_ref[at, :]
                lanes = lax.broadcasted_iota(jnp.int32, (rows, LANE), 1)
                d_gates = jnp.zeros((rows, LANE), F32)
                for expert in range(E):
                    column = jnp.sum(expert_lanes(d_mixed, expert) * got, axis=1, keepdims=True)
                    d_gates = jnp.where(lanes == DH + E + expert, column, d_gates)
                d_gate[at, :] = d_gates
                keys = jnp.concatenate([past_ref[at, :LANE], own_ref[at, :LANE]], axis=0)
                values = jnp.concatenate([past_ref[at, LANE:], own_ref[at, LANE:]], axis=0)
                query = q_ref[at, :]
                soft = probabilities(query, keys, allow_ref[at, :])
                d_soft = dot_nt(d_att, values)
                delta = jnp.sum(soft * d_soft, axis=1, keepdims=True)
                d_scores = (soft * (d_soft - delta)).astype(BF)
                d_query[at, :] = dot_nn(d_scores, keys) * SCALE
                d_keys = dot_tn(d_scores, query) * SCALE
                d_values = dot_tn(soft.astype(BF), d_att)
                d_past[at, :LANE] = d_keys[:rows].astype(BF)
                d_past[at, LANE:] = d_values[:rows].astype(BF)
                d_own[at, :LANE] = d_keys[rows:]
                d_own[at, LANE:] = d_values[rows:]

    arrays = (queries, key_value, memory, squashed, mask, allowed, attended)
    return call(
        body,
        "attend_back",
        (owners, *blocks, *arrays, *weights.arrays),
        [in_scalars()]
        + [whole(block) for block in blocks]
        + [whole(array) for array in arrays]
        + weights.specs(),
        [
            ((total, D), BF),
            ((total, LANE), F32),
            ((total, LANE), F32),
            ((total, 2 * LANE), F32),
            ((total, 2 * LANE), BF),
        ],
        [pltpu.VMEM((D, OUT_COLS), BF), pltpu.SemaphoreType.DMA((weights.count,))],
        ties,
    )


def project_back(
    d_query, d_gate, d_own, returned, squashed, mask, value_all, weights, owners, rows, ties=()
):
    total = d_query.shape[0]
    chains = total // rows

    def body(owner_ref, dq_ref, dg_ref, own_ref, back_ref, squash_ref, mask_ref, value_ref, *refs):
        ws = refs[: len(weights.arrays)]
        d_projected, keep, send, weight, semaphores = refs[len(weights.arrays) :]
        copies = weights.copies(owner_ref, ws, 0, QKV_COLS, weight, semaphores)
        for chain in range(chains):
            at = slice(chain * rows, (chain + 1) * rows)
            d_own = own_ref[at, :] + back_ref[at, :].astype(F32)
            soft = squash_ref[at, :]
            gates = soft * mask_ref[at, :]
            d_value = d_own[:, LANE:].astype(BF).astype(F32)
            lanes = lax.broadcasted_iota(jnp.int32, (rows, LANE), 1)
            d_gates = dg_ref[at, :]
            for expert in range(E):
                column = jnp.sum(
                    d_value * value_ref[at, expert * LANE : (expert + 1) * LANE],
                    axis=1,
                    keepdims=True,
                )
                d_gates = jnp.where(lanes == DH + expert, column, d_gates)
                start = (2 + expert) * LANE
                d_projected[at, start : start + LANE] = (
                    gate_column(gates, 0, expert) * d_value
                ).astype(BF)
            d_select = d_gates * mask_ref[at, :] * soft * (1.0 - soft)
            first = jnp.where(lanes < DH, dq_ref[at, :], d_select)
            d_projected[at, :LANE] = first.astype(BF)
            d_projected[at, LANE : 2 * LANE] = d_own[:, :LANE].astype(BF)
        for copy in copies:
            copy.wait()

        @pl.loop(0, chains // 2)
        def _(pair):
            out = dot_nt(d_projected[pl.ds(pair * 2 * rows, 2 * rows), :], weight[...])
            store_split(keep, send, pair, out, rows)

    arrays = (d_query, d_gate, d_own, returned, squashed, mask, value_all)
    return call(
        body,
        "project_back",
        (owners, *arrays, *weights.arrays),
        [in_scalars()] + [whole(array) for array in arrays] + weights.specs(),
        [((total, QKV_COLS), BF), ((total // 2, D), F32), ((total // 2, D), BF)],
        [pltpu.VMEM((D, QKV_COLS), BF), pltpu.SemaphoreType.DMA((weights.count,))],
        ties,
    )


def join_norm(stream, sums, gain, ties=()):
    rows = stream.shape[0]

    def body(stream_ref, keep_ref, near_ref, far_ref, gain_ref, joined, normed):
        values = (
            stream_ref[...]
            + keep_ref[...]
            + near_ref[...].astype(F32)
            + far_ref[...].astype(F32)
        )
        joined[...] = values
        scale = lax.rsqrt(jnp.mean(values * values, axis=1, keepdims=True) + EPS_NORM)
        normed[...] = (values * scale * gain_ref[...]).astype(BF)

    block = part((rows, D))
    return call(
        body,
        "join_norm",
        (stream, *sums, gain),
        [block, block, block, block, part((1, D))],
        [((rows, D), F32), ((rows, D), BF)],
        [],
        ties,
    )


def norm_back(grad_out, sums, stream, gain, ties=()):
    rows = stream.shape[0]

    def body(out_ref, keep_ref, near_ref, far_ref, stream_ref, gain_ref, grad, low, gain_grad):
        d_norm = keep_ref[...] + near_ref[...].astype(F32) + far_ref[...].astype(F32)
        values = stream_ref[...]
        scale = lax.rsqrt(jnp.mean(values * values, axis=1, keepdims=True) + EPS_NORM)
        unit = values * scale
        gain_grad[...] = jnp.sum(d_norm * unit, axis=0, keepdims=True)
        d_unit = d_norm * gain_ref[...]
        inner = jnp.mean(d_unit * unit, axis=1, keepdims=True)
        total = out_ref[...] + scale * (d_unit - unit * inner)
        grad[...] = total
        low[...] = total.astype(BF)

    block = part((rows, D))
    return call(
        body,
        "norm_back",
        (grad_out, *sums, stream, gain),
        [block] * 5 + [part((1, D))],
        [((rows, D), F32), ((rows, D), BF), ((1, D), F32)],
        [],
        ties,
    )


def grad_whole(pairs, places):
    total = pairs[0][0].shape[0]
    rows = D // places.shape[0]
    together = 2 if places.shape[0] > 1 else 1
    widths = [d_part.shape[1] for _, d_part in pairs]

    def body(place_ref, *refs):
        count = len(pairs) * together
        start = 0
        for index, width in enumerate(widths):
            lefts = refs[index * together : (index + 1) * together]
            part_ref = refs[count + index]
            turned = jnp.concatenate([left[...].T for left in lefts], axis=0)
            for first in range(0, width, 512):
                size = min(512, width - first)
                value = dot_nn(turned, part_ref[:, first : first + size])
                refs[-1][:, start + first : start + first + size] = value.astype(BF)
            start += width

    left_specs = [
        pl.BlockSpec((total, rows), lambda step, at, side=side: (0, at[together * step + side]))
        for side in range(together)
    ]
    return pl.pallas_call(
        body,
        grid_spec=pltpu.PrefetchScalarGridSpec(
            num_scalar_prefetch=1,
            grid=(places.shape[0] // together,),
            in_specs=left_specs * len(pairs)
            + [pl.BlockSpec((total, width), lambda step, at: (0, 0)) for width in widths],
            out_specs=pl.BlockSpec((together * rows, sum(widths)), lambda step, at: (step, 0)),
        ),
        out_shape=jax.ShapeDtypeStruct((D, sum(widths)), BF),
        compiler_params=pltpu.CompilerParams(vmem_limit_bytes=VMEM_LIMIT),
        cost_estimate=pl.CostEstimate(flops=1, bytes_accessed=1, transcendentals=0),
        name="grad_whole",
    )(
        places,
        *[left for left, _ in pairs for _ in range(together)],
        *[d_part for _, d_part in pairs],
    )


def add_blocks(parts, places, received, rows):
    widths = [array.shape[1] for array in parts]
    flat = [array for arrays in received for array in arrays]

    def body(*refs):
        count = len(places)
        part_refs = [refs[side * count : (side + 1) * count] for side in range(len(parts))]
        arrived = list(refs[len(parts) * count : len(parts) * count + len(flat)])
        outs = refs[len(parts) * count + len(flat) :]
        for index in range(count):
            mine = [arrived.pop(0) for _ in received[index]]
            start = 0
            for side, width in zip(part_refs, widths):
                at = slice(start, start + width)
                value = side[index][...].astype(F32)
                for ref in mine:
                    value = value + ref[:, at].astype(F32)
                outs[index][:, at] = value.astype(BF)
                start += width

    def row_blocks(width):
        return [
            pl.BlockSpec((rows, width), lambda step, place=place: (place, 0)) for place in places
        ]

    return call(
        body,
        "add_blocks",
        (*[array for array in parts for _ in places], *flat),
        [spec for width in widths for spec in row_blocks(width)] + [whole(array) for array in flat],
        [((rows, sum(widths)), BF) for _ in places],
        [],
    )


def stream_of_rows(received, owners, own_rows):
    tokens = received.shape[2]
    per_block = D // owners.shape[0] // own_rows

    def body(owner_ref, received_ref, stream, normed, gains):
        for block in range(owners.shape[0]):
            sources = [owner_ref[block] * per_block + member for member in range(per_block)]
            at = slice(block * LANE, (block + 1) * LANE)
            rows = [received_ref[source, :own_rows, :].astype(F32) for source in sources]
            stream[:, at] = jnp.concatenate(rows, axis=0).T
            pieces = [received_ref[source, own_rows:, :].astype(F32) for source in sources]
            gains[:, at] = jnp.concatenate([piece[:, :own_rows] for piece in pieces], axis=1)[:8]
        values = stream[...]
        scale = lax.rsqrt(jnp.mean(values * values, axis=1, keepdims=True) + EPS_NORM)
        normed[...] = (values * scale * gains[0:1, :]).astype(BF)

    return call(
        body,
        "stream_of_rows",
        (owners, received),
        [in_scalars(), whole(received)],
        [((tokens, D), F32), ((tokens, D), BF), ((8, D), F32)],
        [],
    )


def rows_of_stream(d_stream, gain_grads, owners, own_rows):
    tokens = d_stream.shape[0]
    per_block = D // owners.shape[0] // own_rows

    def body(owner_ref, stream_ref, *refs):
        gain_refs, out = refs[:NG], refs[NG]
        for block in range(owners.shape[0]):
            at = slice(block * LANE, (block + 1) * LANE)
            turned = stream_ref[:, at].T.astype(BF)
            gains = jnp.concatenate(
                [ref[:, at] for ref in gain_refs] + [jnp.zeros((16 - NG, LANE), F32)], axis=0
            ).astype(BF)
            for member in range(per_block):
                rows = slice(member * own_rows, (member + 1) * own_rows)
                target = owner_ref[block] * per_block + member
                out[target, :own_rows, :] = turned[rows]
                out[target, own_rows:, :] = jnp.concatenate(
                    [gains[:, rows], jnp.zeros((16, tokens - own_rows), BF)], axis=1
                )

    return call(
        body,
        "rows_of_stream",
        (owners, d_stream, *gain_grads),
        [in_scalars(), whole(d_stream)] + [whole(grad) for grad in gain_grads],
        [((owners.shape[0] * per_block, own_rows + 16, tokens), BF)],
        [],
    )[0]


def spread_blocks(values, feeder=None):
    blocks = {0: values}
    for bit in reversed(group_bits()):
        for known in list(blocks):
            blocks[known ^ bit] = swap_group(blocks[known], bit)
            if feeder is not None and bit > 1:
                blocks[known ^ bit] = feeder.tie(blocks[known ^ bit], feeder.width)
    return [blocks[index] for index in range(len(blocks))]


def merge_sums(keep, send, feeder=None):
    count = lax.axis_size("grp")
    assert count == 4
    rows = keep.shape[0] // (count // 2)
    near = swap_group(send, 1)
    blocks = {
        index: keep[index * rows : (index + 1) * rows] + near[index * rows : (index + 1) * rows].astype(F32)
        for index in range(1, count // 2)
    }
    far = swap_group(blocks[1].astype(BF), 2)
    if feeder is not None:
        far = feeder.tie(far)
    return keep, near, far


def forward_layer(
    state, attention_weights, forward_weights, owners, gains, mask, allowed, rows, feeder
):
    stream, normed_low = state
    blocks = feeder.tie(spread_blocks(normed_low, feeder))
    attention_weights = attention_weights()
    normed, queries, key_value, value_all, squashed = project(
        blocks, attention_weights, owners, mask
    )
    memory = feeder.tie(shifted(key_value, 1))
    attended, mixed, keep, send = attend(
        queries, key_value, memory, squashed, mask, allowed, attention_weights, owners, rows
    )
    stream_mid, second_low = join_norm(stream, merge_sums(keep, send, feeder), gains[0])
    blocks = feeder.tie(spread_blocks(second_low, feeder))
    forward_weights = forward_weights()
    second, hidden, slope, keep, send = feed(blocks, forward_weights, owners)
    send = feeder.tie(send)
    stream_out, next_low = join_norm(stream_mid, merge_sums(keep, send, feeder), gains[1])
    stored = (
        stream,
        normed,
        queries,
        key_value,
        memory,
        value_all,
        squashed,
        attended,
        mixed,
        stream_mid,
        second,
        hidden,
        slope,
    )
    return (stream_out, next_low), stored, (attention_weights, forward_weights)


def backward_layer(
    state,
    attention_weights,
    forward_weights,
    owners,
    gains,
    mask,
    allowed,
    stored,
    rows,
    feeder,
    ring,
    pending,
):
    (
        stream,
        normed,
        queries,
        key_value,
        memory,
        value_all,
        squashed,
        attended,
        mixed,
        stream_mid,
        second,
        hidden,
        slope,
    ) = stored
    grad_out, grad_low = state
    def tied(values):
        return feeder.tie(values) if ring else values

    def products(sums, pairs):
        pairs, near = lax.optimization_barrier((pairs, sums[1]))
        parts = [transposed_times(left, right).astype(BF) for left, right in pairs]
        return lax.optimization_barrier(((sums[0], near, sums[2]), parts))

    blocks = spread_blocks(grad_low, feeder if ring else None)
    d_out, d_pre, keep, send = feed_back(blocks, forward_weights, owners, slope)
    sums, parts = products(merge_sums(keep, send), [(second, d_pre), (d_out, hidden)])
    grad_mid, grad_mid_low, gain_forward = norm_back(grad_out, sums, stream_mid, gains[1])
    blocks = spread_blocks(grad_mid_low)
    d_branch, d_query, d_gate, d_own, d_past = attend_back(
        blocks, queries, key_value, memory, squashed, mask, allowed, attended, attention_weights, owners
    )
    returned = tied(shifted(d_past, -1))
    d_projected, keep, send = project_back(
        d_query, d_gate, d_own, returned, squashed, mask, value_all, attention_weights, owners, rows
    )
    sums = merge_sums(keep, send)
    if ring:
        sums, more = products(sums, [(normed, d_projected), (d_branch, mixed)])
        sums, pending = lax.optimization_barrier((sums, pending))
        sums = tied(sums)
        grads = [(Scatter(*parts, *more), ("up", "down", "project", "output"))]
        feeder.waiting.append(grads[0][0])
        feeder.start(2)
    else:
        pairs, near = lax.optimization_barrier(
            ([(normed, d_projected), (d_branch, mixed)], sums[1])
        )
        sums = (sums[0], near, sums[2])
        whole_grad = grad_whole(pairs, ring_places())
        sums, whole_grad = lax.optimization_barrier((sums, whole_grad))
        pending = scatter_whole(whole_grad)
        grads = [(Scatter(*parts), ("up", "down")), (None, ("project", "output"))]
        feeder.waiting.append(grads[0][0])
        feeder.start()
    grad_in, grad_in_low, gain_attention = norm_back(grad_mid, sums, stream, gains[0])
    return (grad_in, grad_in_low), grads, [gain_attention, gain_forward], pending


def scatter_whole(gradient):
    return lax.psum_scatter(gradient, "seq", scatter_dimension=0, tiled=True)


def own_columns(summed):
    count = lax.axis_size("grp")
    summed = summed.reshape(count, summed.shape[0] // count, summed.shape[1])
    return group_exchange(summed.astype(BF))


def allowed_keys(segment, memory_tail):
    positions = jnp.arange(segment.shape[1], dtype=jnp.int32)
    own_block = (segment[:, :, None] == segment[:, None, :]) & (
        positions[None, None, :] <= positions[None, :, None]
    )
    past_block = (segment[:, :, None] == 0) & (memory_tail[:, None, :] > 0)
    return jnp.concatenate([past_block, own_block], axis=2)


def adamw_update(master, gradient, first, second, factor, rate, decay):
    gradient = gradient * factor
    first_new = BETA_FIRST * first + (1.0 - BETA_FIRST) * gradient
    second_new = BETA_SECOND * second + (1.0 - BETA_SECOND) * gradient * gradient
    first_hat = first_new / (1.0 - BETA_FIRST**STEP)
    second_hat = second_new / (1.0 - BETA_SECOND**STEP)
    master_new = master - rate * (first_hat / (jnp.sqrt(second_hat) + EPS_ADAM) + decay * master)
    return (first_new, second_new, master_new)


def update_layers(factor, grads, masters, firsts, seconds):
    rows = masters[0].shape[1]
    chunk = 8 * DH

    widths = {"up": FF // H, "down": FF // H, "project": QKV_COLS, "output": OUT_COLS}
    flat = [part for parts in grads for part, _ in parts]
    found, index = [], 0
    for parts in grads:
        found.append({})
        for _, names in parts:
            start = 0
            for name in names:
                found[-1][name] = (index, start)
                start += widths[name]
            index += 1

    def body(factor_ref, *refs):
        parts = refs[: len(flat)]
        ins = refs[len(flat) : len(flat) + 6]
        outs = refs[len(flat) + 6 :]
        scale = factor_ref[0, 0]

        def apply(kind, columns, gradient):
            old = [ref[0, :, columns] for ref in ins[3 * kind : 3 * kind + 3]]
            first, second, master = adamw_update(
                old[0], gradient, old[1], old[2], scale, LR_MATRIX, DECAY
            )
            new = (master, first, second)
            for ref, values in zip(outs[3 * kind : 3 * kind + 3], new):
                ref[0, :, columns] = values

        for layer in range(L):

            @pl.when(pl.program_id(0) == layer)
            def _(layer=layer):
                def columns_of(name, member, start, width):
                    place, base = found[layer][name]
                    return parts[place][member, :, base + start : base + start + width].astype(F32)

                def heads(start):
                    return [columns_of("project", member, start, DH) for member in range(H)]

                def experts(name, start):
                    return [
                        columns_of(name, member, start + expert * LANE, DH)
                        for member in range(H)
                        for expert in range(E)
                    ]

                chunks = heads(0) + heads(LANE) + experts("project", 2 * LANE) + experts("output", 0)
                for group in range(len(chunks) // 8):
                    gradient = jnp.concatenate(chunks[8 * group : 8 * group + 8], axis=1)
                    apply(0, slice(group * chunk, (group + 1) * chunk), gradient)
                width = FF // H
                for side, name in enumerate(("up", "down")):
                    for member in range(H):
                        start = QKW + 2 * VW + side * FF + member * width
                        gradient = columns_of(name, member, 0, width)
                        apply(0, slice(start, start + width), gradient)
                selects = [
                    columns_of("project", member, DH + kind * E, E)
                    for kind in range(2)
                    for member in range(H)
                ]
                apply(1, slice(0, SELW), jnp.concatenate(selects, axis=1))

    def layer_block(array):
        return pl.BlockSpec((1,) + array.shape[1:], lambda step: (step, 0, 0))

    states = [masters[0], firsts[0], seconds[0], masters[1], firsts[1], seconds[1]]
    return pl.pallas_call(
        body,
        grid=(L,),
        in_specs=[in_scalars()]
        + [pl.BlockSpec(part.shape, lambda step: (0, 0, 0)) for part in flat]
        + [layer_block(array) for array in states],
        out_specs=[layer_block(array) for array in states],
        out_shape=[jax.ShapeDtypeStruct(array.shape, F32) for array in states],
        compiler_params=pltpu.CompilerParams(vmem_limit_bytes=VMEM_LIMIT),
        name="update_layers",
    )(factor, *flat, *states)


def all_sum(values):
    devices = lax.axis_size("seq") * lax.axis_size("grp")
    sent = jnp.broadcast_to(values[None], (devices,) + values.shape)
    return jnp.sum(
        lax.all_to_all(sent, ("seq", "grp"), split_axis=0, concat_axis=0, tiled=True), axis=0
    )


def document_weights(segment, seg_total, runs, seq_here, row_count):
    seq_count = runs.shape[0]
    device_ids = jnp.arange(seq_count, dtype=jnp.int32)[:, None]
    starts_there = runs[:, :, 0] > 0
    left_pick = jnp.max(jnp.where(starts_there & (device_ids < seq_here), device_ids, -1), axis=0)
    left_run = jnp.where(
        left_pick >= 0,
        jnp.sum(jnp.where(device_ids == left_pick, runs[:, :, 2], 0), axis=0)
        + (seq_here - 1 - left_pick) * row_count,
        0,
    )
    right_pick = jnp.min(
        jnp.where(starts_there & (device_ids > seq_here), device_ids, seq_count), axis=0
    )
    right_run = (
        jnp.sum(jnp.where(device_ids == right_pick, runs[:, :, 1], 0), axis=0)
        + (right_pick - seq_here - 1) * row_count
    )
    local_length = jnp.sum((segment[:, :, None] == segment[:, None, :]).astype(jnp.int32), axis=2)
    doc_length = (
        local_length
        + jnp.where(segment == 0, left_run[:, None], 0)
        + jnp.where(segment == seg_total[:, None], right_run[:, None], 0)
    )
    return 1.0 / doc_length.astype(F32)


def local(
    token_ids,
    target_ids,
    start_flags,
    route_ids,
    embed_table,
    layer_weights,
    router_weights,
    norm_gains,
    embed_mean,
    layer_mean,
    router_mean,
    gains_mean,
    embed_square,
    layer_square,
    router_square,
    gains_square,
):
    row_count = token_ids.shape[1]
    group_count = lax.axis_size("grp")
    own_group = lax.axis_index("grp")
    seq_count = lax.axis_size("seq")
    seq_here = lax.axis_index("seq")
    device_count = seq_count * group_count
    own_rows = embed_table.shape[0]
    positions = jnp.arange(row_count, dtype=jnp.int32)
    quarter = V // group_count

    total_abs = jnp.sum(start_flags, axis=1)
    first_start = jnp.min(jnp.where(start_flags > 0, positions[None, :], row_count), axis=1)
    last_start = jnp.max(jnp.where(start_flags > 0, positions[None, :], -1), axis=1)
    tail_count = jnp.where(total_abs > 0, row_count - last_start, row_count)
    summary = jnp.concatenate([total_abs, first_start, tail_count])
    summary = jnp.pad(summary, (0, row_count - summary.shape[0]))
    told = jnp.stack([token_ids[0], target_ids[0], summary])
    heard = lax.all_to_all(
        jnp.broadcast_to(told[None], (device_count,) + told.shape),
        ("seq", "grp"),
        split_axis=0,
        concat_axis=0,
        tiled=True,
    )
    all_ids = heard[:, 0].reshape(-1)
    heard = heard.reshape(seq_count, group_count, 3, row_count)
    runs = heard[:, 0, 2, : 3 * group_count].reshape(seq_count, 3, group_count).transpose(0, 2, 1)
    doc_count = jnp.sum(runs[:, :, 0]).astype(F32)

    relative = own_group ^ jnp.arange(group_count, dtype=jnp.int32)
    flags = jnp.take(start_flags, relative, axis=0)
    segment = jnp.cumsum(flags, axis=1, dtype=jnp.int32)
    seg_total = segment[:, -1]
    doc_weight = document_weights(
        segment, seg_total, jnp.take(runs, relative, axis=1), seq_here, row_count
    )
    targets = lax.dynamic_index_in_dim(heard[:, :, 1], seq_here, 0, keepdims=False)
    targets = jnp.take(targets, relative, axis=0)
    memory_tail = shifted((segment == seg_total[:, None]).astype(BF), 1)
    routes = jnp.take(route_ids, relative, axis=0).reshape(
        group_count, row_count, 2 * L, H, 2
    )
    routes = lax.dynamic_index_in_dim(routes, own_group, 3, keepdims=False)
    expert_ids = jnp.arange(E, dtype=jnp.int32)
    gate_all = jnp.sum((routes[..., None] == expert_ids).astype(F32), axis=-2)
    gate_all = gate_all.reshape(group_count * row_count, L, 2 * E).transpose(1, 0, 2)
    gate_all = jnp.pad(gate_all, [(0, 0), (0, 0), (DH, LANE - DH - 2 * E)])
    allowed = allowed_keys(segment, memory_tail).astype(F32)
    allowed = allowed.reshape(group_count * row_count, 2 * row_count)

    def exchanged(parts):
        swapped = exchange_parts(parts)
        return swapped.reshape(-1, swapped.shape[2])

    owners = ring_owners()
    own_scalar = own_group.astype(jnp.int32).reshape(1)
    attention_parts, forward_parts = arrange_layer(own_scalar, 0, layer_weights, router_weights)
    first = exchanged(attention_parts)
    first, forward_parts = lax.optimization_barrier((first, forward_parts))
    first_attention = Gather(first)
    first_forward = Gather(exchanged(forward_parts))
    feeder = Feed([first_attention])
    feeder.start()
    all_ids = feeder.tie(all_ids)

    looked = lookup(all_ids, embed_table).astype(BF) * D**0.5
    gate_all, looked, first_forward.flying = lax.optimization_barrier(
        (gate_all, looked, first_forward.flying)
    )
    looked = feeder.tie(looked)
    feeder.waiting.append(first_forward)
    gain_rows = norm_gains.astype(BF).T
    gain_rows = jnp.pad(gain_rows, [(0, 16 - NG), (0, row_count - own_rows)])
    sent = jnp.concatenate(
        [looked, jnp.broadcast_to(gain_rows[None], (device_count,) + gain_rows.shape)], axis=1
    )
    received = lax.all_to_all(sent, ("seq", "grp"), split_axis=0, concat_axis=0, tiled=True)
    received = feeder.tie(received)
    if seq_count > RING_LIMIT:
        stream = received[:, :own_rows].reshape(D, row_count).T.astype(F32)
        gains = received[:, own_rows : own_rows + NG, :own_rows].transpose(1, 0, 2)
        gains = gains.reshape(NG, D).astype(F32)
        state = (stream, rms_norm(stream, gains[0]).astype(BF))
    else:
        stream, normed_low, gains = stream_of_rows(received, owners, own_rows)
        state = (stream, normed_low)
    gains = gains[:NG, None, :]
    later, table_later, normed_here = lax.optimization_barrier(
        (layer_weights, embed_table, state[1])
    )
    state = (stream, normed_here)
    attention_parts, forward_parts = arrange_layer(own_scalar, 1, later, router_weights)
    second_attention = exchanged(attention_parts)
    second_forward = exchanged(forward_parts)
    table_own = exchanged(arrange_table(own_scalar, table_later))
    gathers = [
        first_attention,
        first_forward,
        Gather(second_attention),
        Gather(second_forward),
        Gather(table_own),
    ]
    feeder.waiting.extend(gathers[2:])
    layer_pieces = [
        tuple(lambda gather=gather: Weights(gather.result()) for gather in gathers[start : start + 2])
        for start in (0, 2)
    ]
    saved_layers = []
    saved_pieces = []
    for layer_index in range(L):
        state, stored, pieces = forward_layer(
            state,
            *layer_pieces[layer_index],
            owners,
            gains[2 * layer_index + 1 : 2 * layer_index + 3],
            gate_all[layer_index],
            allowed,
            row_count,
            feeder,
        )
        saved_layers.append(stored)
        saved_pieces.append(pieces)

    stream, final_low = state
    final_gain = gains[2 * L]
    final_all = jnp.concatenate(spread_blocks(final_low, feeder), axis=0)
    table_part = jnp.concatenate(gathers[4].result(), axis=0)
    logits = times_plain(final_all, table_part)
    columns = jnp.arange(logits.shape[1], dtype=jnp.int32)[None, :]
    logits = jnp.where(columns < quarter, logits, -1e30)
    hit = columns == (targets.reshape(-1) - own_group * quarter)[:, None]
    hit = hit & (columns < quarter)
    log_part = jax.nn.logsumexp(logits, axis=-1).reshape(group_count, row_count)
    target_part = jnp.sum(jnp.where(hit, logits, 0.0), axis=1).reshape(group_count, row_count)
    stats = jnp.stack([log_part, target_part], axis=1)
    others = [stats]
    for offset in range(1, group_count):
        got = swap_group(stats, offset)
        others.append(jnp.stack([got[index ^ offset] for index in range(group_count)]))
    others = jnp.stack(others)
    log_total = jax.nn.logsumexp(others[:, :, 0], axis=0)
    target_logit = jnp.sum(others[:, :, 1], axis=0)
    loss_local = jnp.sum((log_total[0] - target_logit[0]) * doc_weight[0])
    scale = (doc_weight / doc_count).reshape(-1)[:, None]
    d_logits = (jnp.exp(logits - log_total.reshape(-1)[:, None]) - hit.astype(F32)) * scale
    d_logits = d_logits.astype(BF)
    d_final = times_transposed(d_logits, table_part).reshape(group_count, row_count, D)
    keep = d_final[0::2].reshape(-1, D)
    send = d_final[1::2].reshape(-1, D).astype(BF)
    keep, send, d_logits = lax.optimization_barrier((keep, send, d_logits))
    sums = merge_sums(keep, send)
    table_grad = grad_whole([(final_all, d_logits)], ring_places())
    sums, table_grad = lax.optimization_barrier((sums, table_grad))
    table_grad = scatter_whole(table_grad)
    feeder = Feed()
    d_stream, d_stream_low, grad_final_gain = norm_back(
        jnp.zeros_like(stream), sums, stream, final_gain
    )

    state = (d_stream, d_stream_low)
    layer_grads = [None] * L
    gain_parts = [None] * L
    pending = ()
    for layer_index in reversed(range(L)):
        state, layer_grads[layer_index], gain_parts[layer_index], pending = backward_layer(
            state,
            *saved_pieces[layer_index],
            owners,
            gains[2 * layer_index : 2 * layer_index + 2],
            gate_all[layer_index],
            allowed,
            saved_layers[layer_index],
            row_count,
            feeder,
            layer_index == 0,
            pending,
        )

    gain_grads = sum(gain_parts, []) + [grad_final_gain]
    if seq_count > RING_LIMIT:
        gain_grads = jnp.concatenate(gain_grads).reshape(NG, device_count, own_rows)
        gain_grads = jnp.pad(
            gain_grads.transpose(1, 0, 2), [(0, 0), (0, 16 - NG), (0, row_count - own_rows)]
        )
        d_stream = state[0].T.reshape(device_count, own_rows, row_count)
        sent = jnp.concatenate([d_stream, gain_grads], axis=1).astype(BF)
    else:
        sent = rows_of_stream(state[0], gain_grads, owners, own_rows)
    received = lax.all_to_all(
        sent, ("seq", "grp"), split_axis=0, concat_axis=0, tiled=True
    ).astype(F32)
    received = feeder.tie(received, 2)
    embed_grad, square = spread_tokens(
        all_ids, received[:, :own_rows], own_columns(table_grad), V
    )
    embed_grad, square = feeder.tie((embed_grad, square))
    gains_grad = jnp.sum(received[:, own_rows : own_rows + NG, :own_rows], axis=0).T
    square = square[0, 0] + jnp.sum(gains_grad * gains_grad)
    layer_parts = []
    for grads in layer_grads:
        parts = []
        for member, names in grads:
            part = pending if member is None else member.result()
            square = square + jnp.sum(jnp.square(part.astype(F32)))
            part = own_columns(part)
            parts.append((part, names))
        layer_parts.append(parts)
    sums = all_sum(jnp.stack([loss_local, square]))
    loss_sum = sums[0]
    grad_norm = jnp.sqrt(sums[1])
    factor = CLIP / jnp.maximum(grad_norm, CLIP)
    embed_out = adamw_update(
        embed_table, embed_grad, embed_mean, embed_square, factor, LR_MATRIX, DECAY
    )
    updated = update_layers(
        factor.reshape(1, 1),
        layer_parts,
        (layer_weights, router_weights),
        (layer_mean, router_mean),
        (layer_square, router_square),
    )
    layer_out, router_out = [(new[1], new[2], new[0]) for new in (updated[:3], updated[3:])]
    gains_out = adamw_update(norm_gains, gains_grad, gains_mean, gains_square, factor, LR_GAIN, 0.0)
    return (
        loss_sum,
        doc_count,
        grad_norm,
        embed_out[0],
        embed_out[1],
        embed_out[2],
        layer_out[0],
        layer_out[1],
        layer_out[2],
        router_out[0],
        router_out[1],
        router_out[2],
        gains_out[0],
        gains_out[1],
        gains_out[2],
    )


def solution(mesh):
    rows = P(("seq", "grp"), None)
    layers = P(None, ("seq", "grp"), None)
    return jax.shard_map(
        local,
        mesh=mesh,
        in_specs=(
            P("grp", "seq"),
            P("grp", "seq"),
            P(None, "seq"),
            P(None, "seq", None, None),
            rows,
            layers,
            layers,
            rows,
            rows,
            layers,
            layers,
            rows,
            rows,
            layers,
            layers,
            rows,
        ),
        out_specs=(P(), P(), P()) + (rows,) * 3 + (layers,) * 6 + (rows,) * 3,
        check_vma=False,
    )
```

```python
import jax
import jax.numpy as jnp
from jax import lax
from jax.experimental import pallas as pl
from jax.experimental.pallas import tpu as pltpu
from jax.sharding import PartitionSpec as P

D = 1024
H = 4
DH = 112
E = 5
FF = 4096
V = 8000
L = 2
STEP = 10
QKW = 896
VW = 2240
SELW = 40
LANE = 128
NG = 5

EPS_NORM = 1e-05
CLIP = 0.05
LR_MATRIX = 0.06
LR_GAIN = 0.3
BETA_FIRST = 0.9
BETA_SECOND = 0.999
EPS_ADAM = 1e-08
DECAY = 0.1

QKV_COLS = (2 + E) * LANE
OUT_COLS = E * LANE
ATT_COLS = QKV_COLS + OUT_COLS
BF = jnp.bfloat16
F32 = jnp.float32


def times_plain(left_side, right_side):
    return jnp.dot(left_side, right_side, preferred_element_type=F32)


def times_transposed(left_side, right_side):
    return lax.dot_general(
        left_side, right_side, (((1,), (1,)), ((), ())), preferred_element_type=F32
    )


def transposed_times(left_side, right_side):
    return lax.dot_general(
        left_side, right_side, (((0,), (0,)), ((), ())), preferred_element_type=F32
    )


def rms_norm(values, gain_row):
    return (
        values * lax.rsqrt(jnp.mean(values * values, axis=-1, keepdims=True) + EPS_NORM) * gain_row
    )


def gelu_exact(values):
    return jax.nn.gelu(values, approximate=False)


def swap_group(values, bit):
    count = lax.axis_size("grp")
    return lax.ppermute(values, "grp", [(member, member ^ bit) for member in range(count)])


def group_bits():
    count = lax.axis_size("grp")
    return [1 << power for power in range(count.bit_length() - 1)]


def spread_rows(values):
    blocks = {0: values}
    for bit in reversed(group_bits()):
        for known in list(blocks):
            blocks[known ^ bit] = swap_group(blocks[known], bit)
    return jnp.concatenate([blocks[index] for index in range(len(blocks))], axis=0)


def merge_rows(values):
    count = lax.axis_size("grp")
    rows = values.shape[0] // count
    blocks = {index: values[index * rows : (index + 1) * rows] for index in range(count)}
    for bit in group_bits():
        away = [index for index in sorted(blocks) if index & bit]
        sent = jnp.concatenate([blocks[index].astype(BF) for index in away], axis=0)
        received = swap_group(sent, bit).astype(F32)
        blocks = {
            index ^ bit: blocks[index ^ bit] + received[place * rows : (place + 1) * rows]
            for place, index in enumerate(away)
        }
    return blocks[0]


def exchange_parts(parts):
    own = lax.axis_index("grp")
    parts = [parts[0]] + [swap_group(part, offset) for offset, part in enumerate(parts) if offset]
    return jnp.stack([lax.select_n(own ^ member, *parts) for member in range(len(parts))])


def group_exchange(values):
    count = lax.axis_size("grp")
    own = lax.axis_index("grp")
    cases = [values[member] for member in range(count)]
    parts = [lax.select_n(own ^ offset, *cases) for offset in range(count)]
    parts = [parts[0]] + [swap_group(parts[offset], offset) for offset in range(1, count)]
    return jnp.stack([lax.select_n(own ^ member, *parts) for member in range(count)])


def shifted(value, steps):
    count = lax.axis_size("seq")
    first, last = (max(0, -steps), min(count, count - steps))
    return lax.ppermute(value, "seq", [(source, source + steps) for source in range(first, last)])


RING_LIMIT = 8


def ring_order(count):
    return list(range(0, count, 2)) + list(range(count - 1, 0, -2))


def ring_pairs(count, step):
    order = ring_order(count)
    return [(order[place], order[(place + step) % count]) for place in range(count)]


def ring_place(device, count):
    return jnp.where(device % 2 == 0, device // 2, count - 1 - device // 2)


def ring_device(place, count):
    return jnp.where(2 * place < count, 2 * place, 2 * (count - 1 - place) + 1)


class Gather:
    def __init__(self, values, ring=True):
        self.count = lax.axis_size("seq")
        self.whole = None
        self.blocks = {0: values}
        self.left = self.count // 2
        if self.count > RING_LIMIT or not ring:
            self.whole = lax.all_gather(values, "seq", axis=0, tiled=True)
            self.left = 0
        self.flying = (values, values)

    def land(self):
        return self.flying

    def step(self, landed):
        ahead, behind = landed
        done = self.count // 2 - self.left + 1
        if done < self.count // 2:
            ahead = lax.ppermute(ahead, "seq", ring_pairs(self.count, 1))
            behind = lax.ppermute(behind, "seq", ring_pairs(self.count, -1))
            self.blocks[self.count - done] = ahead
            self.blocks[done] = behind
        else:
            half = ahead.shape[1] // (2 * LANE) * LANE
            ahead = lax.ppermute(ahead[:, :half], "seq", ring_pairs(self.count, 1))
            behind = lax.ppermute(behind[:, half:], "seq", ring_pairs(self.count, -1))
            self.blocks[done] = jnp.concatenate([ahead, behind], axis=1)
        self.flying = (ahead, behind)
        self.left -= 1

    def result(self):
        while self.left:
            self.step(self.flying)
        if self.whole is not None:
            return [self.whole]
        return [self.blocks[place] for place in range(len(self.blocks))]


class Scatter:
    def __init__(self, *parts):
        self.count = lax.axis_size("seq")
        self.parts, self.rows = parts, D // self.count
        self.left = self.count // 2
        self.whole = None
        if self.count > RING_LIMIT:
            joined = jnp.concatenate(self.parts, axis=1)
            self.whole = lax.psum_scatter(joined, "seq", scatter_dimension=0, tiled=True)
            self.left = 0
        self.flying = ()

    def land(self):
        return self.flying

    def step(self, landed):
        back = self.count - 1 - self.count // 2
        done = self.count // 2 - self.left
        places, received = [self.left], [landed[:1]]
        if done < back:
            places.append(self.count - back + done)
            received.append(landed[1:])
        sums = add_blocks(self.parts, places, received, self.rows)
        ahead = lax.ppermute(sums[0], "seq", ring_pairs(self.count, 1))
        behind = landed[1] if done >= back else lax.ppermute(
            sums[1], "seq", ring_pairs(self.count, -1)
        )
        self.flying = (ahead, behind)
        self.left -= 1

    def result(self):
        while self.left:
            self.step(self.flying)
        if self.whole is not None:
            return self.whole
        return add_blocks(self.parts, [0], [self.flying], self.rows)[0]


class Feed:
    def __init__(self, tasks=(), width=1):
        self.waiting = list(tasks)
        self.width = width
        self.flying = []

    def tie(self, values, width=1):
        landed = [task.land() for task in self.flying]
        values, landed = lax.optimization_barrier((values, landed))
        for task, arrived in zip(self.flying, landed):
            task.flying = tuple(arrived)
        self.start(width)
        return values

    def start(self, width=1):
        self.waiting = [task for task in self.waiting if task.left]
        self.flying = self.waiting[:width]
        for task in self.flying:
            task.step(task.flying)


def ring_owners():
    count = lax.axis_size("seq")
    if count > RING_LIMIT:
        return jnp.zeros((1,), jnp.int32)
    here = ring_place(lax.axis_index("seq"), count)
    return ring_device(lax.rem(jnp.arange(count, dtype=jnp.int32) + here, count), count)


def ring_places():
    count = lax.axis_size("seq")
    if count > RING_LIMIT:
        return jnp.zeros((1,), jnp.int32)
    here = ring_place(lax.axis_index("seq"), count)
    devices = jnp.arange(count, dtype=jnp.int32)
    return lax.rem(ring_place(devices, count) - here + count, count)


def pick_blocks(values, order):
    if order.shape[0] == 1:
        return values
    shape = values.shape
    return jnp.take(values.reshape((order.shape[0], -1) + shape[1:]), order, axis=0).reshape(shape)


def to_ring(values):
    return pick_blocks(values, ring_owners())


def from_ring(values):
    return pick_blocks(values, ring_places())


def after(values, *others):
    return lax.optimization_barrier((values, *others))[0]


def pad_lanes(values):
    return jnp.pad(values, [(0, 0)] * (values.ndim - 1) + [(0, LANE - values.shape[-1])])


def choose(own, offset, cases):
    member = own ^ offset
    value = cases[0]
    for index in range(1, len(cases)):
        value = jnp.where(member == index, cases[index], value)
    return value


def arrange_layer(own, layer, weights, routers):
    rows, columns = weights.shape[1:]
    members = H

    def body(own_ref, weight_ref, router_ref, *outs):
        here = own_ref[0]

        def lanes(pieces):
            filled = sum(piece.shape[1] for piece in pieces)
            zeros = [jnp.zeros((rows, LANE - filled), F32)]
            return jnp.concatenate(pieces + zeros, axis=1).astype(BF)

        def chunk(start):
            return weight_ref[0, :, start : start + DH]

        tiles = []
        for member in range(members):
            picked = [
                router_ref[0, :, (kind * H + member) * E : (kind * H + member + 1) * E]
                for kind in range(2)
            ]
            group = [lanes([chunk(member * DH)] + picked), lanes([chunk((H + member) * DH)])]
            for base in (QKW, QKW + VW):
                for expert in range(E):
                    group.append(lanes([chunk(base + (member * E + expert) * DH)]))
            tiles.append(group)
        base = QKW + 2 * VW
        width = FF // members
        for offset in range(members):
            for index in range(len(tiles[0])):
                outs[offset][:, index * LANE : (index + 1) * LANE] = choose(
                    here, offset, [group[index] for group in tiles]
                )
            for side in range(2):
                start = base + side * FF
                outs[members + offset][:, side * width : (side + 1) * width] = choose(
                    here,
                    offset,
                    [
                        weight_ref[0, :, start + member * width : start + (member + 1) * width]
                        for member in range(members)
                    ],
                ).astype(BF)

    shapes = [(rows, ATT_COLS)] * members + [(rows, 2 * FF // members)] * members
    parts = pl.pallas_call(
        body,
        grid=(1,),
        in_specs=[
            in_scalars(),
            pl.BlockSpec((1, rows, columns), lambda step: (layer, 0, 0)),
            pl.BlockSpec((1, rows, SELW), lambda step: (layer, 0, 0)),
        ],
        out_specs=[part(shape) for shape in shapes],
        out_shape=[jax.ShapeDtypeStruct(shape, BF) for shape in shapes],
        compiler_params=pltpu.CompilerParams(vmem_limit_bytes=VMEM_LIMIT),
        cost_estimate=pl.CostEstimate(flops=1, bytes_accessed=1, transcendentals=0),
        name="arrange_layer",
    )(own, weights, routers)
    return parts[:members], parts[members:]


def arrange_table(own, table):
    rows, width = table.shape
    quarter = width // H
    padded = -(-quarter // LANE) * LANE

    def body(own_ref, table_ref, *outs):
        zeros = jnp.zeros((rows, padded - quarter), F32)
        cases = [
            jnp.concatenate([table_ref[:, member * quarter : (member + 1) * quarter], zeros], axis=1)
            for member in range(H)
        ]
        for offset in range(H):
            outs[offset][...] = choose(own_ref[0], offset, cases).astype(BF)

    return call(
        body,
        "arrange_table",
        (own, table),
        [in_scalars(), whole(table)],
        [((rows, padded), BF) for _ in range(H)],
        [],
    )


def lookup_body(ids_ref, table_ref, out_ref, by_token, picked):
    rows = table_ref.shape[0]
    width = table_ref.shape[1]
    for start in range(0, width, LANE):
        end = min(start + LANE, width)
        by_token[start:end, :rows] = table_ref[:, start:end].T

    @pl.loop(0, out_ref.shape[0])
    def _(device):
        base = device * LANE

        for token in range(LANE):
            picked[pl.ds(token, 1), :] = by_token[pl.ds(ids_ref[base + token], 1), :]
        out_ref[device] = picked[...].T[:rows]


def lookup(ids, table):
    rows, width = table.shape
    devices = ids.shape[0] // LANE
    return pl.pallas_call(
        lookup_body,
        grid_spec=pltpu.PrefetchScalarGridSpec(
            num_scalar_prefetch=1,
            grid=(1,),
            in_specs=[pl.BlockSpec((rows, width), lambda i, ids: (0, 0))],
            out_specs=pl.BlockSpec((devices, rows, LANE), lambda i, ids: (0, 0, 0)),
            scratch_shapes=[pltpu.VMEM((width, LANE), F32), pltpu.VMEM((LANE, LANE), F32)],
        ),
        out_shape=jax.ShapeDtypeStruct((devices, rows, LANE), F32),
        compiler_params=pltpu.CompilerParams(vmem_limit_bytes=48 * 1024 * 1024),
        name="lookup",
    )(ids, table)


ACCUMULATORS = 4


def spread_body(ids_ref, grad_ref, table_ref, out_ref, square_ref, *scratch):
    rows, width = out_ref.shape
    members = table_ref.shape[0]
    totals, picked = scratch[:-1], scratch[-1]
    for total in totals:
        total[...] = jnp.zeros_like(total)

    @pl.loop(0, grad_ref.shape[0])
    def _(device):
        base = device * LANE
        picked[:, :rows] = grad_ref[device].T

        for step in range(LANE // ACCUMULATORS):
            for which, total in enumerate(totals):
                token = step * ACCUMULATORS + which
                place = pl.ds(ids_ref[base + token], 1)
                total[place, :] += picked[pl.ds(token, 1), :]

    for start in range(0, width, LANE):
        end = min(start + LANE, width)
        found = sum(total[start:end, :] for total in totals).T[:rows]
        out_ref[:, start:end] = found * D**0.5
    quarter = width // members
    table = jnp.concatenate([table_ref[member][:, :quarter] for member in range(members)], axis=1)
    total = out_ref[...] + table.astype(F32)
    out_ref[...] = total
    square_ref[0, 0] = jnp.sum(total * total)


def spread_tokens(ids, grads, table_parts, width):
    devices, rows, _ = grads.shape
    return pl.pallas_call(
        spread_body,
        grid_spec=pltpu.PrefetchScalarGridSpec(
            num_scalar_prefetch=1,
            grid=(1,),
            in_specs=[
                pl.BlockSpec((devices, rows, LANE), lambda i, ids: (0, 0, 0)),
                pl.BlockSpec(table_parts.shape, lambda i, ids: (0, 0, 0)),
            ],
            out_specs=[
                pl.BlockSpec((rows, width), lambda i, ids: (0, 0)),
                pl.BlockSpec(memory_space=pltpu.SMEM),
            ],
            scratch_shapes=[pltpu.VMEM((width, LANE), F32) for _ in range(ACCUMULATORS)]
            + [pltpu.VMEM((LANE, LANE), F32)],
        ),
        out_shape=[
            jax.ShapeDtypeStruct((rows, width), F32),
            jax.ShapeDtypeStruct((1, 1), F32),
        ],
        compiler_params=pltpu.CompilerParams(vmem_limit_bytes=48 * 1024 * 1024),
        name="spread",
    )(ids, grads, table_parts)


VMEM_LIMIT = 56 * 1024 * 1024
SCALE = DH ** (-0.5)


def whole(array):
    return pl.BlockSpec(array.shape, lambda step: (0,) * array.ndim)


def part(shape):
    return pl.BlockSpec(shape, lambda step: (0,) * len(shape))


def in_scalars():
    return pl.BlockSpec(memory_space=pltpu.SMEM)


def anywhere():
    return pl.BlockSpec(memory_space=pl.ANY)


def call(body, name, inputs, specs, outputs, scratch, ties=()):
    ties = tuple(ties)

    def wrapped(*refs):
        count = len(inputs)
        body(*refs[:count], *refs[count + len(ties) :])

    return pl.pallas_call(
        wrapped,
        grid=(1,),
        in_specs=list(specs) + [anywhere()] * len(ties),
        out_specs=[part(shape) for shape, _ in outputs],
        out_shape=[jax.ShapeDtypeStruct(shape, kind) for shape, kind in outputs],
        scratch_shapes=scratch,
        compiler_params=pltpu.CompilerParams(vmem_limit_bytes=VMEM_LIMIT),
        cost_estimate=pl.CostEstimate(flops=1, bytes_accessed=1, transcendentals=0),
        name=name,
    )(*inputs, *ties)


class Weights:
    def __init__(self, arrays, base=0):
        self.arrays, self.base = list(arrays), base
        self.natural = len(self.arrays) == 1
        self.count = ring_owners().shape[0] if self.natural else len(self.arrays)

    def specs(self):
        return [anywhere() for _ in self.arrays]

    def copies(self, owners, refs, start, width, target, semaphores):
        copies = []
        rows = D // self.count
        columns = pl.ds(self.base + start, width)
        for index in range(self.count):
            if not self.natural:
                source = refs[index].at[:, columns]
            elif self.count == 1:
                source = refs[0].at[:, columns]
            else:
                place = pl.multiple_of(owners[index] * rows, rows)
                source = refs[0].at[pl.ds(place, rows), columns]
            copy = pltpu.make_async_copy(
                source, target.at[pl.ds(index * rows, rows)], semaphores.at[index]
            )
            copy.start()
            copies.append(copy)
        return copies


def gate_column(gates, kind, expert):
    place = DH + kind * E + expert
    return gates[:, place : place + 1]


def expert_lanes(values, expert):
    return values[:, expert * LANE : (expert + 1) * LANE]


def dot_nn(left, right):
    return lax.dot_general(left, right, (((1,), (0,)), ((), ())), preferred_element_type=F32)


def dot_nt(left, right):
    return lax.dot_general(left, right, (((1,), (1,)), ((), ())), preferred_element_type=F32)


def dot_tn(left, right):
    return lax.dot_general(left, right, (((0,), (0,)), ((), ())), preferred_element_type=F32)


def store_split(keep, send, pair, values, rows):
    keep[pl.ds(pair * rows, rows), :] = values[:rows]
    send[pl.ds(pair * rows, rows), :] = values[rows:].astype(BF)


def project(blocks, weights, owners, mask, ties=()):
    chains, rows = len(blocks), blocks[0].shape[0]
    total = chains * rows
    arrays = len(weights.arrays)

    def body(owner_ref, *refs):
        xs, ws, mask_ref = refs[:chains], refs[chains : chains + arrays], refs[chains + arrays]
        normed, queries, key_value, value_all, squashed, weight, semaphores = refs[
            chains + arrays + 1 :
        ]
        copies = weights.copies(owner_ref, ws, 0, QKV_COLS, weight, semaphores)
        for chain in range(chains):
            normed[chain * rows : (chain + 1) * rows, :] = xs[chain][...]
        for copy in copies:
            copy.wait()

        @pl.loop(0, chains // 2)
        def _(pair):
            at = pl.ds(pair * 2 * rows, 2 * rows)
            projected = dot_nn(normed[at, :], weight[...])
            first = projected[:, :LANE]
            lanes = lax.broadcasted_iota(jnp.int32, first.shape, 1)
            queries[at, :] = jnp.where(lanes < DH, first, 0.0).astype(BF)
            soft = jax.nn.sigmoid(first)
            squashed[at, :] = soft
            gates = soft * mask_ref[at, :]
            values = projected[:, 2 * LANE :]
            value_all[at, :] = values
            mixed = sum(
                gate_column(gates, 0, expert) * expert_lanes(values, expert) for expert in range(E)
            )
            key_value[at, :LANE] = projected[:, LANE : 2 * LANE].astype(BF)
            key_value[at, LANE:] = mixed.astype(BF)

    return call(
        body,
        "project",
        (owners, *blocks, *weights.arrays, mask),
        [in_scalars()] + [whole(block) for block in blocks] + weights.specs() + [whole(mask)],
        [
            ((total, D), BF),
            ((total, LANE), BF),
            ((total, 2 * LANE), BF),
            ((total, E * LANE), F32),
            ((total, LANE), F32),
        ],
        [pltpu.VMEM((D, QKV_COLS), BF), pltpu.SemaphoreType.DMA((weights.count,))],
        ties,
    )


def probabilities(queries, keys, allowed):
    scores = jnp.where(allowed > 0, dot_nt(queries, keys) * SCALE, -1e30)
    raised = jnp.exp(scores - jnp.max(scores, axis=1, keepdims=True))
    return raised / jnp.sum(raised, axis=1, keepdims=True)


def attend(queries, key_value, memory, squashed, mask, allowed, weights, owners, rows, ties=()):
    total = queries.shape[0]
    chains = total // rows

    def body(owner_ref, q_ref, own_ref, past_ref, squash_ref, mask_ref, allow_ref, *refs):
        ws = refs[: len(weights.arrays)]
        attended, mixed, keep, send, weight, semaphores = refs[len(weights.arrays) :]
        copies = weights.copies(owner_ref, ws, QKV_COLS, OUT_COLS, weight, semaphores)
        for chain in range(chains):
            at = slice(chain * rows, (chain + 1) * rows)
            keys = jnp.concatenate([past_ref[at, :LANE], own_ref[at, :LANE]], axis=0)
            values = jnp.concatenate([past_ref[at, LANE:], own_ref[at, LANE:]], axis=0)
            soft = probabilities(q_ref[at, :], keys, allow_ref[at, :])
            got = dot_nn(soft.astype(BF), values)
            attended[at, :] = got
            gates = squash_ref[at, :] * mask_ref[at, :]
            for expert in range(E):
                mixed[at, expert * LANE : (expert + 1) * LANE] = (
                    gate_column(gates, 1, expert) * got
                ).astype(BF)
        for copy in copies:
            copy.wait()

        @pl.loop(0, chains // 2)
        def _(pair):
            out = dot_nt(mixed[pl.ds(pair * 2 * rows, 2 * rows), :], weight[...])
            store_split(keep, send, pair, out, rows)

    return call(
        body,
        "attend",
        (owners, queries, key_value, memory, squashed, mask, allowed, *weights.arrays),
        [in_scalars()]
        + [whole(array) for array in (queries, key_value, memory, squashed, mask, allowed)]
        + weights.specs(),
        [
            ((total, LANE), F32),
            ((total, E * LANE), BF),
            ((total // 2, D), F32),
            ((total // 2, D), BF),
        ],
        [pltpu.VMEM((D, OUT_COLS), BF), pltpu.SemaphoreType.DMA((weights.count,))],
        ties,
    )


def feed(blocks, weights, owners, ties=()):
    chains, rows = len(blocks), blocks[0].shape[0]
    total = chains * rows
    width = FF // H
    count, arrays = weights.count, len(weights.arrays)

    def body(owner_ref, *refs):
        xs, ws = refs[:chains], refs[chains : chains + arrays]
        second, hidden, slope, keep, send, up, down, up_sems, down_sems = refs[
            chains + arrays :
        ]
        up_copies = weights.copies(owner_ref, ws, 0, width, up, up_sems)
        down_copies = weights.copies(owner_ref, ws, width, width, down, down_sems)
        for chain in range(chains):
            second[chain * rows : (chain + 1) * rows, :] = xs[chain][...]
        for copy in up_copies:
            copy.wait()

        @pl.loop(0, chains // 2)
        def _(pair):
            at = pl.ds(pair * 2 * rows, 2 * rows)
            pre = dot_nn(second[at, :], up[...])
            rising = 0.5 * (1.0 + lax.erf(pre * 0.5**0.5))
            hidden[at, :] = (pre * rising).astype(BF)
            slope[at, :] = rising + pre * jnp.exp(-0.5 * pre * pre) * 0.3989422804014327

        for copy in down_copies:
            copy.wait()

        @pl.loop(0, chains // 2)
        def _(pair):
            out = dot_nt(hidden[pl.ds(pair * 2 * rows, 2 * rows), :], down[...])
            store_split(keep, send, pair, out, rows)

    return call(
        body,
        "feed",
        (owners, *blocks, *weights.arrays),
        [in_scalars()] + [whole(block) for block in blocks] + weights.specs(),
        [
            ((total, D), BF),
            ((total, width), BF),
            ((total, width), F32),
            ((total // 2, D), F32),
            ((total // 2, D), BF),
        ],
        [pltpu.VMEM((D, width), BF)] * 2 + [pltpu.SemaphoreType.DMA((count,))] * 2,
        ties,
    )


def feed_back(blocks, weights, owners, slope, ties=()):
    chains, rows = len(blocks), blocks[0].shape[0]
    total = chains * rows
    width = FF // H
    count, arrays = weights.count, len(weights.arrays)

    def body(owner_ref, *refs):
        ds, ws = refs[:chains], refs[chains : chains + arrays]
        slope_ref, d_out, d_pre, keep, send, up, down, up_sems, down_sems = refs[
            chains + arrays :
        ]
        down_copies = weights.copies(owner_ref, ws, width, width, down, down_sems)
        up_copies = weights.copies(owner_ref, ws, 0, width, up, up_sems)
        for chain in range(chains):
            d_out[chain * rows : (chain + 1) * rows, :] = ds[chain][...]
        for copy in down_copies:
            copy.wait()

        @pl.loop(0, chains // 2)
        def _(pair):
            at = pl.ds(pair * 2 * rows, 2 * rows)
            d_pre[at, :] = (dot_nn(d_out[at, :], down[...]) * slope_ref[at, :]).astype(BF)

        for copy in up_copies:
            copy.wait()

        @pl.loop(0, chains // 2)
        def _(pair):
            out = dot_nt(d_pre[pl.ds(pair * 2 * rows, 2 * rows), :], up[...])
            store_split(keep, send, pair, out, rows)

    return call(
        body,
        "feed_back",
        (owners, *blocks, *weights.arrays, slope),
        [in_scalars()] + [whole(block) for block in blocks] + weights.specs() + [whole(slope)],
        [
            ((total, D), BF),
            ((total, width), BF),
            ((total // 2, D), F32),
            ((total // 2, D), BF),
        ],
        [pltpu.VMEM((D, width), BF)] * 2 + [pltpu.SemaphoreType.DMA((count,))] * 2,
        ties,
    )


def attend_back(
    blocks, queries, key_value, memory, squashed, mask, allowed, attended, weights, owners, ties=()
):
    chains, rows = len(blocks), blocks[0].shape[0]
    total = chains * rows
    count = len(weights.arrays)

    def body(owner_ref, *refs):
        ds, refs = refs[:chains], refs[chains:]
        q_ref, own_ref, past_ref, squash_ref, mask_ref, allow_ref, att_ref = refs[:7]
        ws, refs = refs[7 : 7 + count], refs[7 + count :]
        d_branch, d_query, d_gate, d_own, d_past, weight, semaphores = refs
        copies = weights.copies(owner_ref, ws, QKV_COLS, OUT_COLS, weight, semaphores)
        for chain in range(chains):
            d_branch[chain * rows : (chain + 1) * rows, :] = ds[chain][...]
        for copy in copies:
            copy.wait()
        for pair in range(chains // 2):
            pair_mixed = dot_nn(
                d_branch[pair * 2 * rows : (pair + 1) * 2 * rows, :], weight[...]
            ).astype(BF)
            for side in range(2):
                chain = pair * 2 + side
                at = slice(chain * rows, (chain + 1) * rows)
                d_mixed = pair_mixed[side * rows : (side + 1) * rows].astype(F32)
                gates = squash_ref[at, :] * mask_ref[at, :]
                d_att = sum(
                    gate_column(gates, 1, expert) * expert_lanes(d_mixed, expert)
                    for expert in range(E)
                ).astype(BF)
                got = att_ref[at, :]
                lanes = lax.broadcasted_iota(jnp.int32, (rows, LANE), 1)
                d_gates = jnp.zeros((rows, LANE), F32)
                for expert in range(E):
                    column = jnp.sum(expert_lanes(d_mixed, expert) * got, axis=1, keepdims=True)
                    d_gates = jnp.where(lanes == DH + E + expert, column, d_gates)
                d_gate[at, :] = d_gates
                keys = jnp.concatenate([past_ref[at, :LANE], own_ref[at, :LANE]], axis=0)
                values = jnp.concatenate([past_ref[at, LANE:], own_ref[at, LANE:]], axis=0)
                query = q_ref[at, :]
                soft = probabilities(query, keys, allow_ref[at, :])
                d_soft = dot_nt(d_att, values)
                delta = jnp.sum(soft * d_soft, axis=1, keepdims=True)
                d_scores = (soft * (d_soft - delta)).astype(BF)
                d_query[at, :] = dot_nn(d_scores, keys) * SCALE
                d_keys = dot_tn(d_scores, query) * SCALE
                d_values = dot_tn(soft.astype(BF), d_att)
                d_past[at, :LANE] = d_keys[:rows].astype(BF)
                d_past[at, LANE:] = d_values[:rows].astype(BF)
                d_own[at, :LANE] = d_keys[rows:]
                d_own[at, LANE:] = d_values[rows:]

    arrays = (queries, key_value, memory, squashed, mask, allowed, attended)
    return call(
        body,
        "attend_back",
        (owners, *blocks, *arrays, *weights.arrays),
        [in_scalars()]
        + [whole(block) for block in blocks]
        + [whole(array) for array in arrays]
        + weights.specs(),
        [
            ((total, D), BF),
            ((total, LANE), F32),
            ((total, LANE), F32),
            ((total, 2 * LANE), F32),
            ((total, 2 * LANE), BF),
        ],
        [pltpu.VMEM((D, OUT_COLS), BF), pltpu.SemaphoreType.DMA((weights.count,))],
        ties,
    )


def project_back(
    d_query, d_gate, d_own, returned, squashed, mask, value_all, weights, owners, rows, ties=()
):
    total = d_query.shape[0]
    chains = total // rows

    def body(owner_ref, dq_ref, dg_ref, own_ref, back_ref, squash_ref, mask_ref, value_ref, *refs):
        ws = refs[: len(weights.arrays)]
        d_projected, keep, send, weight, semaphores = refs[len(weights.arrays) :]
        copies = weights.copies(owner_ref, ws, 0, QKV_COLS, weight, semaphores)
        for chain in range(chains):
            at = slice(chain * rows, (chain + 1) * rows)
            d_own = own_ref[at, :] + back_ref[at, :].astype(F32)
            soft = squash_ref[at, :]
            gates = soft * mask_ref[at, :]
            d_value = d_own[:, LANE:].astype(BF).astype(F32)
            lanes = lax.broadcasted_iota(jnp.int32, (rows, LANE), 1)
            d_gates = dg_ref[at, :]
            for expert in range(E):
                column = jnp.sum(
                    d_value * value_ref[at, expert * LANE : (expert + 1) * LANE],
                    axis=1,
                    keepdims=True,
                )
                d_gates = jnp.where(lanes == DH + expert, column, d_gates)
                start = (2 + expert) * LANE
                d_projected[at, start : start + LANE] = (
                    gate_column(gates, 0, expert) * d_value
                ).astype(BF)
            d_select = d_gates * mask_ref[at, :] * soft * (1.0 - soft)
            first = jnp.where(lanes < DH, dq_ref[at, :], d_select)
            d_projected[at, :LANE] = first.astype(BF)
            d_projected[at, LANE : 2 * LANE] = d_own[:, :LANE].astype(BF)
        for copy in copies:
            copy.wait()

        @pl.loop(0, chains // 2)
        def _(pair):
            out = dot_nt(d_projected[pl.ds(pair * 2 * rows, 2 * rows), :], weight[...])
            store_split(keep, send, pair, out, rows)

    arrays = (d_query, d_gate, d_own, returned, squashed, mask, value_all)
    return call(
        body,
        "project_back",
        (owners, *arrays, *weights.arrays),
        [in_scalars()] + [whole(array) for array in arrays] + weights.specs(),
        [((total, QKV_COLS), BF), ((total // 2, D), F32), ((total // 2, D), BF)],
        [pltpu.VMEM((D, QKV_COLS), BF), pltpu.SemaphoreType.DMA((weights.count,))],
        ties,
    )


def join_norm(stream, sums, gain, ties=()):
    rows = stream.shape[0]

    def body(stream_ref, keep_ref, near_ref, far_ref, gain_ref, joined, normed):
        values = (
            stream_ref[...]
            + keep_ref[...]
            + near_ref[...].astype(F32)
            + far_ref[...].astype(F32)
        )
        joined[...] = values
        scale = lax.rsqrt(jnp.mean(values * values, axis=1, keepdims=True) + EPS_NORM)
        normed[...] = (values * scale * gain_ref[...]).astype(BF)

    block = part((rows, D))
    return call(
        body,
        "join_norm",
        (stream, *sums, gain),
        [block, block, block, block, part((1, D))],
        [((rows, D), F32), ((rows, D), BF)],
        [],
        ties,
    )


def norm_back(grad_out, sums, stream, gain, ties=()):
    rows = stream.shape[0]

    def body(out_ref, keep_ref, near_ref, far_ref, stream_ref, gain_ref, grad, low, gain_grad):
        d_norm = keep_ref[...] + near_ref[...].astype(F32) + far_ref[...].astype(F32)
        values = stream_ref[...]
        scale = lax.rsqrt(jnp.mean(values * values, axis=1, keepdims=True) + EPS_NORM)
        unit = values * scale
        gain_grad[...] = jnp.sum(d_norm * unit, axis=0, keepdims=True)
        d_unit = d_norm * gain_ref[...]
        inner = jnp.mean(d_unit * unit, axis=1, keepdims=True)
        total = out_ref[...] + scale * (d_unit - unit * inner)
        grad[...] = total
        low[...] = total.astype(BF)

    block = part((rows, D))
    return call(
        body,
        "norm_back",
        (grad_out, *sums, stream, gain),
        [block] * 5 + [part((1, D))],
        [((rows, D), F32), ((rows, D), BF), ((1, D), F32)],
        [],
        ties,
    )


def grad_whole(pairs, places):
    total = pairs[0][0].shape[0]
    rows = D // places.shape[0]
    together = 2 if places.shape[0] > 1 else 1
    widths = [d_part.shape[1] for _, d_part in pairs]

    def body(place_ref, *refs):
        count = len(pairs) * together
        start = 0
        for index, width in enumerate(widths):
            lefts = refs[index * together : (index + 1) * together]
            part_ref = refs[count + index]
            turned = jnp.concatenate([left[...].T for left in lefts], axis=0)
            for first in range(0, width, 512):
                size = min(512, width - first)
                value = dot_nn(turned, part_ref[:, first : first + size])
                refs[-1][:, start + first : start + first + size] = value.astype(BF)
            start += width

    left_specs = [
        pl.BlockSpec((total, rows), lambda step, at, side=side: (0, at[together * step + side]))
        for side in range(together)
    ]
    return pl.pallas_call(
        body,
        grid_spec=pltpu.PrefetchScalarGridSpec(
            num_scalar_prefetch=1,
            grid=(places.shape[0] // together,),
            in_specs=left_specs * len(pairs)
            + [pl.BlockSpec((total, width), lambda step, at: (0, 0)) for width in widths],
            out_specs=pl.BlockSpec((together * rows, sum(widths)), lambda step, at: (step, 0)),
        ),
        out_shape=jax.ShapeDtypeStruct((D, sum(widths)), BF),
        compiler_params=pltpu.CompilerParams(vmem_limit_bytes=VMEM_LIMIT),
        cost_estimate=pl.CostEstimate(flops=1, bytes_accessed=1, transcendentals=0),
        name="grad_whole",
    )(
        places,
        *[left for left, _ in pairs for _ in range(together)],
        *[d_part for _, d_part in pairs],
    )


def add_blocks(parts, places, received, rows):
    widths = [array.shape[1] for array in parts]
    flat = [array for arrays in received for array in arrays]

    def body(*refs):
        count = len(places)
        part_refs = [refs[side * count : (side + 1) * count] for side in range(len(parts))]
        arrived = list(refs[len(parts) * count : len(parts) * count + len(flat)])
        outs = refs[len(parts) * count + len(flat) :]
        for index in range(count):
            mine = [arrived.pop(0) for _ in received[index]]
            start = 0
            for side, width in zip(part_refs, widths):
                at = slice(start, start + width)
                value = side[index][...].astype(F32)
                for ref in mine:
                    value = value + ref[:, at].astype(F32)
                outs[index][:, at] = value.astype(BF)
                start += width

    def row_blocks(width):
        return [
            pl.BlockSpec((rows, width), lambda step, place=place: (place, 0)) for place in places
        ]

    return call(
        body,
        "add_blocks",
        (*[array for array in parts for _ in places], *flat),
        [spec for width in widths for spec in row_blocks(width)] + [whole(array) for array in flat],
        [((rows, sum(widths)), BF) for _ in places],
        [],
    )


def stream_of_rows(received, owners, own_rows):
    tokens = received.shape[2]
    per_block = D // owners.shape[0] // own_rows

    def body(owner_ref, received_ref, stream, normed, gains):
        for block in range(owners.shape[0]):
            sources = [owner_ref[block] * per_block + member for member in range(per_block)]
            at = slice(block * LANE, (block + 1) * LANE)
            rows = [received_ref[source, :own_rows, :].astype(F32) for source in sources]
            stream[:, at] = jnp.concatenate(rows, axis=0).T
            pieces = [received_ref[source, own_rows:, :].astype(F32) for source in sources]
            gains[:, at] = jnp.concatenate([piece[:, :own_rows] for piece in pieces], axis=1)[:8]
        values = stream[...]
        scale = lax.rsqrt(jnp.mean(values * values, axis=1, keepdims=True) + EPS_NORM)
        normed[...] = (values * scale * gains[0:1, :]).astype(BF)

    return call(
        body,
        "stream_of_rows",
        (owners, received),
        [in_scalars(), whole(received)],
        [((tokens, D), F32), ((tokens, D), BF), ((8, D), F32)],
        [],
    )


def rows_of_stream(d_stream, gain_grads, owners, own_rows):
    tokens = d_stream.shape[0]
    per_block = D // owners.shape[0] // own_rows

    def body(owner_ref, stream_ref, *refs):
        gain_refs, out = refs[:NG], refs[NG]
        for block in range(owners.shape[0]):
            at = slice(block * LANE, (block + 1) * LANE)
            turned = stream_ref[:, at].T.astype(BF)
            gains = jnp.concatenate(
                [ref[:, at] for ref in gain_refs] + [jnp.zeros((16 - NG, LANE), F32)], axis=0
            ).astype(BF)
            for member in range(per_block):
                rows = slice(member * own_rows, (member + 1) * own_rows)
                target = owner_ref[block] * per_block + member
                out[target, :own_rows, :] = turned[rows]
                out[target, own_rows:, :] = jnp.concatenate(
                    [gains[:, rows], jnp.zeros((16, tokens - own_rows), BF)], axis=1
                )

    return call(
        body,
        "rows_of_stream",
        (owners, d_stream, *gain_grads),
        [in_scalars(), whole(d_stream)] + [whole(grad) for grad in gain_grads],
        [((owners.shape[0] * per_block, own_rows + 16, tokens), BF)],
        [],
    )[0]


def spread_blocks(values, feeder=None):
    blocks = {0: values}
    for bit in reversed(group_bits()):
        for known in list(blocks):
            blocks[known ^ bit] = swap_group(blocks[known], bit)
            if feeder is not None and bit > 1:
                blocks[known ^ bit] = feeder.tie(blocks[known ^ bit], feeder.width)
    return [blocks[index] for index in range(len(blocks))]


def merge_sums(keep, send, feeder=None):
    count = lax.axis_size("grp")
    assert count == 4
    rows = keep.shape[0] // (count // 2)
    near = swap_group(send, 1)
    blocks = {
        index: keep[index * rows : (index + 1) * rows] + near[index * rows : (index + 1) * rows].astype(F32)
        for index in range(1, count // 2)
    }
    far = swap_group(blocks[1].astype(BF), 2)
    if feeder is not None:
        far = feeder.tie(far)
    return keep, near, far


def forward_layer(
    state, attention_weights, forward_weights, owners, gains, mask, allowed, rows, feeder
):
    stream, normed_low = state
    blocks = feeder.tie(spread_blocks(normed_low, feeder))
    attention_weights = attention_weights()
    normed, queries, key_value, value_all, squashed = project(
        blocks, attention_weights, owners, mask
    )
    memory = feeder.tie(shifted(key_value, 1))
    attended, mixed, keep, send = attend(
        queries, key_value, memory, squashed, mask, allowed, attention_weights, owners, rows
    )
    stream_mid, second_low = join_norm(stream, merge_sums(keep, send, feeder), gains[0])
    blocks = feeder.tie(spread_blocks(second_low, feeder))
    forward_weights = forward_weights()
    second, hidden, slope, keep, send = feed(blocks, forward_weights, owners)
    send = feeder.tie(send)
    stream_out, next_low = join_norm(stream_mid, merge_sums(keep, send, feeder), gains[1])
    stored = (
        stream,
        normed,
        queries,
        key_value,
        memory,
        value_all,
        squashed,
        attended,
        mixed,
        stream_mid,
        second,
        hidden,
        slope,
    )
    return (stream_out, next_low), stored, (attention_weights, forward_weights)


def backward_layer(
    state,
    attention_weights,
    forward_weights,
    owners,
    gains,
    mask,
    allowed,
    stored,
    rows,
    feeder,
    ring,
    pending,
):
    (
        stream,
        normed,
        queries,
        key_value,
        memory,
        value_all,
        squashed,
        attended,
        mixed,
        stream_mid,
        second,
        hidden,
        slope,
    ) = stored
    grad_out, grad_low = state
    def tied(values):
        return feeder.tie(values) if ring else values

    def products(sums, pairs):
        pairs, near = lax.optimization_barrier((pairs, sums[1]))
        parts = [transposed_times(left, right).astype(BF) for left, right in pairs]
        return lax.optimization_barrier(((sums[0], near, sums[2]), parts))

    blocks = spread_blocks(grad_low, feeder if ring else None)
    d_out, d_pre, keep, send = feed_back(blocks, forward_weights, owners, slope)
    sums, parts = products(merge_sums(keep, send), [(second, d_pre), (d_out, hidden)])
    grad_mid, grad_mid_low, gain_forward = norm_back(grad_out, sums, stream_mid, gains[1])
    blocks = spread_blocks(grad_mid_low)
    d_branch, d_query, d_gate, d_own, d_past = attend_back(
        blocks, queries, key_value, memory, squashed, mask, allowed, attended, attention_weights, owners
    )
    returned = tied(shifted(d_past, -1))
    d_projected, keep, send = project_back(
        d_query, d_gate, d_own, returned, squashed, mask, value_all, attention_weights, owners, rows
    )
    sums = merge_sums(keep, send)
    if ring:
        sums, more = products(sums, [(normed, d_projected), (d_branch, mixed)])
        sums, pending = lax.optimization_barrier((sums, pending))
        sums = tied(sums)
        grads = [(Scatter(*parts, *more), ("up", "down", "project", "output"))]
        feeder.waiting.append(grads[0][0])
        feeder.start(2)
    else:
        pairs, near = lax.optimization_barrier(
            ([(normed, d_projected), (d_branch, mixed)], sums[1])
        )
        sums = (sums[0], near, sums[2])
        whole_grad = grad_whole(pairs, ring_places())
        sums, whole_grad = lax.optimization_barrier((sums, whole_grad))
        pending = scatter_whole(whole_grad)
        grads = [(Scatter(*parts), ("up", "down")), (None, ("project", "output"))]
        feeder.waiting.append(grads[0][0])
        feeder.start()
    grad_in, grad_in_low, gain_attention = norm_back(grad_mid, sums, stream, gains[0])
    return (grad_in, grad_in_low), grads, [gain_attention, gain_forward], pending


def scatter_whole(gradient):
    return lax.psum_scatter(gradient, "seq", scatter_dimension=0, tiled=True)


def own_columns(summed):
    count = lax.axis_size("grp")
    summed = summed.reshape(count, summed.shape[0] // count, summed.shape[1])
    return group_exchange(summed.astype(BF))


def allowed_keys(segment, memory_tail):
    positions = jnp.arange(segment.shape[1], dtype=jnp.int32)
    own_block = (segment[:, :, None] == segment[:, None, :]) & (
        positions[None, None, :] <= positions[None, :, None]
    )
    past_block = (segment[:, :, None] == 0) & (memory_tail[:, None, :] > 0)
    return jnp.concatenate([past_block, own_block], axis=2)


def adamw_update(master, gradient, first, second, factor, rate, decay):
    gradient = gradient * factor
    first_new = BETA_FIRST * first + (1.0 - BETA_FIRST) * gradient
    second_new = BETA_SECOND * second + (1.0 - BETA_SECOND) * gradient * gradient
    first_hat = first_new / (1.0 - BETA_FIRST**STEP)
    second_hat = second_new / (1.0 - BETA_SECOND**STEP)
    master_new = master - rate * (first_hat / (jnp.sqrt(second_hat) + EPS_ADAM) + decay * master)
    return (first_new, second_new, master_new)


def update_layers(factor, grads, masters, firsts, seconds):
    rows = masters[0].shape[1]
    chunk = 8 * DH

    widths = {"up": FF // H, "down": FF // H, "project": QKV_COLS, "output": OUT_COLS}
    flat = [part for parts in grads for part, _ in parts]
    found, index = [], 0
    for parts in grads:
        found.append({})
        for _, names in parts:
            start = 0
            for name in names:
                found[-1][name] = (index, start)
                start += widths[name]
            index += 1

    def body(factor_ref, *refs):
        parts = refs[: len(flat)]
        ins = refs[len(flat) : len(flat) + 6]
        outs = refs[len(flat) + 6 :]
        scale = factor_ref[0, 0]

        def apply(kind, columns, gradient):
            old = [ref[0, :, columns] for ref in ins[3 * kind : 3 * kind + 3]]
            first, second, master = adamw_update(
                old[0], gradient, old[1], old[2], scale, LR_MATRIX, DECAY
            )
            new = (master, first, second)
            for ref, values in zip(outs[3 * kind : 3 * kind + 3], new):
                ref[0, :, columns] = values

        for layer in range(L):

            @pl.when(pl.program_id(0) == layer)
            def _(layer=layer):
                def columns_of(name, member, start, width):
                    place, base = found[layer][name]
                    return parts[place][member, :, base + start : base + start + width].astype(F32)

                def heads(start):
                    return [columns_of("project", member, start, DH) for member in range(H)]

                def experts(name, start):
                    return [
                        columns_of(name, member, start + expert * LANE, DH)
                        for member in range(H)
                        for expert in range(E)
                    ]

                chunks = heads(0) + heads(LANE) + experts("project", 2 * LANE) + experts("output", 0)
                for group in range(len(chunks) // 8):
                    gradient = jnp.concatenate(chunks[8 * group : 8 * group + 8], axis=1)
                    apply(0, slice(group * chunk, (group + 1) * chunk), gradient)
                width = FF // H
                for side, name in enumerate(("up", "down")):
                    for member in range(H):
                        start = QKW + 2 * VW + side * FF + member * width
                        gradient = columns_of(name, member, 0, width)
                        apply(0, slice(start, start + width), gradient)
                selects = [
                    columns_of("project", member, DH + kind * E, E)
                    for kind in range(2)
                    for member in range(H)
                ]
                apply(1, slice(0, SELW), jnp.concatenate(selects, axis=1))

    def layer_block(array):
        return pl.BlockSpec((1,) + array.shape[1:], lambda step: (step, 0, 0))

    states = [masters[0], firsts[0], seconds[0], masters[1], firsts[1], seconds[1]]
    return pl.pallas_call(
        body,
        grid=(L,),
        in_specs=[in_scalars()]
        + [pl.BlockSpec(part.shape, lambda step: (0, 0, 0)) for part in flat]
        + [layer_block(array) for array in states],
        out_specs=[layer_block(array) for array in states],
        out_shape=[jax.ShapeDtypeStruct(array.shape, F32) for array in states],
        compiler_params=pltpu.CompilerParams(vmem_limit_bytes=VMEM_LIMIT),
        name="update_layers",
    )(factor, *flat, *states)


def all_sum(values):
    devices = lax.axis_size("seq") * lax.axis_size("grp")
    sent = jnp.broadcast_to(values[None], (devices,) + values.shape)
    return jnp.sum(
        lax.all_to_all(sent, ("seq", "grp"), split_axis=0, concat_axis=0, tiled=True), axis=0
    )


def document_weights(segment, seg_total, runs, seq_here, row_count):
    seq_count = runs.shape[0]
    device_ids = jnp.arange(seq_count, dtype=jnp.int32)[:, None]
    starts_there = runs[:, :, 0] > 0
    left_pick = jnp.max(jnp.where(starts_there & (device_ids < seq_here), device_ids, -1), axis=0)
    left_run = jnp.where(
        left_pick >= 0,
        jnp.sum(jnp.where(device_ids == left_pick, runs[:, :, 2], 0), axis=0)
        + (seq_here - 1 - left_pick) * row_count,
        0,
    )
    right_pick = jnp.min(
        jnp.where(starts_there & (device_ids > seq_here), device_ids, seq_count), axis=0
    )
    right_run = (
        jnp.sum(jnp.where(device_ids == right_pick, runs[:, :, 1], 0), axis=0)
        + (right_pick - seq_here - 1) * row_count
    )
    local_length = jnp.sum((segment[:, :, None] == segment[:, None, :]).astype(jnp.int32), axis=2)
    doc_length = (
        local_length
        + jnp.where(segment == 0, left_run[:, None], 0)
        + jnp.where(segment == seg_total[:, None], right_run[:, None], 0)
    )
    return 1.0 / doc_length.astype(F32)


def local(
    token_ids,
    target_ids,
    start_flags,
    route_ids,
    embed_table,
    layer_weights,
    router_weights,
    norm_gains,
    embed_mean,
    layer_mean,
    router_mean,
    gains_mean,
    embed_square,
    layer_square,
    router_square,
    gains_square,
):
    row_count = token_ids.shape[1]
    group_count = lax.axis_size("grp")
    own_group = lax.axis_index("grp")
    seq_count = lax.axis_size("seq")
    seq_here = lax.axis_index("seq")
    device_count = seq_count * group_count
    own_rows = embed_table.shape[0]
    positions = jnp.arange(row_count, dtype=jnp.int32)
    quarter = V // group_count

    total_abs = jnp.sum(start_flags, axis=1)
    first_start = jnp.min(jnp.where(start_flags > 0, positions[None, :], row_count), axis=1)
    last_start = jnp.max(jnp.where(start_flags > 0, positions[None, :], -1), axis=1)
    tail_count = jnp.where(total_abs > 0, row_count - last_start, row_count)
    summary = jnp.concatenate([total_abs, first_start, tail_count])
    summary = jnp.pad(summary, (0, row_count - summary.shape[0]))
    told = jnp.stack([token_ids[0], target_ids[0], summary])
    heard = lax.all_to_all(
        jnp.broadcast_to(told[None], (device_count,) + told.shape),
        ("seq", "grp"),
        split_axis=0,
        concat_axis=0,
        tiled=True,
    )
    all_ids = heard[:, 0].reshape(-1)
    heard = heard.reshape(seq_count, group_count, 3, row_count)
    runs = heard[:, 0, 2, : 3 * group_count].reshape(seq_count, 3, group_count).transpose(0, 2, 1)
    doc_count = jnp.sum(runs[:, :, 0]).astype(F32)

    relative = own_group ^ jnp.arange(group_count, dtype=jnp.int32)
    flags = jnp.take(start_flags, relative, axis=0)
    segment = jnp.cumsum(flags, axis=1, dtype=jnp.int32)
    seg_total = segment[:, -1]
    doc_weight = document_weights(
        segment, seg_total, jnp.take(runs, relative, axis=1), seq_here, row_count
    )
    targets = lax.dynamic_index_in_dim(heard[:, :, 1], seq_here, 0, keepdims=False)
    targets = jnp.take(targets, relative, axis=0)
    memory_tail = shifted((segment == seg_total[:, None]).astype(BF), 1)
    routes = jnp.take(route_ids, relative, axis=0).reshape(
        group_count, row_count, 2 * L, H, 2
    )
    routes = lax.dynamic_index_in_dim(routes, own_group, 3, keepdims=False)
    expert_ids = jnp.arange(E, dtype=jnp.int32)
    gate_all = jnp.sum((routes[..., None] == expert_ids).astype(F32), axis=-2)
    gate_all = gate_all.reshape(group_count * row_count, L, 2 * E).transpose(1, 0, 2)
    gate_all = jnp.pad(gate_all, [(0, 0), (0, 0), (DH, LANE - DH - 2 * E)])
    allowed = allowed_keys(segment, memory_tail).astype(F32)
    allowed = allowed.reshape(group_count * row_count, 2 * row_count)

    def exchanged(parts):
        swapped = exchange_parts(parts)
        return swapped.reshape(-1, swapped.shape[2])

    owners = ring_owners()
    own_scalar = own_group.astype(jnp.int32).reshape(1)
    attention_parts, forward_parts = arrange_layer(own_scalar, 0, layer_weights, router_weights)
    first = exchanged(attention_parts)
    first, forward_parts = lax.optimization_barrier((first, forward_parts))
    first_attention = Gather(first)
    first_forward = Gather(exchanged(forward_parts))
    feeder = Feed([first_attention])
    feeder.start()
    all_ids = feeder.tie(all_ids)

    looked = lookup(all_ids, embed_table).astype(BF) * D**0.5
    gate_all, looked, first_forward.flying = lax.optimization_barrier(
        (gate_all, looked, first_forward.flying)
    )
    looked = feeder.tie(looked)
    feeder.waiting.append(first_forward)
    gain_rows = norm_gains.astype(BF).T
    gain_rows = jnp.pad(gain_rows, [(0, 16 - NG), (0, row_count - own_rows)])
    sent = jnp.concatenate(
        [looked, jnp.broadcast_to(gain_rows[None], (device_count,) + gain_rows.shape)], axis=1
    )
    received = lax.all_to_all(sent, ("seq", "grp"), split_axis=0, concat_axis=0, tiled=True)
    received = feeder.tie(received)
    if seq_count > RING_LIMIT:
        stream = received[:, :own_rows].reshape(D, row_count).T.astype(F32)
        gains = received[:, own_rows : own_rows + NG, :own_rows].transpose(1, 0, 2)
        gains = gains.reshape(NG, D).astype(F32)
        state = (stream, rms_norm(stream, gains[0]).astype(BF))
    else:
        stream, normed_low, gains = stream_of_rows(received, owners, own_rows)
        state = (stream, normed_low)
    gains = gains[:NG, None, :]
    later, table_later, normed_here = lax.optimization_barrier(
        (layer_weights, embed_table, state[1])
    )
    state = (stream, normed_here)
    attention_parts, forward_parts = arrange_layer(own_scalar, 1, later, router_weights)
    second_attention = exchanged(attention_parts)
    second_forward = exchanged(forward_parts)
    table_own = exchanged(arrange_table(own_scalar, table_later))
    gathers = [
        first_attention,
        first_forward,
        Gather(second_attention),
        Gather(second_forward),
        Gather(table_own),
    ]
    feeder.waiting.extend(gathers[2:])
    layer_pieces = [
        tuple(lambda gather=gather: Weights(gather.result()) for gather in gathers[start : start + 2])
        for start in (0, 2)
    ]
    saved_layers = []
    saved_pieces = []
    for layer_index in range(L):
        state, stored, pieces = forward_layer(
            state,
            *layer_pieces[layer_index],
            owners,
            gains[2 * layer_index + 1 : 2 * layer_index + 3],
            gate_all[layer_index],
            allowed,
            row_count,
            feeder,
        )
        saved_layers.append(stored)
        saved_pieces.append(pieces)

    stream, final_low = state
    final_gain = gains[2 * L]
    final_all = jnp.concatenate(spread_blocks(final_low, feeder), axis=0)
    table_part = jnp.concatenate(gathers[4].result(), axis=0)
    logits = times_plain(final_all, table_part)
    columns = jnp.arange(logits.shape[1], dtype=jnp.int32)[None, :]
    logits = jnp.where(columns < quarter, logits, -1e30)
    hit = columns == (targets.reshape(-1) - own_group * quarter)[:, None]
    hit = hit & (columns < quarter)
    log_part = jax.nn.logsumexp(logits, axis=-1).reshape(group_count, row_count)
    target_part = jnp.sum(jnp.where(hit, logits, 0.0), axis=1).reshape(group_count, row_count)
    stats = jnp.stack([log_part, target_part], axis=1)
    others = [stats]
    for offset in range(1, group_count):
        got = swap_group(stats, offset)
        others.append(jnp.stack([got[index ^ offset] for index in range(group_count)]))
    others = jnp.stack(others)
    log_total = jax.nn.logsumexp(others[:, :, 0], axis=0)
    target_logit = jnp.sum(others[:, :, 1], axis=0)
    loss_local = jnp.sum((log_total[0] - target_logit[0]) * doc_weight[0])
    scale = (doc_weight / doc_count).reshape(-1)[:, None]
    d_logits = (jnp.exp(logits - log_total.reshape(-1)[:, None]) - hit.astype(F32)) * scale
    d_logits = d_logits.astype(BF)
    d_final = times_transposed(d_logits, table_part).reshape(group_count, row_count, D)
    keep = d_final[0::2].reshape(-1, D)
    send = d_final[1::2].reshape(-1, D).astype(BF)
    keep, send, d_logits = lax.optimization_barrier((keep, send, d_logits))
    sums = merge_sums(keep, send)
    table_grad = grad_whole([(final_all, d_logits)], ring_places())
    sums, table_grad = lax.optimization_barrier((sums, table_grad))
    table_grad = scatter_whole(table_grad)
    feeder = Feed()
    d_stream, d_stream_low, grad_final_gain = norm_back(
        jnp.zeros_like(stream), sums, stream, final_gain
    )

    state = (d_stream, d_stream_low)
    layer_grads = [None] * L
    gain_parts = [None] * L
    pending = ()
    for layer_index in reversed(range(L)):
        state, layer_grads[layer_index], gain_parts[layer_index], pending = backward_layer(
            state,
            *saved_pieces[layer_index],
            owners,
            gains[2 * layer_index : 2 * layer_index + 2],
            gate_all[layer_index],
            allowed,
            saved_layers[layer_index],
            row_count,
            feeder,
            layer_index == 0,
            pending,
        )

    gain_grads = sum(gain_parts, []) + [grad_final_gain]
    if seq_count > RING_LIMIT:
        gain_grads = jnp.concatenate(gain_grads).reshape(NG, device_count, own_rows)
        gain_grads = jnp.pad(
            gain_grads.transpose(1, 0, 2), [(0, 0), (0, 16 - NG), (0, row_count - own_rows)]
        )
        d_stream = state[0].T.reshape(device_count, own_rows, row_count)
        sent = jnp.concatenate([d_stream, gain_grads], axis=1).astype(BF)
    else:
        sent = rows_of_stream(state[0], gain_grads, owners, own_rows)
    received = lax.all_to_all(
        sent, ("seq", "grp"), split_axis=0, concat_axis=0, tiled=True
    ).astype(F32)
    received = feeder.tie(received, 2)
    embed_grad, square = spread_tokens(
        all_ids, received[:, :own_rows], own_columns(table_grad), V
    )
    embed_grad, square = feeder.tie((embed_grad, square))
    gains_grad = jnp.sum(received[:, own_rows : own_rows + NG, :own_rows], axis=0).T
    square = square[0, 0] + jnp.sum(gains_grad * gains_grad)
    layer_parts = []
    for grads in layer_grads:
        parts = []
        for member, names in grads:
            part = pending if member is None else member.result()
            square = square + jnp.sum(jnp.square(part.astype(F32)))
            part = own_columns(part)
            parts.append((part, names))
        layer_parts.append(parts)
    sums = all_sum(jnp.stack([loss_local, square]))
    loss_sum = sums[0]
    grad_norm = jnp.sqrt(sums[1])
    factor = CLIP / jnp.maximum(grad_norm, CLIP)
    embed_out = adamw_update(
        embed_table, embed_grad, embed_mean, embed_square, factor, LR_MATRIX, DECAY
    )
    updated = update_layers(
        factor.reshape(1, 1),
        layer_parts,
        (layer_weights, router_weights),
        (layer_mean, router_mean),
        (layer_square, router_square),
    )
    layer_out, router_out = [(new[1], new[2], new[0]) for new in (updated[:3], updated[3:])]
    gains_out = adamw_update(norm_gains, gains_grad, gains_mean, gains_square, factor, LR_GAIN, 0.0)
    return (
        loss_sum,
        doc_count,
        grad_norm,
        embed_out[0],
        embed_out[1],
        embed_out[2],
        layer_out[0],
        layer_out[1],
        layer_out[2],
        router_out[0],
        router_out[1],
        router_out[2],
        gains_out[0],
        gains_out[1],
        gains_out[2],
    )


def solution(mesh):
    rows = P(("seq", "grp"), None)
    layers = P(None, ("seq", "grp"), None)
    return jax.shard_map(
        local,
        mesh=mesh,
        in_specs=(
            P("grp", "seq"),
            P("grp", "seq"),
            P(None, "seq"),
            P(None, "seq", None, None),
            rows,
            layers,
            layers,
            rows,
            rows,
            layers,
            layers,
            rows,
            rows,
            layers,
            layers,
            rows,
        ),
        out_specs=(P(), P(), P()) + (rows,) * 3 + (layers,) * 6 + (rows,) * 3,
        check_vma=False,
    )
```
